256 devices in a mesh: ctx: 64 (over y, z, core), heads: 4 (over x).
Axes of the slice: x: 4, y: 4, z: 8, core: 2. Of those that a mesh axis runs over, the one named last changes fastest.
Arguments:
- q_in: bfloat16 [8192, 2048], P('ctx', 'heads'), may hold values from -6 to 6
- k_in: bfloat16 [8192, 2048], P('ctx', 'heads'), may hold values from -6 to 6
- v_in: bfloat16 [8192, 4096], P('ctx', 'heads'), may hold values from -6 to 6
- conv_q: bfloat16 [4, 2048], P(None, 'heads'), may hold values from -3 to 3
- conv_k: bfloat16 [4, 2048], P(None, 'heads'), may hold values from -3 to 3
- conv_v: bfloat16 [4, 4096], P(None, 'heads'), may hold values from -3 to 3
- a_in: float32 [8192, 32], P('ctx', 'heads')
- b_in: float32 [8192, 32], P('ctx', 'heads'), as said below
- a_log: float32 [32], P('heads')
- dt_bias: float32 [32], P('heads'), may hold values from -2 to 2
- norm_weight: float32 [128], replicated, may hold values from 0.1 to 1.9
- z_in: bfloat16 [8192, 4096], P('ctx', 'heads'), may hold values from -6 to 6
- out_weight: bfloat16 [4096, 2048], P('heads'), may hold values from -0.09375 to 0.09375
Outputs:
- mixed: float32 [8192, 2048], P('ctx', 'heads')
The draws below stay inside these ranges and needn't reach their ends.
Inputs may be any that keep to these rules, and one draw needn't show every extreme that they name: `b_in`: write strength logits.
All inputs are finite; a program needn't handle non-finite values.
Results may differ from the reference program's by a relative error of at most 0.0039.
Values may be sent and summed in bfloat16 or wider, within the bound.
A program may use at most 192 MiB of HBM per device.

```python
import math
import jax
import jax.numpy as jnp
from jax import lax

D = 2048
KH = 16
VH = 32
DK = 128
DV = 128
CONV = 4
TOKENS = 8192


def head_law(key):
    base_key = jax.random.fold_in(key, 7)
    picked = jax.random.uniform(jax.random.fold_in(base_key, 1), (VH,))
    slow_share = 0.625
    gradual_heads = picked < slow_share
    spread = jnp.exp(jax.random.uniform(jax.random.fold_in(base_key, 2), (VH,), minval=-0.7, maxval=0.7))
    quick_decay_rate = 1.0 / (16.0 + 24.0 * jax.random.uniform(jax.random.fold_in(base_key, 3), (VH,)))
    decay_rates = jnp.where(gradual_heads, spread * 0.1 / TOKENS, quick_decay_rate)
    return (gradual_heads, decay_rates)


def draw_a_log(key, part):
    gradual_heads, decay_rates = head_law(key)
    return jnp.log(decay_rates).astype(jnp.float32)


def draw_a_in(key, part):
    gradual_heads, decay_rates = head_law(key)
    baseline_level = jax.random.uniform(jax.random.fold_in(key, 21), (TOKENS, VH), minval=-1.5, maxval=1.5)
    places = jax.random.randint(jax.random.fold_in(key, 22), (3,), 0, TOKENS)
    spiked_positions = jnp.any(jnp.arange(TOKENS)[:, None] == places[None, :], axis=1)
    desired_output = jax.random.uniform(jax.random.fold_in(key, 23), (TOKENS, VH), minval=0.22, maxval=0.7)
    spike_events = desired_output / decay_rates[None, :]
    return jnp.where(spiked_positions[:, None] & gradual_heads[None, :], spike_events, baseline_level).astype(jnp.float32)


def draw_b_in(key, part):
    gradual_heads, decay_rates = head_law(key)
    fast_logit = jax.random.uniform(jax.random.fold_in(key, 31), (TOKENS, VH), minval=-1.0, maxval=2.0)
    token_factor = jnp.exp(jax.random.uniform(jax.random.fold_in(key, 32), (TOKENS, VH), minval=-1.5, maxval=1.5)) / 1.42
    gradual_beta = jnp.minimum(2.5 * DK / TOKENS * token_factor, 0.5)
    slow_logit = jnp.log(gradual_beta) - jnp.log1p(-gradual_beta)
    return jnp.where(gradual_heads[None, :], slow_logit, fast_logit).astype(jnp.float32)


def levels(own_key, dims, cuts, smallest, top_value):
    factor_of = 1.0
    for dim, shards_of in cuts:
        steps = jax.random.uniform(jax.random.fold_in(jax.random.fold_in(own_key, 6), dim), (shards_of,), jnp.float32, smallest / len(cuts), top_value / len(cuts))
        factor_of = factor_of * jnp.repeat(jnp.exp(steps), dims[dim] // shards_of).reshape((-1,) + (1,) * (len(dims) - 1 - dim))
    return factor_of


def normal_values(own_key, shape, width, bound, pieces=(), held_as=jnp.bfloat16):
    values = jax.random.normal(own_key, shape, jnp.float32) * width
    if len(pieces) > 0:
        values = levels(own_key, shape, pieces, -0.22, 0.18) * values
    return jnp.clip(values, min=-bound, max=bound).astype(held_as)


def setup_inputs(seed: int = 0) -> dict:
    key_of = jax.random.split(jax.random.key(seed), 14)
    q_in = normal_values(key_of[0], (TOKENS, KH * DK), 1.0, 6.0, ((0, 64), (1, 4)))
    k_in = normal_values(key_of[1], (TOKENS, KH * DK), 1.0, 6.0, ((0, 64), (1, 4)))
    v_in = normal_values(key_of[2], (TOKENS, VH * DV), 1.0, 6.0, ((0, 64), (1, 4)))
    conv_q = normal_values(key_of[3], (CONV, KH * DK), CONV ** -0.5, 3.0, ((1, 4),))
    conv_k = normal_values(key_of[4], (CONV, KH * DK), CONV ** -0.5, 3.0, ((1, 4),))
    conv_v = normal_values(key_of[5], (CONV, VH * DV), CONV ** -0.5, 3.0, ((1, 4),))
    a_in = draw_a_in(jax.random.fold_in(key_of[13], 71), 0)
    b_in = draw_b_in(jax.random.fold_in(key_of[13], 71), 0)
    a_log = draw_a_log(jax.random.fold_in(key_of[13], 71), 0)
    dt_bias = normal_values(key_of[9], (VH,), 0.5, 2.0, ((0, 4),), jnp.float32)
    norm_weight = jnp.clip(1.0 + 0.18 * jax.random.normal(key_of[10], (DV,), jnp.float32), 0.1, 1.9)
    z_in = normal_values(key_of[11], (TOKENS, VH * DV), 1.0, 6.0, ((0, 64), (1, 4)))
    out_weight = normal_values(key_of[12], (VH * DV, D), (VH * DV) ** -0.5, 0.09375, ((0, 4),))
    return dict(q_in=q_in, k_in=k_in, v_in=v_in, conv_q=conv_q, conv_k=conv_k, conv_v=conv_v, a_in=a_in, b_in=b_in, a_log=a_log, dt_bias=dt_bias, norm_weight=norm_weight, z_in=z_in, out_weight=out_weight)


highest = lax.Precision.HIGHEST

def conv_silu(rim_rows, rows_in, weights):
    joined = jnp.concatenate([rim_rows, rows_in], axis=0).astype(jnp.float32)
    length = rows_in.shape[0]
    total = jnp.zeros(rows_in.shape, jnp.float32)
    for offset in range(weights.shape[0]):
        total = total + weights[offset].astype(jnp.float32) * joined[offset:offset + length]
    return jax.nn.silu(total).astype(jnp.bfloat16)

def unit_norm(blocked):
    entries = blocked.astype(jnp.float32)
    return entries * lax.rsqrt(lax.optimization_barrier(jnp.sum(entries * entries, axis=-1, keepdims=True)) + 1e-06)

def span_step(state, queries, key_rows, values, logdecay, beta_rows):
    length = queries.shape[1]
    positions = jnp.arange(length)
    strict = positions[:, None] > positions[None, :]
    upto = positions[:, None] >= positions[None, :]
    cumulative = jnp.cumsum(logdecay, axis=1)
    gaps = cumulative[:, :, None] - cumulative[:, None, :]
    within = jnp.exp(jnp.where(upto[None], gaps, -jnp.inf))
    key_gram = jnp.einsum('htd,hjd->htj', key_rows, key_rows, precision=highest)
    lower_part = jnp.where(strict[None], beta_rows[:, :, None] * key_gram * within, 0.0)
    identity_m = jnp.eye(length, dtype=queries.dtype)
    negated = -lower_part
    inverse = identity_m[None] + negated
    powers = negated
    for level in range(max(1, (length - 1).bit_length()) - 1):
        powers = jnp.einsum('hij,hjk->hik', powers, powers, precision=highest)
        inverse = inverse + jnp.einsum('hij,hjk->hik', inverse, powers, precision=highest)
    start_decay = jnp.exp(cumulative)
    seen = jnp.einsum('htd,hvd->htv', key_rows, state, precision=highest)
    right_side = beta_rows[:, :, None] * (values - start_decay[:, :, None] * seen)
    writes = jnp.einsum('htj,hjv->htv', inverse, right_side, precision=highest)
    query_gram = jnp.einsum('htd,hjd->htj', queries, key_rows, precision=highest) * within
    outputs = start_decay[:, :, None] * jnp.einsum('htd,hvd->htv', queries, state, precision=highest)
    outputs = outputs + jnp.einsum('htj,hjv->htv', query_gram, writes, precision=highest)
    tail_decay = jnp.exp(cumulative[:, -1:] - cumulative)
    new_state = jnp.exp(cumulative[:, -1])[:, None, None] * state
    new_state = new_state + jnp.einsum('hjv,hjd->hvd', writes * tail_decay[:, :, None], key_rows, precision=highest)
    return (outputs, new_state)

def scan_spans(state, query_blocks, key_blocks, value_blocks, decay_blocks, beta_blocks, group_size, extra):

    def advance(carried, inputs):
        query_block, key_block, value_block, decay_block, beta_block = inputs
        scale_q = query_block.shape[-1] ** (-0.5)
        queries = jnp.repeat(unit_norm(query_block) * scale_q, group_size, axis=1).transpose(1, 0, 2)
        key_rows = jnp.repeat(unit_norm(key_block), group_size, axis=1).transpose(1, 0, 2)
        values = value_block.astype(jnp.float32).transpose(1, 0, 2)
        if extra:
            values = jnp.concatenate([values, jnp.zeros(values.shape[:2] + (extra,), jnp.float32)], axis=2)
        outputs, new_state = span_step(carried, queries, key_rows, values, decay_block.T, beta_block.T)
        return (new_state, outputs)
    return lax.scan(advance, state, (query_blocks, key_blocks, value_blocks, decay_blocks, beta_blocks))

def gate_norm(core_out, gate_rows, weight):
    scaled = core_out * lax.rsqrt(lax.optimization_barrier(jnp.mean(core_out * core_out, axis=-1, keepdims=True)) + 1e-06) * weight
    gated = scaled.reshape(gate_rows.shape) * jax.nn.silu(gate_rows.astype(jnp.float32))
    return gated.astype(jnp.bfloat16)

def reference(q_in, k_in, v_in, conv_q, conv_k, conv_v, a_in, b_in, a_log, dt_bias, norm_weight, z_in, out_weight):
    rim_len = conv_q.shape[0] - 1
    query_conv = conv_silu(jnp.zeros((rim_len, q_in.shape[1]), jnp.bfloat16), q_in, conv_q)
    key_conv = conv_silu(jnp.zeros((rim_len, k_in.shape[1]), jnp.bfloat16), k_in, conv_k)
    value_conv = conv_silu(jnp.zeros((rim_len, v_in.shape[1]), jnp.bfloat16), v_in, conv_v)
    logdecay = -jnp.exp(a_log)[None, :] * jax.nn.softplus(a_in + dt_bias[None, :])
    beta_rows = jax.nn.sigmoid(b_in)
    block_len = math.gcd(64, TOKENS)
    block_count = TOKENS // block_len
    zero_state = jnp.zeros((VH, DV, DK), jnp.float32)
    final_state, outputs = scan_spans(zero_state, query_conv.reshape(block_count, block_len, KH, DK), key_conv.reshape(block_count, block_len, KH, DK), value_conv.reshape(block_count, block_len, VH, DV), logdecay.reshape(block_count, block_len, VH), beta_rows.reshape(block_count, block_len, VH), VH // KH, 0)
    core_out = outputs.transpose(0, 2, 1, 3).reshape(TOKENS, VH, DV)
    normed = gate_norm(core_out, z_in, norm_weight)
    return jnp.dot(normed, out_weight, preferred_element_type=jnp.float32)
```

```python
import functools

import jax
import jax.numpy as jnp
from jax import lax
from jax.experimental import pallas as pl
from jax.experimental.pallas import tpu as pltpu
from jax.sharding import PartitionSpec as P

DK = 128
DV = 128
TAIL = 16
MESH = pl.DeviceIdType.MESH
F32 = jnp.float32
BF16 = jnp.bfloat16
HIGHEST = lax.Precision.HIGHEST
KEY_GROUP = 2


def split(value):
    high = value.astype(BF16)
    return high, (value - high.astype(F32)).astype(BF16)


def mm(left, right):
    return jnp.dot(left, right, preferred_element_type=F32)


def one_pass(left, right):
    return mm(left.astype(BF16), right.astype(BF16))


def split_left(left, right):
    high, low = split(left)
    return mm(jnp.concatenate([high, low], axis=1), jnp.concatenate([right, right], axis=0))


def split_right(left, right):
    high, low = split(right)
    return mm(jnp.concatenate([left, left], axis=1), jnp.concatenate([high, low], axis=0))


def split_both(left, right):
    left_high, left_low = split(left)
    right_high, right_low = split(right)
    return mm(
        jnp.concatenate([left_high, left_low], axis=1),
        jnp.concatenate([right_high, right_high], axis=0),
    ) + mm(left_high, right_low)


def silu(value):
    return value * (1.0 / (1.0 + jnp.exp(-value)))


def three_parts(value):
    first = value.astype(BF16).astype(F32)
    second = (value - first).astype(BF16).astype(F32)
    return first, second, value - first - second


def pack_decay(decay, width):
    row = lax.broadcasted_iota(jnp.int32, (TAIL, width), 0)
    first, second, third = three_parts(decay)
    zero = jnp.zeros((TAIL, width), F32)
    block = jnp.where(row == 0, first, jnp.where(row == 1, second, jnp.where(row == 2, third, zero)))
    return block.astype(BF16)


def kernel(
    nx,
    ny,
    nz,
    q_hbm,
    k_hbm,
    v_hbm,
    z_hbm,
    w_hbm,
    a_ref,
    b_ref,
    alog_ref,
    bias_ref,
    gain_ref,
    cq_ref,
    ck_ref,
    cv_ref,
    out_ref,
    q_in,
    k_in,
    v_in,
    z_in,
    w_in,
    halo_q,
    halo_k,
    halo_v,
    ext,
    vc_all,
    kc_all,
    qc_all,
    up_out,
    up_in,
    pair,
    carry,
    pre_state,
    pre_map,
    pre_decay,
    sigma,
    down_out,
    down_in,
    reads,
    local,
    normed,
    rs_out,
    rs_in,
    load_sem,
    halo_send,
    halo_recv,
    up_send,
    up_recv,
    pair_sem,
    y_send,
    y_recv,
    down_send,
    down_recv,
    rs_send,
    rs_recv,
):
    rows = q_in.shape[0]
    key_heads = nz // 2
    ring = 2 * nz
    count = ny * ring
    me = lax.axis_index("ctx")
    x = lax.axis_index("heads")
    y = me // ring
    place = lax.rem(me, ring)
    z = place // 2
    core = lax.rem(place, 2)
    half = place // nz
    mine = lax.rem(place, nz)
    base = 2 * (z // 2)
    width = out_ref.shape[1]

    def head_of(slot):
        return lax.rem(base + slot, nz)

    loads = [
        pltpu.make_async_copy(source, target, load_sem.at[i])
        for i, (source, target) in enumerate(
            ((k_hbm, k_in), (v_hbm, v_in), (q_hbm, q_in), (z_hbm, z_in), (w_hbm, w_in))
        )
    ]
    for load in loads:
        load.start()

    barrier = pltpu.get_barrier_semaphore()

    def greet(ctx, heads):
        pl.semaphore_signal(barrier, inc=1, device_id=(ctx, heads), device_id_type=MESH)

    for step in range(1, ring):
        greet(y * ring + lax.rem(place + step, ring), x)
    for step in range(1, ny):
        greet(lax.rem(me + step * ring, count), x)
    for step in range(1, nx):
        greet(me, lax.rem(x + step, nx))
    over = jnp.logical_and(place == ring - 1, me < count - 1)
    under = jnp.logical_and(place == 0, me > 0)

    @pl.when(over)
    def _():
        greet(me + 1, x)

    @pl.when(under)
    def _():
        greet(me - 1, x)

    pl.semaphore_wait(
        barrier,
        (ring - 1) + (ny - 1) + (nx - 1) + over.astype(jnp.int32) + under.astype(jnp.int32),
    )

    def halo_copies(ctx):
        return [
            pltpu.make_async_remote_copy(
                src_ref=source.at[pl.ds(rows - TAIL, TAIL), :],
                dst_ref=target,
                send_sem=halo_send.at[i],
                recv_sem=halo_recv.at[i],
                device_id=(ctx, x),
                device_id_type=MESH,
            )
            for i, (source, target) in enumerate(
                ((k_hbm, halo_k), (v_hbm, halo_v), (q_hbm, halo_q))
            )
        ]

    following = lax.rem(me + 1, count)

    @pl.when(me < count - 1)
    def _():
        for copy in halo_copies(following):
            copy.start()

    @pl.when(me == 0)
    def _():
        halo_k[...] = jnp.zeros_like(halo_k)
        halo_v[...] = jnp.zeros_like(halo_v)
        halo_q[...] = jnp.zeros_like(halo_q)

    row = lax.broadcasted_iota(jnp.int32, (rows, rows), 0)
    col = lax.broadcasted_iota(jnp.int32, (rows, rows), 1)
    upto = row >= col
    strict = row > col
    apart = jnp.bitwise_xor(row, col)
    gate_in = a_ref[...] + bias_ref[...]
    softplus = jnp.maximum(gate_in, 0.0) + jnp.log1p(jnp.exp(-jnp.abs(gate_in)))
    logdecay = -jnp.exp(alog_ref[...]) * softplus
    beta = 1.0 / (1.0 + jnp.exp(-b_ref[...]))
    cumulative = jnp.dot(
        jnp.where(upto, 1.0, 0.0), logdecay, preferred_element_type=F32, precision=HIGHEST
    )
    from_head = lax.broadcasted_iota(jnp.int32, (nz, 128), 0)
    lane = lax.broadcasted_iota(jnp.int32, (nz, 128), 1)

    def placing(first):
        wanted = base + lane - first
        wanted = jnp.where(wanted >= nz, wanted - nz, wanted)
        inside = jnp.logical_and(lane >= first, lane < first + nz)
        return jnp.where(jnp.logical_and(inside, wanted == from_head), 1.0, 0.0)

    columns = jnp.dot(
        cumulative, placing(0), preferred_element_type=F32, precision=HIGHEST
    ) + jnp.dot(beta, placing(nz), preferred_element_type=F32, precision=HIGHEST)

    def conv(data, halo, taps_ref, start, size):
        cols = pl.ds(pl.multiple_of(start, 128), size)
        ext[0:8, 0:size] = halo[:, cols].astype(F32)[8:16]
        ext[8 : 8 + rows, 0:size] = data[:, cols].astype(F32)
        taps = taps_ref[:, cols].astype(F32)
        total = jnp.zeros((rows, size), F32)
        for j in range(4):
            total = total + taps[j : j + 1] * ext[5 + j : 5 + j + rows, 0:size]
        return silu(total).astype(BF16)

    def inverse_norm(block):
        entries = block.astype(F32)
        return lax.rsqrt(jnp.sum(entries * entries, axis=1, keepdims=True) + 1e-6)

    for load in loads[:3]:
        load.wait()

    @pl.when(me > 0)
    def _():
        for copy in halo_copies(following):
            copy.wait_recv()

    wide_lane = lax.broadcasted_iota(jnp.int32, (rows, 128), 1)
    for s in range(key_heads):
        kh = lax.rem(base // 2 + s, key_heads)
        kc_all[s] = conv(k_in, halo_k, ck_ref, kh * 128, 128)
        vc_all[s] = conv(v_in, halo_v, cv_ref, kh * 256, 256)
        qc_all[s] = conv(q_in, halo_q, cq_ref, kh * 128, 128)
        columns = jnp.where(wide_lane == 2 * nz + s, inverse_norm(kc_all[s]), columns)
        columns = jnp.where(
            wide_lane == 2 * nz + key_heads + s, inverse_norm(qc_all[s]) * DK**-0.5, columns
        )
    by_row = jnp.transpose(columns)

    def column(index):
        return columns[:, index : index + 1]

    def lane_row(index):
        return by_row[index : index + 1, :]

    def up_copy(slot):
        head = head_of(slot)
        return pltpu.make_async_remote_copy(
            src_ref=up_out.at[slot],
            dst_ref=up_in.at[mine],
            send_sem=up_send.at[slot],
            recv_sem=up_recv.at[mine],
            device_id=(y * ring + 2 * head + half, x),
            device_id_type=MESH,
        )

    def at_home(slot):
        return jnp.logical_and(head_of(slot) == z, half == core)

    for first in range(0, key_heads, KEY_GROUP):
        keys = range(first, first + KEY_GROUP)
        heads = [2 * s + p for s in keys for p in range(2)]
        gram, query_gram = {}, {}
        for s in keys:
            kc_t = kc_all[s]
            contract = (((1,), (1,)), ((), ()))
            gram[s] = lax.dot_general(kc_t, kc_t, contract, preferred_element_type=F32)
            query_gram[s] = lax.dot_general(
                qc_all[s], kc_t, contract, preferred_element_type=F32
            )
        within, lower, inverse = {}, {}, {}
        for h in heads:
            s = h // 2
            gaps = column(h) - lane_row(h)
            within[h] = jnp.exp(jnp.where(upto, gaps, -1e30)) * lane_row(2 * nz + s)
            scale = column(nz + h) * column(2 * nz + s)
            lower[h] = jnp.where(strict, scale * gram[s] * within[h], 0.0)
            inverse[h] = jnp.where(apart == 1, -lower[h], 0.0)
        level = 1
        while (1 << level) < rows:
            block, inner = {}, {}
            for h in heads:
                block[h] = jnp.where((apart >> level) == 1, lower[h], 0.0)
                inner[h] = block[h] + one_pass(block[h], inverse[h])
            for h in heads:
                inverse[h] = inverse[h] - inner[h] - one_pass(inverse[h], inner[h])
            level += 1
        values, maps = {}, {}
        for h in heads:
            s = h // 2
            solve = jnp.where(row == col, 1.0, inverse[h]) * lane_row(nz + h)
            values[h] = split_left(solve, vc_all[s, :, (h % 2) * 128 : (h % 2 + 1) * 128])
            key_solve = solve * (jnp.exp(lane_row(h)) * lane_row(2 * nz + s))
            maps[h] = split_left(key_solve, kc_all[s])
        for h in heads:
            s = h // 2
            last = columns[rows - 1 : rows, h : h + 1]
            tail = jnp.exp(last - column(h)) * column(2 * nz + s)
            both = jnp.concatenate([values[h] * tail, maps[h] * tail], axis=1)
            kc_t = jnp.transpose(kc_all[s].astype(F32)).astype(BF16)
            up_out[h, 0:DK, :] = split_right(kc_t, both).astype(BF16)
            up_out[h, DK:, :] = pack_decay(jnp.exp(last), DK + DV)

        for h in heads:
            home = at_home(h)

            @pl.when(home)
            def _(h=h):
                up_in[mine] = up_out[h]

            @pl.when(jnp.logical_not(home))
            def _(h=h):
                up_copy(h).start()

        for h in heads:
            s = h // 2
            attend = jnp.where(
                upto, query_gram[s] * within[h] * column(2 * nz + key_heads + s), 0.0
            )
            both = split_both(attend, jnp.concatenate([values[h], maps[h]], axis=1))
            local[h] = both[:, 0:DV]
            start = jnp.exp(column(h)) * column(2 * nz + key_heads + s)
            high, low = split(start * qc_all[s].astype(F32) - both[:, DV:])
            reads[h, :, 0:DK] = high
            reads[h, :, DK:] = low

    eye = lax.broadcasted_iota(jnp.int32, (DK, DK), 0) == lax.broadcasted_iota(
        jnp.int32, (DK, DK), 1
    )

    def decay_of(block):
        return jnp.sum(block.astype(F32), axis=0, keepdims=True)

    def up_wait(j):
        at = half_place(j)

        @pl.when(at != me)
        def _():
            pltpu.make_async_remote_copy(
                src_ref=up_out.at[0],
                dst_ref=up_in.at[j],
                send_sem=up_send.at[0],
                recv_sem=up_recv.at[j],
                device_id=(at, x),
                device_id_type=MESH,
            ).wait_recv()

    def half_place(j):
        return y * ring + core * nz + j

    def with_map(state, map_part, decay):
        return jnp.concatenate(
            [state.astype(F32), jnp.where(eye, decay, 0.0) - map_part.astype(F32)], axis=1
        )

    def compose(message, carried):
        decay = decay_of(message[DK:, :])
        fresh = jnp.concatenate(
            [message[0:DK, 0:DV].astype(F32), jnp.zeros((DK, DK), F32)], axis=1
        )
        return decay, decay * carried - mm(message[0:DK, DV:], carried.astype(BF16)) + fresh

    pre_state[0] = jnp.zeros((DK, DV), F32)
    pre_map[0] = jnp.zeros((DK, DK), BF16)
    pre_decay[0] = jnp.ones((8, 128), F32)
    total_decay = None
    carried = None
    for j in range(nz):
        up_wait(j)
        message = up_in[j]
        if j == 0:
            total_decay = decay_of(message[DK:, :])
            carried = with_map(message[0:DK, 0:DV], message[0:DK, DV:], total_decay[:, 0:DK])
        else:
            decay, carried = compose(message, carried)
            total_decay = total_decay * decay
        map_part = jnp.where(eye, total_decay[:, 0:DK], 0.0) - carried[:, DV:]
        if j < nz - 1:
            pre_state[j + 1] = carried[:, 0:DV]
            pre_map[j + 1] = map_part.astype(BF16)
            pre_decay[j + 1] = jnp.broadcast_to(total_decay[:, 0:128], (8, 128))

    def put_message(target, carried, total_decay):
        target[0:DK, 0:DV] = carried[:, 0:DV].astype(BF16)
        target[0:DK, DV:] = (
            jnp.where(eye, total_decay[:, 0:DK], 0.0) - carried[:, DV:]
        ).astype(BF16)
        target[DK:, :] = pack_decay(total_decay[:, 0:1], DK + DV)

    other = me + 1 - 2 * core
    put_message(pair.at[core], carried, total_decay)
    swap = pltpu.make_async_remote_copy(
        src_ref=pair.at[core],
        dst_ref=pair.at[core],
        send_sem=pair_sem.at[0],
        recv_sem=pair_sem.at[1],
        device_id=(other, x),
        device_id_type=MESH,
    )
    swap.start()
    pltpu.make_async_remote_copy(
        src_ref=pair.at[core],
        dst_ref=pair.at[1 - core],
        send_sem=pair_sem.at[0],
        recv_sem=pair_sem.at[1],
        device_id=(other, x),
        device_id_type=MESH,
    ).wait_recv()
    early = pair[0]
    early_decay = decay_of(early[DK:, :])
    decay, carried = compose(
        pair[1], with_map(early[0:DK, 0:DV], early[0:DK, DV:], early_decay[:, 0:DK])
    )
    put_message(carry.at[y], carried, early_decay * decay)

    def carry_copy(source, target_y):
        return pltpu.make_async_remote_copy(
            src_ref=carry.at[source],
            dst_ref=carry.at[source],
            send_sem=y_send.at[target_y],
            recv_sem=y_recv.at[source],
            device_id=(target_y * ring + place, x),
            device_id_type=MESH,
        )

    for later in range(1, ny):

        @pl.when(y < later)
        def _(later=later):
            carry_copy(y, later).start()

    sigma[...] = jnp.zeros((DK, DV), F32)

    def advance(message):
        state = sigma[...]
        sigma[...] = (
            decay_of(message[DK:, 0:DV]) * state
            - mm(message[0:DK, DV:], state.astype(BF16))
            + message[0:DK, 0:DV].astype(F32)
        )

    for earlier in range(ny - 1):

        @pl.when(y > earlier)
        def _(earlier=earlier):
            carry_copy(earlier, y).wait_recv()
            advance(carry[earlier])

    @pl.when(core == 1)
    def _():
        advance(pair[0])

    def down_copy(j):
        return pltpu.make_async_remote_copy(
            src_ref=down_out.at[j],
            dst_ref=down_in.at[z],
            send_sem=down_send.at[j],
            recv_sem=down_recv.at[z],
            device_id=(half_place(j), x),
            device_id_type=MESH,
        )

    start_state = sigma[...]
    rounded = start_state.astype(BF16)
    for j in range(nz):
        state = (
            pre_decay[j, 0:1, :] * start_state - mm(pre_map[j], rounded) + pre_state[j]
        ).astype(BF16)
        down_out[j] = state
        home = half_place(j) == me

        @pl.when(home)
        def _(j=j):
            down_in[z] = down_out[j]

        @pl.when(jnp.logical_not(home))
        def _(j=j):
            down_copy(j).start()

    for load in loads[3:]:
        load.wait()
    for h in range(nz):
        head = head_of(h)
        sender = y * ring + 2 * head + half

        @pl.when(sender != me)
        def _(head=head, sender=sender):
            pltpu.make_async_remote_copy(
                src_ref=down_out.at[0],
                dst_ref=down_in.at[head],
                send_sem=down_send.at[0],
                recv_sem=down_recv.at[head],
                device_id=(sender, x),
                device_id_type=MESH,
            ).wait_recv()

        state = down_in[head]
        core_out = mm(reads[h], jnp.concatenate([state, state], axis=0)) + local[h]
        cols = pl.ds(pl.multiple_of(head * DV, DV), DV)
        power = jnp.mean(core_out * core_out, axis=1, keepdims=True)
        gated = core_out * lax.rsqrt(power + 1e-6) * gain_ref[...]
        normed[:, cols] = (gated * silu(z_in[:, cols].astype(F32))).astype(BF16)

    def part(step):
        cols = pl.ds(pl.multiple_of(lax.rem(x + step, nx) * width, 128), width)
        return mm(normed[...], w_in[:, cols])

    def rs_copy(step):
        return pltpu.make_async_remote_copy(
            src_ref=rs_out.at[step - 1],
            dst_ref=rs_in.at[step - 1],
            send_sem=rs_send.at[step - 1],
            recv_sem=rs_recv.at[step - 1],
            device_id=(me, lax.rem(x + step, nx)),
            device_id_type=MESH,
        )

    order = sorted(range(1, nx), key=lambda step: -min(step, nx - step))
    for step in order:
        rs_out[step - 1] = part(step).astype(BF16)
        rs_copy(step).start()
    total = part(0)
    for step in reversed(order):
        rs_copy(step).wait_recv()
        total = total + rs_in[step - 1].astype(F32)
    out_ref[...] = total

    @pl.when(me < count - 1)
    def _():
        for copy in halo_copies(following):
            copy.wait_send()

    for slot in range(nz):

        @pl.when(jnp.logical_not(at_home(slot)))
        def _(slot=slot):
            up_copy(slot).wait_send()

        @pl.when(half_place(slot) != me)
        def _(slot=slot):
            down_copy(slot).wait_send()

    swap.wait_send()
    for later in range(1, ny):

        @pl.when(y < later)
        def _(later=later):
            carry_copy(y, later).wait_send()

    for step in order:
        rs_copy(step).wait_send()


def shards(
    q_in, k_in, v_in, conv_q, conv_k, conv_v, a_in, b_in, a_log, dt_bias, norm_weight, z_in, out_weight
):
    rows = q_in.shape[0]
    nz = v_in.shape[1] // DV
    nx = lax.axis_size("heads")
    ny = lax.axis_size("ctx") // (2 * nz)
    key_heads = nz // 2
    width = out_weight.shape[1] // nx
    hbm = pl.BlockSpec(memory_space=pl.ANY)
    vmem = pl.BlockSpec(memory_space=pltpu.VMEM)
    dma = pltpu.SemaphoreType.DMA
    message = (DK + TAIL, DK + DV)
    scratch = [
        pltpu.VMEM(q_in.shape, BF16),
        pltpu.VMEM(k_in.shape, BF16),
        pltpu.VMEM(v_in.shape, BF16),
        pltpu.VMEM(z_in.shape, BF16),
        pltpu.VMEM(out_weight.shape, BF16),
        pltpu.VMEM((TAIL, q_in.shape[1]), BF16),
        pltpu.VMEM((TAIL, k_in.shape[1]), BF16),
        pltpu.VMEM((TAIL, v_in.shape[1]), BF16),
        pltpu.VMEM((rows + 8, 2 * DV), F32),
        pltpu.VMEM((key_heads, rows, 2 * DV), BF16),
        pltpu.VMEM((key_heads, rows, DK), BF16),
        pltpu.VMEM((key_heads, rows, DK), BF16),
        pltpu.VMEM((nz,) + message, BF16),
        pltpu.VMEM((nz,) + message, BF16),
        pltpu.VMEM((2,) + message, BF16),
        pltpu.VMEM((ny,) + message, BF16),
        pltpu.VMEM((nz, DK, DV), F32),
        pltpu.VMEM((nz, DK, DK), BF16),
        pltpu.VMEM((nz, 8, 128), F32),
        pltpu.VMEM((DK, DV), F32),
        pltpu.VMEM((nz, DK, DV), BF16),
        pltpu.VMEM((nz, DK, DV), BF16),
        pltpu.VMEM((nz, rows, 2 * DK), BF16),
        pltpu.VMEM((nz, rows, DV), F32),
        pltpu.VMEM((rows, nz * DV), BF16),
        pltpu.VMEM((nx - 1, rows, width), BF16),
        pltpu.VMEM((nx - 1, rows, width), BF16),
        dma((5,)),
        dma((3,)),
        dma((3,)),
        dma((nz,)),
        dma((nz,)),
        dma((2,)),
        dma((ny,)),
        dma((ny,)),
        dma((nz,)),
        dma((nz,)),
        dma((nx - 1,)),
        dma((nx - 1,)),
    ]
    call = pl.pallas_call(
        functools.partial(kernel, nx, ny, nz),
        out_shape=jax.ShapeDtypeStruct((rows, width), F32),
        in_specs=[hbm] * 5 + [vmem] * 8,
        out_specs=vmem,
        scratch_shapes=scratch,
        compiler_params=pltpu.CompilerParams(
            collective_id=0, has_side_effects=True, vmem_limit_bytes=40 * 1024 * 1024
        ),
        cost_estimate=pl.CostEstimate(
            flops=2_000_000_000, bytes_accessed=6_000_000, transcendentals=1_000_000
        ),
    )
    return call(
        q_in,
        k_in,
        v_in,
        z_in,
        out_weight,
        a_in,
        b_in,
        a_log.reshape(1, nz),
        dt_bias.reshape(1, nz),
        norm_weight.reshape(1, DV),
        conv_q,
        conv_k,
        conv_v,
    )


def solution(mesh):
    in_specs = (
        P("ctx", "heads"),
        P("ctx", "heads"),
        P("ctx", "heads"),
        P(None, "heads"),
        P(None, "heads"),
        P(None, "heads"),
        P("ctx", "heads"),
        P("ctx", "heads"),
        P("heads"),
        P("heads"),
        P(),
        P("ctx", "heads"),
        P("heads", None),
    )
    out_specs = P("ctx", "heads")
    return jax.shard_map(shards, mesh=mesh, in_specs=in_specs, out_specs=out_specs, check_vma=False)
```

```python
import functools

import jax
import jax.numpy as jnp
from jax import lax
from jax.experimental import pallas as pl
from jax.experimental.pallas import tpu as pltpu
from jax.sharding import PartitionSpec as P

DK = 128
DV = 128
TAIL = 16
MESH = pl.DeviceIdType.MESH
F32 = jnp.float32
BF16 = jnp.bfloat16
HIGHEST = lax.Precision.HIGHEST


def split(value):
    high = value.astype(BF16)
    return high, (value - high.astype(F32)).astype(BF16)


def mm(left, right):
    return jnp.dot(left, right, preferred_element_type=F32)


def one_pass(left, right):
    return mm(left.astype(BF16), right.astype(BF16))


def split_left(left, right):
    high, low = split(left)
    return mm(jnp.concatenate([high, low], axis=1), jnp.concatenate([right, right], axis=0))


def split_right(left, right):
    high, low = split(right)
    return mm(jnp.concatenate([left, left], axis=1), jnp.concatenate([high, low], axis=0))


def split_both(left, right):
    left_high, left_low = split(left)
    right_high, right_low = split(right)
    return mm(
        jnp.concatenate([left_high, left_low], axis=1),
        jnp.concatenate([right_high, right_high], axis=0),
    ) + mm(left_high, right_low)


def silu(value):
    return value * (1.0 / (1.0 + jnp.exp(-value)))


def three_parts(value):
    first = value.astype(BF16).astype(F32)
    second = (value - first).astype(BF16).astype(F32)
    return first, second, value - first - second


def pack_decay(decay, width):
    row = lax.broadcasted_iota(jnp.int32, (TAIL, width), 0)
    first, second, third = three_parts(decay)
    zero = jnp.zeros((TAIL, width), F32)
    block = jnp.where(row == 0, first, jnp.where(row == 1, second, jnp.where(row == 2, third, zero)))
    return block.astype(BF16)


def kernel(
    nx,
    ny,
    nz,
    q_hbm,
    k_hbm,
    v_hbm,
    z_hbm,
    w_hbm,
    a_hbm,
    b_hbm,
    alog_hbm,
    bias_hbm,
    gain_hbm,
    cq_hbm,
    ck_hbm,
    cv_hbm,
    out_ref,
    q_in,
    k_in,
    v_in,
    z_in,
    w_in,
    a_ref,
    b_ref,
    alog_ref,
    bias_ref,
    gain_ref,
    cq_ref,
    ck_ref,
    cv_ref,
    halo_q,
    halo_k,
    halo_v,
    ext,
    vc_all,
    kc_all,
    qc_all,
    chunk_maps,
    up_out,
    up_in,
    carry,
    pre_state,
    pre_map,
    pre_decay,
    sigma,
    down_out,
    down_in,
    reads,
    local,
    normed,
    rs_out,
    rs_in,
    load_sem,
    halo_send,
    halo_recv,
    chip_send,
    chip_recv,
    up_send,
    up_recv,
    y_send,
    y_recv,
    down_send,
    down_recv,
    pass_send,
    pass_recv,
    rs_send,
    rs_recv,
):
    rows = q_in.shape[0]
    key_heads = nz // 2
    ring = 2 * nz
    count = ny * ring
    me = lax.axis_index("ctx")
    x = lax.axis_index("heads")
    y = me // ring
    place = lax.rem(me, ring)
    z = place // 2
    core = lax.rem(place, 2)
    partner = me + 1 - 2 * core
    width = out_ref.shape[1]

    def first_head(chip):
        return lax.rem(2 * (chip // 2 + 1), nz)

    base = first_head(z)
    own_slots = [2 * (core + 2 * g) + p for g in range(nz // 4) for p in range(2)]
    other_slots = [2 * (1 - core + 2 * g) + p for g in range(nz // 4) for p in range(2)]

    def head_of(slot):
        return lax.rem(base + slot, nz)

    def owner_of(slot):
        return y * ring + 2 * head_of(slot)

    loads = [
        pltpu.make_async_copy(source, target, load_sem.at[i])
        for i, (source, target) in enumerate(
            (
                (a_hbm, a_ref),
                (b_hbm, b_ref),
                (alog_hbm, alog_ref),
                (bias_hbm, bias_ref),
                (ck_hbm, ck_ref),
                (cv_hbm, cv_ref),
                (cq_hbm, cq_ref),
                (k_hbm, k_in),
                (v_hbm, v_in),
                (q_hbm, q_in),
                (gain_hbm, gain_ref),
                (z_hbm, z_in),
                (w_hbm, w_in),
            )
        )
    ]
    for load in loads:
        load.start()

    barrier = pltpu.get_barrier_semaphore()

    def greet(ctx, heads):
        pl.semaphore_signal(barrier, inc=1, device_id=(ctx, heads), device_id_type=MESH)

    for step in range(1, ring):
        greet(y * ring + lax.rem(place + step, ring), x)
    for step in range(1, ny):
        greet(lax.rem(me + step * ring, count), x)
    for step in range(1, nx):
        greet(me, lax.rem(x + step, nx))
    over = jnp.logical_and(place == ring - 1, me < count - 1)
    under = jnp.logical_and(place == 0, me > 0)

    @pl.when(over)
    def _():
        greet(me + 1, x)

    @pl.when(under)
    def _():
        greet(me - 1, x)

    pl.semaphore_wait(
        barrier,
        (ring - 1) + (ny - 1) + (nx - 1) + over.astype(jnp.int32) + under.astype(jnp.int32),
    )

    def halo_copies(ctx):
        return [
            pltpu.make_async_remote_copy(
                src_ref=source.at[pl.ds(rows - TAIL, TAIL), :],
                dst_ref=target,
                send_sem=halo_send.at[i],
                recv_sem=halo_recv.at[i],
                device_id=(ctx, x),
                device_id_type=MESH,
            )
            for i, (source, target) in enumerate(
                ((k_hbm, halo_k), (v_hbm, halo_v), (q_hbm, halo_q))
            )
        ]

    following = lax.rem(me + 1, count)

    @pl.when(me < count - 1)
    def _():
        for copy in halo_copies(following):
            copy.start()

    @pl.when(me == 0)
    def _():
        halo_k[...] = jnp.zeros_like(halo_k)
        halo_v[...] = jnp.zeros_like(halo_v)
        halo_q[...] = jnp.zeros_like(halo_q)

    row = lax.broadcasted_iota(jnp.int32, (rows, rows), 0)
    col = lax.broadcasted_iota(jnp.int32, (rows, rows), 1)
    upto = row >= col
    strict = row > col
    apart = jnp.bitwise_xor(row, col)
    for load in loads[:4]:
        load.wait()
    head_row = lax.broadcasted_iota(jnp.int32, (nz, nz), 0)
    head_lane = lax.broadcasted_iota(jnp.int32, (nz, nz), 1)

    def per_head(values):
        return jnp.sum(jnp.where(head_row == head_lane, values, 0.0), axis=1, keepdims=True)

    gate_in = a_ref[...] + per_head(bias_ref[...])
    softplus = jnp.maximum(gate_in, 0.0) + jnp.log1p(jnp.exp(-jnp.abs(gate_in)))
    logdecay = -jnp.exp(per_head(alog_ref[...])) * softplus
    beta = 1.0 / (1.0 + jnp.exp(-b_ref[...]))
    cumulative = jnp.dot(
        logdecay, jnp.where(row <= col, 1.0, 0.0), preferred_element_type=F32, precision=HIGHEST
    )
    slot = lax.broadcasted_iota(jnp.int32, (128, nz), 0)
    from_head = lax.broadcasted_iota(jnp.int32, (128, nz), 1)

    def placing(first):
        wanted = base + slot - first
        wanted = jnp.where(wanted >= nz, wanted - nz, wanted)
        inside = jnp.logical_and(slot >= first, slot < first + nz)
        return jnp.where(jnp.logical_and(inside, wanted == from_head), 1.0, 0.0)

    columns = jnp.transpose(
        jnp.dot(placing(0), cumulative, preferred_element_type=F32, precision=HIGHEST)
        + jnp.dot(placing(nz), beta, preferred_element_type=F32, precision=HIGHEST)
    )

    def conv(before, data, taps_ref, start, size, count_rows):
        cols = pl.ds(pl.multiple_of(start, 128), size)
        ext[0:8, 0:size] = before
        ext[8 : 8 + count_rows, 0:size] = data[0:count_rows, cols].astype(F32)
        taps = taps_ref[:, cols].astype(F32)
        total = jnp.zeros((count_rows, size), F32)
        for j in range(4):
            total = total + taps[j : j + 1] * ext[5 + j : 5 + j + count_rows, 0:size]
        return silu(total).astype(BF16)

    def inverse_norm(block):
        entries = block.astype(F32)
        return lax.rsqrt(jnp.sum(entries * entries, axis=1, keepdims=True) + 1e-6)

    for load in loads[4:10]:
        load.wait()

    streams = (
        (k_in, halo_k, ck_ref, kc_all, DK),
        (v_in, halo_v, cv_ref, vc_all, 2 * DV),
        (q_in, halo_q, cq_ref, qc_all, DK),
    )
    for s in range(key_heads):
        kh = lax.rem(base // 2 + s, key_heads)
        for data, halo, taps_ref, result, size in streams:
            before = jnp.zeros((8, size), F32)
            result[s] = conv(before, data, taps_ref, kh * size, size, rows)

    @pl.when(me > 0)
    def _():
        for copy in halo_copies(following):
            copy.wait_recv()

    wide_lane = lax.broadcasted_iota(jnp.int32, (rows, 128), 1)
    for s in range(key_heads):
        kh = lax.rem(base // 2 + s, key_heads)
        for data, halo, taps_ref, result, size in streams:
            cols = pl.ds(pl.multiple_of(kh * size, 128), size)
            before = halo[:, cols].astype(F32)[8:16]
            result[s, 0:TAIL, :] = conv(before, data, taps_ref, kh * size, size, TAIL)
        columns = jnp.where(wide_lane == 2 * nz + s, inverse_norm(kc_all[s]), columns)
        columns = jnp.where(
            wide_lane == 2 * nz + key_heads + s, inverse_norm(qc_all[s]) * DK**-0.5, columns
        )
    by_row = jnp.transpose(columns)

    def column(index):
        return columns[:, index : index + 1]

    def lane_row(index):
        return by_row[index : index + 1, :]

    def chip_copy(slot):
        return pltpu.make_async_remote_copy(
            src_ref=chunk_maps.at[core, slot],
            dst_ref=chunk_maps.at[core, slot],
            send_sem=chip_send.at[slot],
            recv_sem=chip_recv.at[slot],
            device_id=(partner, x),
            device_id_type=MESH,
        )

    def chip_wait(slot):
        pltpu.make_async_remote_copy(
            src_ref=chunk_maps.at[core, slot],
            dst_ref=chunk_maps.at[1 - core, slot],
            send_sem=chip_send.at[slot],
            recv_sem=chip_recv.at[slot],
            device_id=(partner, x),
            device_id_type=MESH,
        ).wait_recv()

    def up_copy(index, slot):
        return pltpu.make_async_remote_copy(
            src_ref=up_out.at[index],
            dst_ref=up_in.at[z],
            send_sem=up_send.at[index],
            recv_sem=up_recv.at[z],
            device_id=(owner_of(slot), x),
            device_id_type=MESH,
        )

    keys = range(key_heads)
    heads = range(nz)
    gram, query_gram = {}, {}
    for s in keys:
        kc_t = kc_all[s]
        contract = (((1,), (1,)), ((), ()))
        gram[s] = lax.dot_general(kc_t, kc_t, contract, preferred_element_type=F32)
        query_gram[s] = lax.dot_general(
            qc_all[s], kc_t, contract, preferred_element_type=F32
        )
    within, lower, inverse = {}, {}, {}
    for h in heads:
        s = h // 2
        gaps = column(h) - lane_row(h)
        within[h] = jnp.exp(jnp.where(upto, gaps, -1e30)) * lane_row(2 * nz + s)
        scale = column(nz + h) * column(2 * nz + s)
        lower[h] = jnp.where(strict, scale * gram[s] * within[h], 0.0)
        inverse[h] = jnp.where(apart == 1, -lower[h], 0.0)
    level = 1
    while (1 << level) < rows:
        block, inner = {}, {}
        for h in heads:
            block[h] = jnp.where((apart >> level) == 1, lower[h], 0.0)
            inner[h] = block[h] + one_pass(block[h], inverse[h])
        for h in heads:
            inverse[h] = inverse[h] - inner[h] - one_pass(inverse[h], inner[h])
        level += 1
    values, maps = {}, {}
    for h in heads:
        s = h // 2
        solve = jnp.where(row == col, 1.0, inverse[h]) * lane_row(nz + h)
        values[h] = split_left(solve, vc_all[s, :, (h % 2) * 128 : (h % 2 + 1) * 128])
        key_solve = solve * (jnp.exp(lane_row(h)) * lane_row(2 * nz + s))
        maps[h] = split_left(key_solve, kc_all[s])
    for h in heads:
        s = h // 2
        last = columns[rows - 1 : rows, h : h + 1]
        tail = jnp.exp(last - column(h)) * column(2 * nz + s)
        both = jnp.concatenate([values[h] * tail, maps[h] * tail], axis=1)
        kc_t = jnp.transpose(kc_all[s].astype(F32)).astype(BF16)
        chunk_maps[core, h, 0:DK, :] = split_right(kc_t, both).astype(BF16)
        chunk_maps[core, h, DK:, :] = pack_decay(jnp.exp(last), DK + DV)
    for h in heads:
        chip_copy(h).start()

    def read_out(h):
        s = h // 2
        attend = jnp.where(
            upto, query_gram[s] * within[h] * column(2 * nz + key_heads + s), 0.0
        )
        both = split_both(attend, jnp.concatenate([values[h], maps[h]], axis=1))
        local[h] = both[:, 0:DV]
        start = jnp.exp(column(h)) * column(2 * nz + key_heads + s)
        high, low = split(start * qc_all[s].astype(F32) - both[:, DV:])
        reads[h, :, 0:DK] = high
        reads[h, :, DK:] = low

    eye = lax.broadcasted_iota(jnp.int32, (DK, DK), 0) == lax.broadcasted_iota(
        jnp.int32, (DK, DK), 1
    )

    def decay_of(block):
        return jnp.sum(block.astype(F32), axis=0, keepdims=True)

    def with_map(message, decay):
        map_part = jnp.where(eye, decay[:, 0:DK], 0.0) - message[0:DK, DV:].astype(F32)
        return jnp.concatenate([message[0:DK, 0:DV].astype(F32), map_part], axis=1)

    def compose(message, carried):
        decay = decay_of(message[DK:, :])
        fresh = jnp.concatenate(
            [message[0:DK, 0:DV].astype(F32), jnp.zeros((DK, DK), F32)], axis=1
        )
        return decay, decay * carried - mm(message[0:DK, DV:], carried.astype(BF16)) + fresh

    def put_message(target, carried, total_decay):
        target[0:DK, 0:DV] = carried[:, 0:DV].astype(BF16)
        target[0:DK, DV:] = (
            jnp.where(eye, total_decay[:, 0:DK], 0.0) - carried[:, DV:]
        ).astype(BF16)
        target[DK:, :] = pack_decay(total_decay[:, 0:1], DK + DV)

    for h in heads[: nz // 2]:
        read_out(h)
    for slot in own_slots:
        chip_wait(slot)
    joined = []
    for slot in own_slots:
        early, late = chunk_maps[0, slot], chunk_maps[1, slot]
        early_decay = decay_of(early[DK:, :])
        decay, carried = compose(late, with_map(early, early_decay))
        joined.append((carried, early_decay * decay))
    for index, slot in enumerate(own_slots):
        put_message(up_out.at[index], *joined[index])
        up_copy(index, slot).start()
    for h in heads[nz // 2 :]:
        read_out(h)

    for slot in other_slots:
        chip_wait(slot)

    @pl.when(core == 1)
    def _():
        for h in heads:
            early = chunk_maps[0, h]
            decay = decay_of(early[DK:, 0:DK])
            moved = mm(reads[h], jnp.concatenate([early[0:DK, :], early[0:DK, :]], axis=0))
            local[h] = local[h] + moved[:, 0:DV]
            whole = reads[h, :, 0:DK].astype(F32) + reads[h, :, DK:].astype(F32)
            high, low = split(decay * whole - moved[:, DV:])
            reads[h, :, 0:DK] = high
            reads[h, :, DK:] = low

    def carry_copy(source, target_y):
        return pltpu.make_async_remote_copy(
            src_ref=carry.at[source],
            dst_ref=carry.at[source],
            send_sem=y_send.at[target_y],
            recv_sem=y_recv.at[source],
            device_id=(target_y * ring + place, x),
            device_id_type=MESH,
        )

    def down_copy(chip):
        slot = lax.rem(z - first_head(chip) + nz, nz)
        return pltpu.make_async_remote_copy(
            src_ref=down_out.at[chip],
            dst_ref=down_in.at[slot],
            send_sem=down_send.at[chip],
            recv_sem=down_recv.at[slot],
            device_id=(y * ring + 2 * chip + lax.rem(slot // 2, 2), x),
            device_id_type=MESH,
        )

    @pl.when(core == 0)
    def _():
        pre_state[0] = jnp.zeros((DK, DV), F32)
        pre_map[0] = jnp.zeros((DK, DK), BF16)
        pre_decay[0] = jnp.ones((8, 128), F32)
        total_decay = None
        carried = None
        for j in range(nz):
            pltpu.make_async_remote_copy(
                src_ref=up_out.at[0],
                dst_ref=up_in.at[j],
                send_sem=up_send.at[0],
                recv_sem=up_recv.at[j],
                device_id=(partner, x),
                device_id_type=MESH,
            ).wait_recv()
            message = up_in[j]
            if j == 0:
                total_decay = decay_of(message[DK:, :])
                carried = with_map(message, total_decay)
            else:
                decay, carried = compose(message, carried)
                total_decay = total_decay * decay
            if j < nz - 1:
                pre_state[j + 1] = carried[:, 0:DV]
                pre_map[j + 1] = (
                    jnp.where(eye, total_decay[:, 0:DK], 0.0) - carried[:, DV:]
                ).astype(BF16)
                pre_decay[j + 1] = jnp.broadcast_to(total_decay[:, 0:128], (8, 128))
        put_message(carry.at[y], carried, total_decay)

        for later in range(1, ny):

            @pl.when(y < later)
            def _(later=later):
                carry_copy(y, later).start()

        sigma[...] = jnp.zeros((DK, DV), F32)
        for earlier in range(ny - 1):

            @pl.when(y > earlier)
            def _(earlier=earlier):
                carry_copy(earlier, y).wait_recv()
                message = carry[earlier]
                state = sigma[...]
                sigma[...] = (
                    decay_of(message[DK:, 0:DV]) * state
                    - mm(message[0:DK, DV:], state.astype(BF16))
                    + message[0:DK, 0:DV].astype(F32)
                )

        start_state = sigma[...]
        rounded = start_state.astype(BF16)
        for offset in sorted(range(nz), key=lambda offset: -min(offset, nz - offset)):
            chip = lax.rem(z + offset, nz)
            down_out[chip] = (
                pre_decay[chip, 0:1, :] * start_state - mm(pre_map[chip], rounded) + pre_state[chip]
            ).astype(BF16)
            down_copy(chip).start()

    def pass_copy(slot):
        return pltpu.make_async_remote_copy(
            src_ref=down_in.at[slot],
            dst_ref=down_in.at[slot],
            send_sem=pass_send.at[slot],
            recv_sem=pass_recv.at[slot],
            device_id=(partner, x),
            device_id_type=MESH,
        )

    for load in loads[10:]:
        load.wait()
    nearest = own_slots[len(own_slots) // 2 :] + own_slots[: len(own_slots) // 2]
    for slot in nearest:
        pltpu.make_async_remote_copy(
            src_ref=down_out.at[0],
            dst_ref=down_in.at[slot],
            send_sem=down_send.at[0],
            recv_sem=down_recv.at[slot],
            device_id=(owner_of(slot), x),
            device_id_type=MESH,
        ).wait_recv()
        pass_copy(slot).start()

    def finish(slots):
        cores = []
        for slot in slots:
            state = down_in[slot]
            cores.append(mm(reads[slot], jnp.concatenate([state, state], axis=0)) + local[slot])
        for slot, core_out in zip(slots, cores):
            head = head_of(slot)
            cols = pl.ds(pl.multiple_of(head * DV, DV), DV)
            power = jnp.mean(core_out * core_out, axis=1, keepdims=True)
            gated = core_out * lax.rsqrt(power + 1e-6) * gain_ref[...]
            normed[:, cols] = (gated * silu(z_in[:, cols].astype(F32))).astype(BF16)

    finish(nearest)
    for slot in other_slots:
        pass_copy(slot).wait_recv()
    finish(other_slots)

    def part(step):
        cols = pl.ds(pl.multiple_of(lax.rem(x + step, nx) * width, 128), width)
        return mm(normed[...], w_in[:, cols])

    def rs_copy(step):
        return pltpu.make_async_remote_copy(
            src_ref=rs_out.at[step - 1],
            dst_ref=rs_in.at[step - 1],
            send_sem=rs_send.at[step - 1],
            recv_sem=rs_recv.at[step - 1],
            device_id=(me, lax.rem(x + step, nx)),
            device_id_type=MESH,
        )

    order = sorted(range(1, nx), key=lambda step: -min(step, nx - step))
    for step in order:
        rs_out[step - 1] = part(step).astype(BF16)
        rs_copy(step).start()
    total = part(0)
    for step in reversed(order):
        rs_copy(step).wait_recv()
        total = total + rs_in[step - 1].astype(F32)
    out_ref[...] = total

    @pl.when(me < count - 1)
    def _():
        for copy in halo_copies(following):
            copy.wait_send()

    for h in heads:
        chip_copy(h).wait_send()
    for index, slot in enumerate(own_slots):
        up_copy(index, slot).wait_send()
        pass_copy(slot).wait_send()

    @pl.when(core == 0)
    def _():
        for chip in range(nz):
            down_copy(chip).wait_send()
        for later in range(1, ny):

            @pl.when(y < later)
            def _(later=later):
                carry_copy(y, later).wait_send()

    for step in order:
        rs_copy(step).wait_send()


def shards(
    q_in, k_in, v_in, conv_q, conv_k, conv_v, a_in, b_in, a_log, dt_bias, norm_weight, z_in, out_weight
):
    rows = q_in.shape[0]
    nz = v_in.shape[1] // DV
    nx = lax.axis_size("heads")
    ny = lax.axis_size("ctx") // (2 * nz)
    key_heads = nz // 2
    width = out_weight.shape[1] // nx
    hbm = pl.BlockSpec(memory_space=pltpu.HBM)
    vmem = pl.BlockSpec(memory_space=pltpu.VMEM)
    dma = pltpu.SemaphoreType.DMA
    message = (DK + TAIL, DK + DV)
    scratch = [
        pltpu.VMEM(q_in.shape, BF16),
        pltpu.VMEM(k_in.shape, BF16),
        pltpu.VMEM(v_in.shape, BF16),
        pltpu.VMEM(z_in.shape, BF16),
        pltpu.VMEM(out_weight.shape, BF16),
        pltpu.VMEM((nz, rows), F32),
        pltpu.VMEM((nz, rows), F32),
        pltpu.VMEM((1, nz), F32),
        pltpu.VMEM((1, nz), F32),
        pltpu.VMEM((1, DV), F32),
        pltpu.VMEM(conv_q.shape, BF16),
        pltpu.VMEM(conv_k.shape, BF16),
        pltpu.VMEM(conv_v.shape, BF16),
        pltpu.VMEM((TAIL, q_in.shape[1]), BF16),
        pltpu.VMEM((TAIL, k_in.shape[1]), BF16),
        pltpu.VMEM((TAIL, v_in.shape[1]), BF16),
        pltpu.VMEM((rows + 8, 2 * DV), F32),
        pltpu.VMEM((key_heads, rows, 2 * DV), BF16),
        pltpu.VMEM((key_heads, rows, DK), BF16),
        pltpu.VMEM((key_heads, rows, DK), BF16),
        pltpu.VMEM((2, nz) + message, BF16),
        pltpu.VMEM((nz // 2,) + message, BF16),
        pltpu.VMEM((nz,) + message, BF16),
        pltpu.VMEM((ny,) + message, BF16),
        pltpu.VMEM((nz, DK, DV), F32),
        pltpu.VMEM((nz, DK, DK), BF16),
        pltpu.VMEM((nz, 8, 128), F32),
        pltpu.VMEM((DK, DV), F32),
        pltpu.VMEM((nz, DK, DV), BF16),
        pltpu.VMEM((nz, DK, DV), BF16),
        pltpu.VMEM((nz, rows, 2 * DK), BF16),
        pltpu.VMEM((nz, rows, DV), F32),
        pltpu.VMEM((rows, nz * DV), BF16),
        pltpu.VMEM((nx - 1, rows, width), BF16),
        pltpu.VMEM((nx - 1, rows, width), BF16),
        dma((13,)),
        dma((3,)),
        dma((3,)),
        dma((nz,)),
        dma((nz,)),
        dma((nz // 2,)),
        dma((nz,)),
        dma((ny,)),
        dma((ny,)),
        dma((nz,)),
        dma((nz,)),
        dma((nz,)),
        dma((nz,)),
        dma((nx - 1,)),
        dma((nx - 1,)),
    ]
    call = pl.pallas_call(
        functools.partial(kernel, nx, ny, nz),
        out_shape=jax.ShapeDtypeStruct((rows, width), F32),
        in_specs=[hbm] * 13,
        out_specs=vmem,
        scratch_shapes=scratch,
        compiler_params=pltpu.CompilerParams(
            collective_id=0, has_side_effects=True, vmem_limit_bytes=60 * 1024 * 1024
        ),
        cost_estimate=pl.CostEstimate(
            flops=2_000_000_000, bytes_accessed=6_000_000, transcendentals=1_000_000
        ),
    )
    return call(
        q_in,
        k_in,
        v_in,
        z_in,
        out_weight,
        a_in.T,
        b_in.T,
        a_log.reshape(1, nz),
        dt_bias.reshape(1, nz),
        norm_weight.reshape(1, DV),
        conv_q,
        conv_k,
        conv_v,
    )


def solution(mesh):
    in_specs = (
        P("ctx", "heads"),
        P("ctx", "heads"),
        P("ctx", "heads"),
        P(None, "heads"),
        P(None, "heads"),
        P(None, "heads"),
        P("ctx", "heads"),
        P("ctx", "heads"),
        P("heads"),
        P("heads"),
        P(),
        P("ctx", "heads"),
        P("heads", None),
    )
    out_specs = P("ctx", "heads")
    return jax.shard_map(shards, mesh=mesh, in_specs=in_specs, out_specs=out_specs, check_vma=False)
```

```python
import functools

import jax
import jax.numpy as jnp
from jax import lax
from jax.experimental import pallas as pl
from jax.experimental.pallas import tpu as pltpu
from jax.sharding import PartitionSpec as P

DK = 128
DV = 128
TAIL = 16
MESH = pl.DeviceIdType.MESH
F32 = jnp.float32
BF16 = jnp.bfloat16
HIGHEST = lax.Precision.HIGHEST


def split(value):
    high = value.astype(BF16)
    return high, (value - high.astype(F32)).astype(BF16)


def mm(left, right):
    return jnp.dot(left, right, preferred_element_type=F32)


def one_pass(left, right):
    return mm(left.astype(BF16), right.astype(BF16))


def split_left(left, right):
    high, low = split(left)
    return mm(jnp.concatenate([high, low], axis=1), jnp.concatenate([right, right], axis=0))


def split_right(left, right):
    high, low = split(right)
    return mm(jnp.concatenate([left, left], axis=1), jnp.concatenate([high, low], axis=0))


def split_both(left, right):
    left_high, left_low = split(left)
    right_high, right_low = split(right)
    return mm(
        jnp.concatenate([left_high, left_low], axis=1),
        jnp.concatenate([right_high, right_high], axis=0),
    ) + mm(left_high, right_low)


def silu(value):
    return value * (1.0 / (1.0 + jnp.exp(-value)))


def three_parts(value):
    first = value.astype(BF16).astype(F32)
    second = (value - first).astype(BF16).astype(F32)
    return first, second, value - first - second


def pack_decay(decay, width):
    row = lax.broadcasted_iota(jnp.int32, (TAIL, width), 0)
    first, second, third = three_parts(decay)
    zero = jnp.zeros((TAIL, width), F32)
    block = jnp.where(row == 0, first, jnp.where(row == 1, second, jnp.where(row == 2, third, zero)))
    return block.astype(BF16)


def kernel(
    nx,
    ny,
    nz,
    q_hbm,
    k_hbm,
    v_hbm,
    z_hbm,
    w_hbm,
    a_hbm,
    b_hbm,
    alog_hbm,
    bias_hbm,
    gain_hbm,
    cq_hbm,
    ck_hbm,
    cv_hbm,
    out_ref,
    q_in,
    k_in,
    v_in,
    z_in,
    w_in,
    a_in,
    b_in,
    alog_ref,
    bias_ref,
    gain_ref,
    cq_ref,
    ck_ref,
    cv_ref,
    halo_q,
    halo_k,
    halo_v,
    ext,
    qc_all,
    kc_all,
    vc_all,
    up_out,
    up_in,
    carry,
    pre_state,
    pre_map,
    pre_decay,
    sigma,
    down_out,
    down_in,
    reads,
    local,
    normed,
    pass_out,
    rs_out,
    rs_in,
    load_sem,
    swap_send,
    swap_recv,
    halo_send,
    halo_recv,
    up_send,
    up_recv,
    y_send,
    y_recv,
    down_send,
    down_recv,
    pass_sem,
    rs_send,
    rs_recv,
):
    rows = out_ref.shape[0]
    width = out_ref.shape[1]
    set_heads = nz // 2
    set_keys = nz // 4
    ring = 2 * nz
    count = ny * ring
    me = lax.axis_index("ctx")
    x = lax.axis_index("heads")
    y = me // ring
    place = lax.rem(me, ring)
    z = place // 2
    core = lax.rem(place, 2)
    chip = me // 2
    chips = count // 2
    partner = me + 1 - 2 * core
    heads = range(set_heads)
    keys = range(set_keys)
    both_shards = range(2)
    units = [(u, h) for u in both_shards for h in heads]
    key_units = [(u, s) for u in both_shards for s in keys]

    sender_core = z // set_heads
    owns = core != sender_core

    def owner_of(h):
        return y * ring + 2 * (set_heads * core + h) + 1 - core

    def cols_of(which, size):
        return pl.ds(pl.multiple_of(which * size, 128), size)

    streams = (
        (k_hbm, k_in, halo_k, ck_ref, kc_all, set_keys * DK),
        (v_hbm, v_in, halo_v, cv_ref, vc_all, set_heads * DV),
        (q_hbm, q_in, halo_q, cq_ref, qc_all, set_keys * DK),
    )
    wide = [(source, target, size) for source, target, _, _, _, size in streams]
    wide.append((z_hbm, z_in, set_heads * DV))
    pairs = [(source.at[:, cols_of(core, size)], target.at[core]) for source, target, size in wide]
    pairs += [
        (a_hbm, a_in.at[core]),
        (b_hbm, b_in.at[core]),
        (alog_hbm, alog_ref),
        (bias_hbm, bias_ref),
        (ck_hbm, ck_ref),
        (cv_hbm, cv_ref),
        (cq_hbm, cq_ref),
        (gain_hbm, gain_ref),
        (w_hbm, w_in),
    ]
    loads = [
        pltpu.make_async_copy(source, target, load_sem.at[i])
        for i, (source, target) in enumerate(pairs)
    ]
    first = [0, 1, 2, 8, 9, 10, 4, 5, 6, 7]
    rest = [3, 11, 12]
    for i in first + rest:
        loads[i].start()

    barrier = pltpu.get_barrier_semaphore()

    def greet(ctx, heads):
        pl.semaphore_signal(barrier, inc=1, device_id=(ctx, heads), device_id_type=MESH)

    for step in range(1, ring):
        greet(y * ring + lax.rem(place + step, ring), x)
    for step in range(1, ny):
        greet(lax.rem(me + step * ring, count), x)
    for step in range(1, nx):
        greet(me, lax.rem(x + step, nx))
    over = jnp.logical_and(place == ring - 1, me < count - 1)
    under = jnp.logical_and(z == 0, y > 0)

    @pl.when(over)
    def _():
        greet(me + 1, x)
        greet(me + 2, x)

    @pl.when(under)
    def _():
        greet(y * ring - 1, x)

    pl.semaphore_wait(
        barrier,
        (ring - 1) + (ny - 1) + (nx - 1) + 2 * over.astype(jnp.int32) + under.astype(jnp.int32),
    )

    def halo_copies(side):
        return [
            pltpu.make_async_remote_copy(
                src_ref=source.at[pl.ds(rows - TAIL, TAIL), cols_of(side, size)],
                dst_ref=target,
                send_sem=halo_send.at[3 * side + i],
                recv_sem=halo_recv.at[i],
                device_id=(2 * lax.rem(chip + 1, chips) + side, x),
                device_id_type=MESH,
            )
            for i, (source, _, target, _, _, size) in enumerate(streams)
        ]

    sends_halo = jnp.logical_and(core == 1, chip < chips - 1)

    @pl.when(sends_halo)
    def _():
        for side in range(2):
            for copy in halo_copies(side):
                copy.start()

    def swap_copies(shard):
        return [
            pltpu.make_async_remote_copy(
                src_ref=source,
                dst_ref=target.at[shard],
                send_sem=swap_send.at[i],
                recv_sem=swap_recv.at[i],
                device_id=(partner, x),
                device_id_type=MESH,
            )
            for i, (source, target) in enumerate(
                [
                    (source.at[:, cols_of(1 - core, size)], target)
                    for source, target, size in wide[:3]
                ]
                + [(a_hbm, a_in), (b_hbm, b_in)]
                + [
                    (source.at[:, cols_of(1 - core, size)], target)
                    for source, target, size in wide[3:]
                ]
            )
        ]

    swap = swap_copies(core)
    swapped = swap_copies(1 - core)
    for copy in swap:
        copy.start()

    @pl.when(chip == 0)
    def _():
        halo_k[...] = jnp.zeros_like(halo_k)
        halo_v[...] = jnp.zeros_like(halo_v)
        halo_q[...] = jnp.zeros_like(halo_q)

    def conv(before, data, taps_ref, size):
        height = data.shape[0]
        ext[0:8, 0:size] = before
        ext[8 : 8 + height, 0:size] = data.astype(F32)
        taps = taps_ref[:, cols_of(core, size)].astype(F32)
        total = jnp.zeros((height, size), F32)
        for j in range(4):
            total = total + taps[j : j + 1] * ext[5 + j : 5 + j + height, 0:size]
        return silu(total).astype(BF16)

    for i in first:
        loads[i].wait()
    for _, data, _, taps_ref, result, size in streams:
        result[core] = conv(jnp.zeros((8, size), F32), data[core], taps_ref, size)

    row = lax.broadcasted_iota(jnp.int32, (rows, rows), 0)
    col = lax.broadcasted_iota(jnp.int32, (rows, rows), 1)
    upto = row >= col
    strict = row > col
    apart = jnp.bitwise_xor(row, col)

    for i in range(3):
        swapped[i].wait_recv()
    for _, data, _, taps_ref, result, size in streams:
        result[1 - core] = conv(jnp.zeros((8, size), F32), data[1 - core], taps_ref, size)

    for i in range(3, 5):
        swapped[i].wait_recv()
    head_row = lax.broadcasted_iota(jnp.int32, (nz, nz), 0)
    head_lane = lax.broadcasted_iota(jnp.int32, (nz, nz), 1)

    def per_head(values):
        return jnp.sum(jnp.where(head_row == head_lane, values, 0.0), axis=1, keepdims=True)

    slot = lax.broadcasted_iota(jnp.int32, (128, nz), 0)
    from_head = lax.broadcasted_iota(jnp.int32, (128, nz), 1)

    def placing(start):
        wanted = set_heads * core + slot - start
        inside = jnp.logical_and(slot >= start, slot < start + set_heads)
        return jnp.where(jnp.logical_and(inside, wanted == from_head), 1.0, 0.0)

    def exact(left, right):
        return jnp.dot(left, right, preferred_element_type=F32, precision=HIGHEST)

    bias, rate = per_head(bias_ref[...]), jnp.exp(per_head(alog_ref[...]))
    before_or_at = jnp.where(row <= col, 1.0, 0.0)
    by_row = jnp.zeros((128, rows), F32)
    for u in both_shards:
        gate_in = a_in[u] + bias
        softplus = jnp.maximum(gate_in, 0.0) + jnp.log1p(jnp.exp(-jnp.abs(gate_in)))
        cumulative = exact(-rate * softplus, before_or_at)
        beta = 1.0 / (1.0 + jnp.exp(-b_in[u]))
        by_row = by_row + exact(placing(16 * u), cumulative)
        by_row = by_row + exact(placing(16 * u + set_heads), beta)
    columns = jnp.transpose(by_row)

    @pl.when(chip > 0)
    def _():
        for copy in halo_copies(0):
            copy.wait_recv()

    def inverse_norm(block):
        entries = block.astype(F32)
        return lax.rsqrt(jnp.sum(entries * entries, axis=1, keepdims=True) + 1e-6)

    for _, data, halo, taps_ref, result, size in streams:
        for u in both_shards:
            before = halo[...] if u == 0 else data[0, rows - TAIL : rows, :]
            result[u, 0:TAIL, :] = conv(
                before.astype(F32)[8:16], data[u, 0:TAIL, :], taps_ref, size
            )

    def key_of(u, s):
        return kc_all[u, :, s * DK : (s + 1) * DK]

    def query_of(u, s):
        return qc_all[u, :, s * DK : (s + 1) * DK]

    wide_lane = lax.broadcasted_iota(jnp.int32, (rows, 128), 1)
    for u, s in key_units:
        place_of = 16 * u + 2 * set_heads + s
        columns = jnp.where(wide_lane == place_of, inverse_norm(key_of(u, s)), columns)
        columns = jnp.where(
            wide_lane == place_of + set_keys, inverse_norm(query_of(u, s)) * DK**-0.5, columns
        )
    by_row = jnp.transpose(columns)

    def column(u, index):
        return columns[:, 16 * u + index : 16 * u + index + 1]

    def lane_row(u, index):
        return by_row[16 * u + index : 16 * u + index + 1, :]

    gram, query_gram, key_t = {}, {}, {}
    for u, s in key_units:
        contract = (((1,), (1,)), ((), ()))
        gram[u, s] = lax.dot_general(
            key_of(u, s), key_of(u, s), contract, preferred_element_type=F32
        )
        query_gram[u, s] = lax.dot_general(
            query_of(u, s), key_of(u, s), contract, preferred_element_type=F32
        )
        key_t[u, s] = jnp.transpose(key_of(u, s).astype(F32)).astype(BF16)
    within, lower, inverse = {}, {}, {}
    for u, h in units:
        s = h // 2
        gaps = column(u, h) - lane_row(u, h)
        within[u, h] = jnp.exp(jnp.where(upto, gaps, -1e30)) * lane_row(u, 2 * set_heads + s)
        scale = column(u, set_heads + h) * column(u, 2 * set_heads + s)
        lower[u, h] = jnp.where(strict, scale * gram[u, s] * within[u, h], 0.0)
        inverse[u, h] = jnp.where(apart == 1, -lower[u, h], 0.0)
    level = 1
    while (1 << level) < rows:
        inner = {}
        for i in units:
            block = jnp.where((apart >> level) == 1, lower[i], 0.0)
            inner[i] = block + one_pass(block, inverse[i])
        for i in units:
            inverse[i] = inverse[i] - inner[i] - one_pass(inverse[i], inner[i])
        level += 1
    values, maps, shard_maps, decays = {}, {}, {}, {}
    for u, h in units:
        s = h // 2
        solve = jnp.where(row == col, 1.0, inverse[u, h]) * lane_row(u, set_heads + h)
        values[u, h] = split_left(solve, vc_all[u, :, h * DV : (h + 1) * DV])
        key_solve = solve * (jnp.exp(lane_row(u, h)) * lane_row(u, 2 * set_heads + s))
        maps[u, h] = split_left(key_solve, key_of(u, s))
    for u, h in units:
        s = h // 2
        last = column(u, h)[rows - 1 : rows, :]
        tail = jnp.exp(last - column(u, h)) * column(u, 2 * set_heads + s)
        both = jnp.concatenate([values[u, h] * tail, maps[u, h] * tail], axis=1)
        shard_maps[u, h] = split_right(key_t[u, s], both)
        decays[u, h] = jnp.exp(last)

    eye = row[0:DK, 0:DK] == col[0:DK, 0:DK]

    def decay_of(block):
        return jnp.sum(block.astype(F32), axis=0, keepdims=True)

    def map_of(message, decay):
        return jnp.where(eye, decay[:, 0:1], 0.0) - message[:, DV:].astype(F32)

    def compose(message, decay, carried):
        state = decay * carried[:, 0:DV] + message[:, 0:DV].astype(F32)
        fresh = jnp.concatenate([state, decay * carried[:, DV:]], axis=1)
        return fresh - mm(message[:, DV:].astype(BF16), carried.astype(BF16))

    def put_message(target, carried, decay):
        target[0:DK, 0:DV] = carried[:, 0:DV].astype(BF16)
        target[0:DK, DV:] = map_of(carried, decay).astype(BF16)
        target[DK:, :] = pack_decay(decay, DK + DV)

    def up_copy(h):
        return pltpu.make_async_remote_copy(
            src_ref=up_out.at[h],
            dst_ref=up_in.at[z],
            send_sem=up_send.at[h],
            recv_sem=up_recv.at[z],
            device_id=(owner_of(h), x),
            device_id_type=MESH,
        )

    joined = {}
    for h in heads:
        early = shard_maps[0, h]
        carried = jnp.concatenate([early[:, 0:DV], map_of(early, decays[0, h])], axis=1)
        joined[h] = compose(shard_maps[1, h], decays[1, h], carried)
    for h in heads:
        put_message(up_out.at[h], joined[h], decays[0, h] * decays[1, h])
        up_copy(h).start()

    for u, h in units:
        s = h // 2
        scale = column(u, 2 * set_heads + set_keys + s)
        attend = jnp.where(upto, query_gram[u, s] * within[u, h] * scale, 0.0)
        both = split_both(attend, jnp.concatenate([values[u, h], maps[u, h]], axis=1))
        fixed = both[:, 0:DV]
        read = jnp.exp(column(u, h)) * scale * query_of(u, s).astype(F32) - both[:, DV:]
        if u == 1:
            moved = split_both(read, shard_maps[0, h])
            fixed = fixed + moved[:, 0:DV]
            read = decays[0, h] * read - moved[:, DV:]
        high, low = split(read)
        local[h, u * rows : (u + 1) * rows, :] = fixed
        reads[h, u * rows : (u + 1) * rows, 0:DK] = high
        reads[h, u * rows : (u + 1) * rows, DK:] = low

    def carry_copy(source, target_y):
        return pltpu.make_async_remote_copy(
            src_ref=carry.at[source],
            dst_ref=carry.at[source],
            send_sem=y_send.at[target_y],
            recv_sem=y_recv.at[source],
            device_id=(target_y * ring + place, x),
            device_id_type=MESH,
        )

    def down_copy(target):
        slot = lax.rem(z, set_heads)
        return pltpu.make_async_remote_copy(
            src_ref=down_out.at[target],
            dst_ref=down_in.at[slot],
            send_sem=down_send.at[target],
            recv_sem=down_recv.at[slot],
            device_id=(y * ring + 2 * target + sender_core, x),
            device_id_type=MESH,
        )

    @pl.when(owns)
    def _():
        pre_state[0] = jnp.zeros((DK, DV), F32)
        pre_map[0] = jnp.zeros((DK, DK), BF16)
        pre_decay[0] = jnp.ones((8, 128), F32)
        total_decay = None
        carried = None
        for j in range(nz):
            pltpu.make_async_remote_copy(
                src_ref=up_out.at[0],
                dst_ref=up_in.at[j],
                send_sem=up_send.at[0],
                recv_sem=up_recv.at[j],
                device_id=(partner, x),
                device_id_type=MESH,
            ).wait_recv()
            message = up_in[j, 0:DK, :]
            decay = decay_of(up_in[j, DK:, 0:DK])
            if j == 0:
                total_decay = decay
                carried = jnp.concatenate(
                    [message[:, 0:DV].astype(F32), map_of(message, decay)], axis=1
                )
            else:
                carried = compose(message, decay, carried)
                total_decay = total_decay * decay
            if j < nz - 1:
                pre_state[j + 1] = carried[:, 0:DV]
                pre_map[j + 1] = map_of(carried, total_decay).astype(BF16)
                pre_decay[j + 1] = jnp.broadcast_to(total_decay, (8, 128))
        put_message(carry.at[y], carried, total_decay[:, 0:1])

        for later in range(1, ny):

            @pl.when(y < later)
            def _(later=later):
                carry_copy(y, later).start()

        sigma[...] = jnp.zeros((DK, DV), F32)
        for earlier in range(ny - 1):

            @pl.when(y > earlier)
            def _(earlier=earlier):
                carry_copy(earlier, y).wait_recv()
                message = carry[earlier]
                state = sigma[...]
                sigma[...] = (
                    decay_of(message[DK:, 0:DV]) * state
                    - mm(message[0:DK, DV:], state.astype(BF16))
                    + message[0:DK, 0:DV].astype(F32)
                )

        start_state = sigma[...]
        rounded = start_state.astype(BF16)
        for offset in sorted(range(nz), key=lambda offset: -min(offset, nz - offset)):
            target = lax.rem(z + offset, nz)
            down_out[target] = (
                pre_decay[target, 0:1, :] * start_state
                - mm(pre_map[target], rounded)
                + pre_state[target]
            ).astype(BF16)
            down_copy(target).start()

    for i in rest:
        loads[i].wait()
    swapped[5].wait_recv()

    cores = {}
    for h in heads:
        pltpu.make_async_remote_copy(
            src_ref=down_out.at[0],
            dst_ref=down_in.at[h],
            send_sem=down_send.at[0],
            recv_sem=down_recv.at[h],
            device_id=(owner_of(h), x),
            device_id_type=MESH,
        ).wait_recv()
    for h in heads:
        state = down_in[h]
        cores[h] = mm(reads[h], jnp.concatenate([state, state], axis=0)) + local[h]
    hand_over = pltpu.make_async_remote_copy(
        src_ref=pass_out.at[1 - core],
        dst_ref=normed.at[core],
        send_sem=pass_sem.at[0],
        recv_sem=pass_sem.at[1],
        device_id=(partner, x),
        device_id_type=MESH,
    )
    for h in heads:
        power = jnp.mean(cores[h] * cores[h], axis=1, keepdims=True)
        gated = cores[h] * lax.rsqrt(power + 1e-6) * gain_ref[...]
        cols = slice(h * DV, (h + 1) * DV)
        for u in both_shards:
            gate = silu(z_in[u, :, cols].astype(F32))
            pass_out[u, :, cols] = (gated[u * rows : (u + 1) * rows] * gate).astype(BF16)
    hand_over.start()
    normed[core] = pass_out[core]
    pltpu.make_async_remote_copy(
        src_ref=pass_out.at[core],
        dst_ref=normed.at[1 - core],
        send_sem=pass_sem.at[0],
        recv_sem=pass_sem.at[1],
        device_id=(partner, x),
        device_id_type=MESH,
    ).wait_recv()

    depth = set_heads * DV

    def part(step):
        cols = cols_of(lax.rem(x + step, nx), width)
        return mm(normed[0], w_in[0:depth, cols]) + mm(normed[1], w_in[depth:, cols])

    def rs_copy(step):
        return pltpu.make_async_remote_copy(
            src_ref=rs_out.at[step - 1],
            dst_ref=rs_in.at[step - 1],
            send_sem=rs_send.at[step - 1],
            recv_sem=rs_recv.at[step - 1],
            device_id=(me, lax.rem(x + step, nx)),
            device_id_type=MESH,
        )

    order = sorted(range(1, nx), key=lambda step: -min(step, nx - step))
    for step in order:
        rs_out[step - 1] = part(step).astype(BF16)
        rs_copy(step).start()
    total = part(0)
    for step in reversed(order):
        rs_copy(step).wait_recv()
        total = total + rs_in[step - 1].astype(F32)
    out_ref[...] = total

    @pl.when(sends_halo)
    def _():
        for side in range(2):
            for copy in halo_copies(side):
                copy.wait_send()

    for copy in swap:
        copy.wait_send()
    for h in heads:
        up_copy(h).wait_send()

    @pl.when(owns)
    def _():
        for target in range(nz):
            down_copy(target).wait_send()
        for later in range(1, ny):

            @pl.when(y < later)
            def _(later=later):
                carry_copy(y, later).wait_send()

    hand_over.wait_send()
    for step in order:
        rs_copy(step).wait_send()


def shards(
    q_in, k_in, v_in, conv_q, conv_k, conv_v, a_in, b_in, a_log, dt_bias, norm_weight, z_in, out_weight
):
    rows = q_in.shape[0]
    nz = v_in.shape[1] // DV
    nx = lax.axis_size("heads")
    ny = lax.axis_size("ctx") // (2 * nz)
    width = out_weight.shape[1] // nx
    half = q_in.shape[1] // 2
    half_v = v_in.shape[1] // 2
    hbm = pl.BlockSpec(memory_space=pltpu.HBM)
    vmem = pl.BlockSpec(memory_space=pltpu.VMEM)
    dma = pltpu.SemaphoreType.DMA
    message = (DK + TAIL, DK + DV)
    scratch = [
        pltpu.VMEM((2, rows, half), BF16),
        pltpu.VMEM((2, rows, half), BF16),
        pltpu.VMEM((2, rows, half_v), BF16),
        pltpu.VMEM((2, rows, half_v), BF16),
        pltpu.VMEM(out_weight.shape, BF16),
        pltpu.VMEM((2, nz, rows), F32),
        pltpu.VMEM((2, nz, rows), F32),
        pltpu.VMEM((1, nz), F32),
        pltpu.VMEM((1, nz), F32),
        pltpu.VMEM((1, DV), F32),
        pltpu.VMEM(conv_q.shape, BF16),
        pltpu.VMEM(conv_k.shape, BF16),
        pltpu.VMEM(conv_v.shape, BF16),
        pltpu.VMEM((TAIL, half), BF16),
        pltpu.VMEM((TAIL, half), BF16),
        pltpu.VMEM((TAIL, half_v), BF16),
        pltpu.VMEM((rows + 8, half_v), F32),
        pltpu.VMEM((2, rows, half), BF16),
        pltpu.VMEM((2, rows, half), BF16),
        pltpu.VMEM((2, rows, half_v), BF16),
        pltpu.VMEM((nz // 2,) + message, BF16),
        pltpu.VMEM((nz,) + message, BF16),
        pltpu.VMEM((ny,) + message, BF16),
        pltpu.VMEM((nz, DK, DV), F32),
        pltpu.VMEM((nz, DK, DK), BF16),
        pltpu.VMEM((nz, 8, 128), F32),
        pltpu.VMEM((DK, DV), F32),
        pltpu.VMEM((nz, DK, DV), BF16),
        pltpu.VMEM((nz // 2, DK, DV), BF16),
        pltpu.VMEM((nz // 2, 2 * rows, 2 * DK), BF16),
        pltpu.VMEM((nz // 2, 2 * rows, DV), F32),
        pltpu.VMEM((2, rows, half_v), BF16),
        pltpu.VMEM((2, rows, half_v), BF16),
        pltpu.VMEM((nx - 1, rows, width), BF16),
        pltpu.VMEM((nx - 1, rows, width), BF16),
        dma((13,)),
        dma((6,)),
        dma((6,)),
        dma((6,)),
        dma((3,)),
        dma((nz // 2,)),
        dma((nz,)),
        dma((ny,)),
        dma((ny,)),
        dma((nz,)),
        dma((nz // 2,)),
        dma((2,)),
        dma((nx - 1,)),
        dma((nx - 1,)),
    ]
    call = pl.pallas_call(
        functools.partial(kernel, nx, ny, nz),
        out_shape=jax.ShapeDtypeStruct((rows, width), F32),
        in_specs=[hbm] * 13,
        out_specs=vmem,
        scratch_shapes=scratch,
        compiler_params=pltpu.CompilerParams(
            collective_id=0, has_side_effects=True, vmem_limit_bytes=40 * 1024 * 1024
        ),
        cost_estimate=pl.CostEstimate(
            flops=2_000_000_000, bytes_accessed=6_000_000, transcendentals=1_000_000
        ),
    )
    operands = (
        q_in,
        k_in,
        v_in,
        z_in,
        out_weight,
        a_in.T,
        b_in.T,
        a_log.reshape(1, nz),
        dt_bias.reshape(1, nz),
        norm_weight.reshape(1, DV),
        conv_q,
        conv_k,
        conv_v,
    )
    return call(*(pltpu.with_memory_space_constraint(value, pltpu.HBM) for value in operands))


def solution(mesh):
    in_specs = (
        P("ctx", "heads"),
        P("ctx", "heads"),
        P("ctx", "heads"),
        P(None, "heads"),
        P(None, "heads"),
        P(None, "heads"),
        P("ctx", "heads"),
        P("ctx", "heads"),
        P("heads"),
        P("heads"),
        P(),
        P("ctx", "heads"),
        P("heads", None),
    )
    out_specs = P("ctx", "heads")
    return jax.shard_map(shards, mesh=mesh, in_specs=in_specs, out_specs=out_specs, check_vma=False)
```

```python
import functools

import jax
import jax.numpy as jnp
from jax import lax
from jax.experimental import pallas as pl
from jax.experimental.pallas import tpu as pltpu
from jax.sharding import PartitionSpec as P

DK = 128
DV = 128
TAIL = 16
MESH = pl.DeviceIdType.MESH
F32 = jnp.float32
BF16 = jnp.bfloat16
HIGHEST = lax.Precision.HIGHEST


def split(value):
    high = value.astype(BF16)
    return high, (value - high.astype(F32)).astype(BF16)


def mm(left, right):
    return jnp.dot(left, right, preferred_element_type=F32)


def one_pass(left, right):
    return mm(left.astype(BF16), right.astype(BF16))


def split_left(left, right):
    high, low = split(left)
    return mm(jnp.concatenate([high, low], axis=1), jnp.concatenate([right, right], axis=0))


def split_right(left, right):
    high, low = split(right)
    return mm(jnp.concatenate([left, left], axis=1), jnp.concatenate([high, low], axis=0))


def split_both(left, right):
    left_high, left_low = split(left)
    right_high, right_low = split(right)
    return mm(
        jnp.concatenate([left_high, left_low], axis=1),
        jnp.concatenate([right_high, right_high], axis=0),
    ) + mm(left_high, right_low)


def silu(value):
    return value * (1.0 / (1.0 + jnp.exp(-value)))


def three_parts(value):
    first = value.astype(BF16).astype(F32)
    second = (value - first).astype(BF16).astype(F32)
    return first, second, value - first - second


def pack_decay(decay, width):
    row = lax.broadcasted_iota(jnp.int32, (TAIL, width), 0)
    first, second, third = three_parts(decay)
    zero = jnp.zeros((TAIL, width), F32)
    block = jnp.where(row == 0, first, jnp.where(row == 1, second, jnp.where(row == 2, third, zero)))
    return block.astype(BF16)


def kernel(
    nx,
    ny,
    nz,
    q_hbm,
    k_hbm,
    v_hbm,
    z_hbm,
    w_hbm,
    a_hbm,
    b_hbm,
    alog_hbm,
    bias_hbm,
    gain_hbm,
    cq_hbm,
    ck_hbm,
    cv_hbm,
    out_ref,
    q_in,
    k_in,
    v_in,
    z_in,
    w_in,
    a_in,
    b_in,
    alog_ref,
    bias_ref,
    gain_ref,
    cq_ref,
    ck_ref,
    cv_ref,
    halo_q,
    halo_k,
    halo_v,
    ext,
    qc_all,
    kc_all,
    vc_all,
    decay_out,
    decay_in,
    up_out,
    up_in,
    carry,
    pre_state,
    pre_map,
    pre_decay,
    sigma,
    down_out,
    down_in,
    reads,
    local,
    normed,
    pass_out,
    gates,
    rs_out,
    rs_in,
    load_sem,
    swap_send,
    swap_recv,
    halo_send,
    halo_recv,
    decay_send,
    decay_recv,
    up_send,
    up_recv,
    y_send,
    y_recv,
    down_send,
    down_recv,
    pass_sem,
    rs_send,
    rs_recv,
):
    rows = out_ref.shape[0]
    width = out_ref.shape[1]
    set_heads = nz // 2
    set_keys = nz // 4
    ring = 2 * nz
    count = ny * ring
    me = lax.axis_index("ctx")
    x = lax.axis_index("heads")
    y = me // ring
    place = lax.rem(me, ring)
    z = place // 2
    core = lax.rem(place, 2)
    chip = me // 2
    chips = count // 2
    partner = me + 1 - 2 * core
    heads = range(set_heads)
    keys = range(set_keys)
    both_shards = range(2)
    units = [(u, h) for u in both_shards for h in heads]
    key_units = [(u, s) for u in both_shards for s in keys]

    sender_core = z // set_heads
    owns = core != sender_core

    def owner_of(h):
        return y * ring + 2 * (set_heads * core + h) + 1 - core

    def cols_of(which, size):
        return pl.ds(pl.multiple_of(which * size, 128), size)

    streams = (
        (k_hbm, k_in, halo_k, ck_ref, kc_all, set_keys * DK),
        (v_hbm, v_in, halo_v, cv_ref, vc_all, set_heads * DV),
        (q_hbm, q_in, halo_q, cq_ref, qc_all, set_keys * DK),
    )
    wide = [(source, target, size) for source, target, _, _, _, size in streams]
    wide.append((z_hbm, z_in, set_heads * DV))
    pairs = [(source.at[:, cols_of(core, size)], target.at[core]) for source, target, size in wide]
    pairs += [
        (a_hbm, a_in.at[core]),
        (b_hbm, b_in.at[core]),
        (alog_hbm, alog_ref),
        (bias_hbm, bias_ref),
        (ck_hbm, ck_ref),
        (cv_hbm, cv_ref),
        (cq_hbm, cq_ref),
        (gain_hbm, gain_ref),
        (w_hbm, w_in),
    ]
    loads = [
        pltpu.make_async_copy(source, target, load_sem.at[i])
        for i, (source, target) in enumerate(pairs)
    ]
    first = [0, 1, 2, 8, 9, 10, 4, 5, 6, 7]
    rest = [3, 11, 12]
    for i in first + rest:
        loads[i].start()

    barrier = pltpu.get_barrier_semaphore()

    def greet(ctx, heads):
        pl.semaphore_signal(barrier, inc=1, device_id=(ctx, heads), device_id_type=MESH)

    for step in range(1, ring):
        greet(y * ring + lax.rem(place + step, ring), x)
    for step in range(1, ny):
        greet(lax.rem(me + step * ring, count), x)
    for step in range(1, nx):
        greet(me, lax.rem(x + step, nx))
    over = jnp.logical_and(place == ring - 1, me < count - 1)
    under = jnp.logical_and(z == 0, y > 0)

    @pl.when(over)
    def _():
        greet(me + 1, x)
        greet(me + 2, x)

    @pl.when(under)
    def _():
        greet(y * ring - 1, x)

    pl.semaphore_wait(
        barrier,
        (ring - 1) + (ny - 1) + (nx - 1) + 2 * over.astype(jnp.int32) + under.astype(jnp.int32),
    )

    def halo_copies(side):
        return [
            pltpu.make_async_remote_copy(
                src_ref=source.at[pl.ds(rows - TAIL, TAIL), cols_of(side, size)],
                dst_ref=target,
                send_sem=halo_send.at[3 * side + i],
                recv_sem=halo_recv.at[i],
                device_id=(2 * lax.rem(chip + 1, chips) + side, x),
                device_id_type=MESH,
            )
            for i, (source, _, target, _, _, size) in enumerate(streams)
        ]

    sends_halo = jnp.logical_and(core == 1, chip < chips - 1)

    @pl.when(sends_halo)
    def _():
        for side in range(2):
            for copy in halo_copies(side):
                copy.start()

    def swap_copies(shard):
        return [
            pltpu.make_async_remote_copy(
                src_ref=source,
                dst_ref=target.at[shard],
                send_sem=swap_send.at[i],
                recv_sem=swap_recv.at[i],
                device_id=(partner, x),
                device_id_type=MESH,
            )
            for i, (source, target) in enumerate(
                [
                    (source.at[:, cols_of(1 - core, size)], target)
                    for source, target, size in wide[:3]
                ]
                + [(a_hbm, a_in), (b_hbm, b_in)]
                + [
                    (source.at[:, cols_of(1 - core, size)], target)
                    for source, target, size in wide[3:]
                ]
            )
        ]

    swap = swap_copies(core)
    swapped = swap_copies(1 - core)
    for copy in swap:
        copy.start()

    @pl.when(chip == 0)
    def _():
        halo_k[...] = jnp.zeros_like(halo_k)
        halo_v[...] = jnp.zeros_like(halo_v)
        halo_q[...] = jnp.zeros_like(halo_q)

    def conv(before, data, taps_ref, size):
        height = data.shape[0]
        ext[0:8, 0:size] = before
        ext[8 : 8 + height, 0:size] = data.astype(F32)
        taps = taps_ref[:, cols_of(core, size)].astype(F32)
        total = jnp.zeros((height, size), F32)
        for j in range(4):
            total = total + taps[j : j + 1] * ext[5 + j : 5 + j + height, 0:size]
        return silu(total).astype(BF16)

    for i in first:
        loads[i].wait()
    for _, data, _, taps_ref, result, size in streams:
        result[core] = conv(jnp.zeros((8, size), F32), data[core], taps_ref, size)

    row = lax.broadcasted_iota(jnp.int32, (rows, rows), 0)
    col = lax.broadcasted_iota(jnp.int32, (rows, rows), 1)
    upto = row >= col
    strict = row > col
    apart = jnp.bitwise_xor(row, col)

    for i in range(3):
        swapped[i].wait_recv()
    for _, data, _, taps_ref, result, size in streams:
        result[1 - core] = conv(jnp.zeros((8, size), F32), data[1 - core], taps_ref, size)

    for i in range(3, 5):
        swapped[i].wait_recv()
    head_row = lax.broadcasted_iota(jnp.int32, (nz, nz), 0)
    head_lane = lax.broadcasted_iota(jnp.int32, (nz, nz), 1)

    def per_head(values):
        return jnp.sum(jnp.where(head_row == head_lane, values, 0.0), axis=1, keepdims=True)

    slot = lax.broadcasted_iota(jnp.int32, (128, nz), 0)
    from_head = lax.broadcasted_iota(jnp.int32, (128, nz), 1)

    def placing(start):
        wanted = set_heads * core + slot - start
        inside = jnp.logical_and(slot >= start, slot < start + set_heads)
        return jnp.where(jnp.logical_and(inside, wanted == from_head), 1.0, 0.0)

    def exact(left, right):
        return jnp.dot(left, right, preferred_element_type=F32, precision=HIGHEST)

    bias, rate = per_head(bias_ref[...]), jnp.exp(per_head(alog_ref[...]))
    before_or_at = jnp.where(row <= col, 1.0, 0.0)
    by_row = jnp.zeros((128, rows), F32)
    for u in both_shards:
        gate_in = a_in[u] + bias
        softplus = jnp.maximum(gate_in, 0.0) + jnp.log1p(jnp.exp(-jnp.abs(gate_in)))
        cumulative = exact(-rate * softplus, before_or_at)
        beta = 1.0 / (1.0 + jnp.exp(-b_in[u]))
        by_row = by_row + exact(placing(16 * u), cumulative)
        by_row = by_row + exact(placing(16 * u + set_heads), beta)
    columns = jnp.transpose(by_row)

    def decay_copy(h):
        return pltpu.make_async_remote_copy(
            src_ref=decay_out.at[h],
            dst_ref=decay_in.at[z],
            send_sem=decay_send.at[h],
            recv_sem=decay_recv.at[z],
            device_id=(owner_of(h), x),
            device_id_type=MESH,
        )

    for h in heads:
        chip_decay = [
            jnp.exp(columns[rows - 1 : rows, 16 * u + h : 16 * u + h + 1]) for u in both_shards
        ]
        decay_out[h] = jnp.broadcast_to(chip_decay[0] * chip_decay[1], (8, 128))
        decay_copy(h).start()

    @pl.when(chip > 0)
    def _():
        for copy in halo_copies(0):
            copy.wait_recv()

    def inverse_norm(block):
        entries = block.astype(F32)
        return lax.rsqrt(jnp.sum(entries * entries, axis=1, keepdims=True) + 1e-6)

    for _, data, halo, taps_ref, result, size in streams:
        for u in both_shards:
            before = halo[...] if u == 0 else data[0, rows - TAIL : rows, :]
            result[u, 0:TAIL, :] = conv(
                before.astype(F32)[8:16], data[u, 0:TAIL, :], taps_ref, size
            )

    def key_of(u, s):
        return kc_all[u, :, s * DK : (s + 1) * DK]

    def query_of(u, s):
        return qc_all[u, :, s * DK : (s + 1) * DK]

    wide_lane = lax.broadcasted_iota(jnp.int32, (rows, 128), 1)
    for u, s in key_units:
        place_of = 16 * u + 2 * set_heads + s
        columns = jnp.where(wide_lane == place_of, inverse_norm(key_of(u, s)), columns)
        columns = jnp.where(
            wide_lane == place_of + set_keys, inverse_norm(query_of(u, s)) * DK**-0.5, columns
        )
    by_row = jnp.transpose(columns)

    def column(u, index):
        return columns[:, 16 * u + index : 16 * u + index + 1]

    def lane_row(u, index):
        return by_row[16 * u + index : 16 * u + index + 1, :]

    gram, query_gram, key_t = {}, {}, {}
    for u, s in key_units:
        contract = (((1,), (1,)), ((), ()))
        gram[u, s] = lax.dot_general(
            key_of(u, s), key_of(u, s), contract, preferred_element_type=F32
        )
        query_gram[u, s] = lax.dot_general(
            query_of(u, s), key_of(u, s), contract, preferred_element_type=F32
        )
        key_t[u, s] = jnp.transpose(key_of(u, s).astype(F32)).astype(BF16)
    within, lower, inverse = {}, {}, {}
    for u, h in units:
        s = h // 2
        gaps = column(u, h) - lane_row(u, h)
        within[u, h] = jnp.exp(jnp.where(upto, gaps, -1e30)) * lane_row(u, 2 * set_heads + s)
        scale = column(u, set_heads + h) * column(u, 2 * set_heads + s)
        lower[u, h] = jnp.where(strict, scale * gram[u, s] * within[u, h], 0.0)
        inverse[u, h] = jnp.where(apart == 1, -lower[u, h], 0.0)
    level = 1
    while (1 << level) < rows:
        inner = {}
        for i in units:
            block = jnp.where((apart >> level) == 1, lower[i], 0.0)
            inner[i] = block + one_pass(block, inverse[i])
        for i in units:
            inverse[i] = inverse[i] - inner[i] - one_pass(inverse[i], inner[i])
        level += 1
    values, maps, shard_maps, decays = {}, {}, {}, {}
    for u, h in units:
        s = h // 2
        solve = jnp.where(row == col, 1.0, inverse[u, h]) * lane_row(u, set_heads + h)
        values[u, h] = split_left(solve, vc_all[u, :, h * DV : (h + 1) * DV])
        key_solve = solve * (jnp.exp(lane_row(u, h)) * lane_row(u, 2 * set_heads + s))
        maps[u, h] = split_left(key_solve, key_of(u, s))
    for u, h in units:
        s = h // 2
        last = column(u, h)[rows - 1 : rows, :]
        tail = jnp.exp(last - column(u, h)) * column(u, 2 * set_heads + s)
        both = jnp.concatenate([values[u, h] * tail, maps[u, h] * tail], axis=1)
        shard_maps[u, h] = split_right(key_t[u, s], both)
        decays[u, h] = jnp.exp(last)

    eye = row[0:DK, 0:DK] == col[0:DK, 0:DK]

    def decay_of(block):
        return jnp.sum(block.astype(F32), axis=0, keepdims=True)

    def map_of(message, decay):
        return jnp.where(eye, decay[:, 0:1], 0.0) - message[:, DV:].astype(F32)

    def compose(message, decay, carried):
        state = decay * carried[:, 0:DV] + message[:, 0:DV].astype(F32)
        fresh = jnp.concatenate([state, decay * carried[:, DV:]], axis=1)
        return fresh - mm(message[:, DV:].astype(BF16), carried.astype(BF16))

    def put_maps(target, carried, decay):
        target[0:DK, 0:DV] = carried[:, 0:DV].astype(BF16)
        target[0:DK, DV:] = map_of(carried, decay).astype(BF16)

    def up_copy(h):
        return pltpu.make_async_remote_copy(
            src_ref=up_out.at[h],
            dst_ref=up_in.at[z],
            send_sem=up_send.at[h],
            recv_sem=up_recv.at[z],
            device_id=(owner_of(h), x),
            device_id_type=MESH,
        )

    joined = {}
    for h in heads:
        early = shard_maps[0, h]
        carried = jnp.concatenate([early[:, 0:DV], map_of(early, decays[0, h])], axis=1)
        joined[h] = compose(shard_maps[1, h], decays[1, h], carried)
    for h in heads:
        put_maps(up_out.at[h], joined[h], decays[0, h] * decays[1, h])
    far_first = sorted(range(nz), key=lambda offset: -min(offset, nz - offset))
    for offset in far_first:
        target_chip = lax.rem(z + offset, nz)

        @pl.when(target_chip // set_heads == core)
        def _(h=lax.rem(target_chip, set_heads)):
            up_copy(h).start()

    for u, h in units:
        s = h // 2
        scale = column(u, 2 * set_heads + set_keys + s)
        attend = jnp.where(upto, query_gram[u, s] * within[u, h] * scale, 0.0)
        both = split_both(attend, jnp.concatenate([values[u, h], maps[u, h]], axis=1))
        fixed = both[:, 0:DV]
        read = jnp.exp(column(u, h)) * scale * query_of(u, s).astype(F32) - both[:, DV:]
        if u == 1:
            moved = split_both(read, shard_maps[0, h])
            fixed = fixed + moved[:, 0:DV]
            read = decays[0, h] * read - moved[:, DV:]
        high, low = split(read)
        local[h, u * rows : (u + 1) * rows, :] = fixed
        reads[h, u * rows : (u + 1) * rows, 0:DK] = high
        reads[h, u * rows : (u + 1) * rows, DK:] = low

    def carry_copy(source, target_y):
        return pltpu.make_async_remote_copy(
            src_ref=carry.at[source],
            dst_ref=carry.at[source],
            send_sem=y_send.at[target_y],
            recv_sem=y_recv.at[source],
            device_id=(target_y * ring + place, x),
            device_id_type=MESH,
        )

    def down_copy(target):
        slot = lax.rem(z, set_heads)
        return pltpu.make_async_remote_copy(
            src_ref=down_out.at[target],
            dst_ref=down_in.at[slot],
            send_sem=down_send.at[target],
            recv_sem=down_recv.at[slot],
            device_id=(y * ring + 2 * target + sender_core, x),
            device_id_type=MESH,
        )

    for i in rest:
        loads[i].wait()
    swapped[5].wait_recv()
    for h in heads:
        cols = slice(h * DV, (h + 1) * DV)
        for u in both_shards:
            gates[u, :, cols] = silu(z_in[u, :, cols].astype(F32)) * gain_ref[...]

    @pl.when(owns)
    def _():
        pre_state[0] = jnp.zeros((DK, DV), F32)
        pre_map[0] = jnp.zeros((DK, DK), BF16)
        pre_decay[0] = jnp.ones((8, 128), F32)
        spans = {}
        for j in range(nz):
            for source, target, sent, received in (
                (decay_out, decay_in, decay_send, decay_recv),
                (up_out, up_in, up_send, up_recv),
            ):
                pltpu.make_async_remote_copy(
                    src_ref=source.at[0],
                    dst_ref=target.at[j],
                    send_sem=sent.at[0],
                    recv_sem=received.at[j],
                    device_id=(partner, x),
                    device_id_type=MESH,
                ).wait_recv()
            decay = decay_in[j, 0:1, :]
            state, taken = up_in[j, :, 0:DV].astype(F32), up_in[j, :, DV:].astype(F32)
            carried = jnp.concatenate([state, jnp.where(eye, decay, 0.0) - taken], axis=1)
            spans[j, j + 1] = (carried, decay)

        def after(early, late):
            (carried, decay), (later_maps, later_decay) = spans[early], spans[late]
            message = jnp.concatenate(
                [later_maps[:, 0:DV], map_of(later_maps, later_decay)], axis=1
            )
            spans[early[0], late[1]] = (compose(message, later_decay, carried), decay * later_decay)

        size = 1
        while size < nz:
            for start in range(0, nz, 2 * size):
                after((start, start + size), (start + size, start + 2 * size))
            size *= 2
        carried, total_decay = spans[0, nz]
        put_maps(carry.at[y], carried, total_decay)
        carry[y, DK:, :] = pack_decay(total_decay[:, 0:1], DK + DV)

        for later in range(1, ny):

            @pl.when(y < later)
            def _(later=later):
                carry_copy(y, later).start()

        for j in range(1, nz):
            if (0, j) not in spans:
                size = j & -j
                after((0, j - size), (j - size, j))
            carried, total_decay = spans[0, j]
            pre_state[j] = carried[:, 0:DV]
            pre_map[j] = map_of(carried, total_decay).astype(BF16)
            pre_decay[j] = jnp.broadcast_to(total_decay, (8, 128))

        sigma[...] = jnp.zeros((DK, DV), F32)
        for earlier in range(ny - 1):

            @pl.when(y > earlier)
            def _(earlier=earlier):
                carry_copy(earlier, y).wait_recv()
                message = carry[earlier]
                state = sigma[...]
                sigma[...] = (
                    decay_of(message[DK:, 0:DV]) * state
                    - mm(message[0:DK, DV:], state.astype(BF16))
                    + message[0:DK, 0:DV].astype(F32)
                )

        start_state = sigma[...]
        rounded = start_state.astype(BF16)
        for offset in far_first:
            target = lax.rem(z + offset, nz)
            down_out[target] = (
                pre_decay[target, 0:1, :] * start_state
                - mm(pre_map[target], rounded)
                + pre_state[target]
            ).astype(BF16)
            down_copy(target).start()

    cores = {}
    for h in heads:
        pltpu.make_async_remote_copy(
            src_ref=down_out.at[0],
            dst_ref=down_in.at[h],
            send_sem=down_send.at[0],
            recv_sem=down_recv.at[h],
            device_id=(owner_of(h), x),
            device_id_type=MESH,
        ).wait_recv()
    for h in heads:
        state = down_in[h]
        cores[h] = mm(reads[h], jnp.concatenate([state, state], axis=0)) + local[h]
    hand_over = pltpu.make_async_remote_copy(
        src_ref=pass_out.at[1 - core],
        dst_ref=normed,
        send_sem=pass_sem.at[0],
        recv_sem=pass_sem.at[1],
        device_id=(partner, x),
        device_id_type=MESH,
    )
    for h in heads:
        power = jnp.mean(cores[h] * cores[h], axis=1, keepdims=True)
        scaled = cores[h] * lax.rsqrt(power + 1e-6)
        cols = slice(h * DV, (h + 1) * DV)
        for u in both_shards:
            part_rows = scaled[u * rows : (u + 1) * rows]
            pass_out[u, :, cols] = (part_rows * gates[u, :, cols]).astype(BF16)
    hand_over.start()

    depth = set_heads * DV

    def part(step, which, operand):
        depth_rows = pl.ds(pl.multiple_of(which * depth, 128), depth)
        return mm(operand, w_in[depth_rows, cols_of(lax.rem(x + step, nx), width)])

    order = sorted(range(1, nx), key=lambda step: -min(step, nx - step))
    parts = {step: part(step, core, pass_out[core]) for step in order}
    pltpu.make_async_remote_copy(
        src_ref=pass_out.at[core],
        dst_ref=normed,
        send_sem=pass_sem.at[0],
        recv_sem=pass_sem.at[1],
        device_id=(partner, x),
        device_id_type=MESH,
    ).wait_recv()

    def rs_copy(step):
        return pltpu.make_async_remote_copy(
            src_ref=rs_out.at[step - 1],
            dst_ref=rs_in.at[step - 1],
            send_sem=rs_send.at[step - 1],
            recv_sem=rs_recv.at[step - 1],
            device_id=(me, lax.rem(x + step, nx)),
            device_id_type=MESH,
        )

    for step in order:
        rs_out[step - 1] = (parts[step] + part(step, 1 - core, normed[...])).astype(BF16)
        rs_copy(step).start()
    total = part(0, core, pass_out[core]) + part(0, 1 - core, normed[...])
    for step in reversed(order):
        rs_copy(step).wait_recv()
        total = total + rs_in[step - 1].astype(F32)
    out_ref[...] = total

    @pl.when(sends_halo)
    def _():
        for side in range(2):
            for copy in halo_copies(side):
                copy.wait_send()

    for copy in swap:
        copy.wait_send()
    for h in heads:
        decay_copy(h).wait_send()
        up_copy(h).wait_send()

    @pl.when(owns)
    def _():
        for target in range(nz):
            down_copy(target).wait_send()
        for later in range(1, ny):

            @pl.when(y < later)
            def _(later=later):
                carry_copy(y, later).wait_send()

    hand_over.wait_send()
    for step in order:
        rs_copy(step).wait_send()


def shards(
    q_in, k_in, v_in, conv_q, conv_k, conv_v, a_in, b_in, a_log, dt_bias, norm_weight, z_in, out_weight
):
    rows = q_in.shape[0]
    nz = v_in.shape[1] // DV
    nx = lax.axis_size("heads")
    ny = lax.axis_size("ctx") // (2 * nz)
    width = out_weight.shape[1] // nx
    half = q_in.shape[1] // 2
    half_v = v_in.shape[1] // 2
    hbm = pl.BlockSpec(memory_space=pltpu.HBM)
    vmem = pl.BlockSpec(memory_space=pltpu.VMEM)
    dma = pltpu.SemaphoreType.DMA
    message = (DK + TAIL, DK + DV)
    scratch = [
        pltpu.VMEM((2, rows, half), BF16),
        pltpu.VMEM((2, rows, half), BF16),
        pltpu.VMEM((2, rows, half_v), BF16),
        pltpu.VMEM((2, rows, half_v), BF16),
        pltpu.VMEM(out_weight.shape, BF16),
        pltpu.VMEM((2, nz, rows), F32),
        pltpu.VMEM((2, nz, rows), F32),
        pltpu.VMEM((1, nz), F32),
        pltpu.VMEM((1, nz), F32),
        pltpu.VMEM((1, DV), F32),
        pltpu.VMEM(conv_q.shape, BF16),
        pltpu.VMEM(conv_k.shape, BF16),
        pltpu.VMEM(conv_v.shape, BF16),
        pltpu.VMEM((TAIL, half), BF16),
        pltpu.VMEM((TAIL, half), BF16),
        pltpu.VMEM((TAIL, half_v), BF16),
        pltpu.VMEM((rows + 8, half_v), F32),
        pltpu.VMEM((2, rows, half), BF16),
        pltpu.VMEM((2, rows, half), BF16),
        pltpu.VMEM((2, rows, half_v), BF16),
        pltpu.VMEM((nz // 2, 8, 128), F32),
        pltpu.VMEM((nz, 8, 128), F32),
        pltpu.VMEM((nz // 2, DK, DK + DV), BF16),
        pltpu.VMEM((nz, DK, DK + DV), BF16),
        pltpu.VMEM((ny,) + message, BF16),
        pltpu.VMEM((nz, DK, DV), F32),
        pltpu.VMEM((nz, DK, DK), BF16),
        pltpu.VMEM((nz, 8, 128), F32),
        pltpu.VMEM((DK, DV), F32),
        pltpu.VMEM((nz, DK, DV), BF16),
        pltpu.VMEM((nz // 2, DK, DV), BF16),
        pltpu.VMEM((nz // 2, 2 * rows, 2 * DK), BF16),
        pltpu.VMEM((nz // 2, 2 * rows, DV), F32),
        pltpu.VMEM((rows, half_v), BF16),
        pltpu.VMEM((2, rows, half_v), BF16),
        pltpu.VMEM((2, rows, half_v), F32),
        pltpu.VMEM((nx - 1, rows, width), BF16),
        pltpu.VMEM((nx - 1, rows, width), BF16),
        dma((13,)),
        dma((6,)),
        dma((6,)),
        dma((6,)),
        dma((3,)),
        dma((nz // 2,)),
        dma((nz,)),
        dma((nz // 2,)),
        dma((nz,)),
        dma((ny,)),
        dma((ny,)),
        dma((nz,)),
        dma((nz // 2,)),
        dma((2,)),
        dma((nx - 1,)),
        dma((nx - 1,)),
    ]
    call = pl.pallas_call(
        functools.partial(kernel, nx, ny, nz),
        out_shape=jax.ShapeDtypeStruct((rows, width), F32),
        in_specs=[hbm] * 13,
        out_specs=vmem,
        scratch_shapes=scratch,
        compiler_params=pltpu.CompilerParams(
            collective_id=0, has_side_effects=True, vmem_limit_bytes=40 * 1024 * 1024
        ),
        cost_estimate=pl.CostEstimate(
            flops=2_000_000_000, bytes_accessed=6_000_000, transcendentals=1_000_000
        ),
    )
    operands = (
        q_in,
        k_in,
        v_in,
        z_in,
        out_weight,
        a_in.T,
        b_in.T,
        a_log.reshape(1, nz),
        dt_bias.reshape(1, nz),
        norm_weight.reshape(1, DV),
        conv_q,
        conv_k,
        conv_v,
    )
    return call(*(pltpu.with_memory_space_constraint(value, pltpu.HBM) for value in operands))


def solution(mesh):
    in_specs = (
        P("ctx", "heads"),
        P("ctx", "heads"),
        P("ctx", "heads"),
        P(None, "heads"),
        P(None, "heads"),
        P(None, "heads"),
        P("ctx", "heads"),
        P("ctx", "heads"),
        P("heads"),
        P("heads"),
        P(),
        P("ctx", "heads"),
        P("heads", None),
    )
    out_specs = P("ctx", "heads")
    return jax.shard_map(shards, mesh=mesh, in_specs=in_specs, out_specs=out_specs, check_vma=False)
```

```python
import functools

import jax
import jax.numpy as jnp
from jax import lax
from jax.experimental import pallas as pl
from jax.experimental.pallas import tpu as pltpu
from jax.sharding import PartitionSpec as P

DK = 128
DV = 128
TAIL = 16
MESH = pl.DeviceIdType.MESH
F32 = jnp.float32
BF16 = jnp.bfloat16
HIGHEST = lax.Precision.HIGHEST


def split(value):
    high = value.astype(BF16)
    return high, (value - high.astype(F32)).astype(BF16)


def mm(left, right):
    return jnp.dot(left, right, preferred_element_type=F32)


def one_pass(left, right):
    return mm(left.astype(BF16), right.astype(BF16))


def split_left(left, right):
    high, low = split(left)
    return mm(jnp.concatenate([high, low], axis=1), jnp.concatenate([right, right], axis=0))


def split_right(left, right):
    high, low = split(right)
    return mm(jnp.concatenate([left, left], axis=1), jnp.concatenate([high, low], axis=0))


def split_both(left, right):
    left_high, left_low = split(left)
    right_high, right_low = split(right)
    return mm(
        jnp.concatenate([left_high, left_low], axis=1),
        jnp.concatenate([right_high, right_high], axis=0),
    ) + mm(left_high, right_low)


def silu(value):
    return value * (1.0 / (1.0 + jnp.exp(-value)))


def three_parts(value):
    first = value.astype(BF16).astype(F32)
    second = (value - first).astype(BF16).astype(F32)
    return first, second, value - first - second


def pack_decay(decay, width):
    row = lax.broadcasted_iota(jnp.int32, (TAIL, width), 0)
    first, second, third = three_parts(decay)
    zero = jnp.zeros((TAIL, width), F32)
    block = jnp.where(row == 0, first, jnp.where(row == 1, second, jnp.where(row == 2, third, zero)))
    return block.astype(BF16)


def kernel(
    nx,
    ny,
    nz,
    q_hbm,
    k_hbm,
    v_hbm,
    z_hbm,
    w_hbm,
    a_hbm,
    b_hbm,
    alog_hbm,
    bias_hbm,
    gain_hbm,
    cq_hbm,
    ck_hbm,
    cv_hbm,
    out_ref,
    q_in,
    k_in,
    v_in,
    z_in,
    w_in,
    a_in,
    b_in,
    alog_ref,
    bias_ref,
    gain_ref,
    cq_ref,
    ck_ref,
    cv_ref,
    halo_q,
    halo_k,
    halo_v,
    ext,
    qc_all,
    kc_all,
    vc_all,
    decay_out,
    decay_in,
    up_out,
    up_in,
    carry,
    pre_state,
    pre_map,
    pre_decay,
    sigma,
    down_out,
    down_in,
    reads,
    local,
    normed,
    pass_out,
    gates,
    relay_out,
    relay_in,
    rs_out,
    rs_in,
    load_sem,
    swap_send,
    swap_recv,
    halo_send,
    halo_recv,
    decay_send,
    decay_recv,
    up_send,
    up_recv,
    y_send,
    y_recv,
    down_send,
    down_recv,
    pass_sem,
    rs_send,
    rs_recv,
):
    rows = out_ref.shape[0]
    width = out_ref.shape[1]
    set_heads = nz // 2
    set_keys = nz // 4
    ring = 2 * nz
    count = ny * ring
    me = lax.axis_index("ctx")
    x = lax.axis_index("heads")
    y = me // ring
    place = lax.rem(me, ring)
    z = place // 2
    core = lax.rem(place, 2)
    chip = me // 2
    chips = count // 2
    partner = me + 1 - 2 * core
    heads = range(set_heads)
    keys = range(set_keys)
    both_shards = range(2)
    units = [(u, h) for u in both_shards for h in heads]
    key_units = [(u, s) for u in both_shards for s in keys]

    sender_core = z // set_heads
    owns = core != sender_core

    def owner_of(h):
        return y * ring + 2 * (set_heads * core + h) + 1 - core

    def cols_of(which, size):
        return pl.ds(pl.multiple_of(which * size, 128), size)

    streams = (
        (k_hbm, k_in, halo_k, ck_ref, kc_all, set_keys * DK),
        (v_hbm, v_in, halo_v, cv_ref, vc_all, set_heads * DV),
        (q_hbm, q_in, halo_q, cq_ref, qc_all, set_keys * DK),
    )
    wide = [(source, target, size) for source, target, _, _, _, size in streams]
    wide.append((z_hbm, z_in, set_heads * DV))
    pairs = [(source.at[:, cols_of(core, size)], target.at[core]) for source, target, size in wide]
    pairs += [
        (a_hbm, a_in.at[core]),
        (b_hbm, b_in.at[core]),
        (alog_hbm, alog_ref),
        (bias_hbm, bias_ref),
        (ck_hbm, ck_ref),
        (cv_hbm, cv_ref),
        (cq_hbm, cq_ref),
        (gain_hbm, gain_ref),
        (w_hbm, w_in),
    ]
    loads = [
        pltpu.make_async_copy(source, target, load_sem.at[i])
        for i, (source, target) in enumerate(pairs)
    ]
    first = [0, 1, 2, 8, 9, 10, 4, 5, 6, 7]
    rest = [3, 11, 12]
    for i in first + rest:
        loads[i].start()

    barrier = pltpu.get_barrier_semaphore()

    def greet(ctx, heads):
        pl.semaphore_signal(barrier, inc=1, device_id=(ctx, heads), device_id_type=MESH)

    over = jnp.logical_and(place == ring - 1, me < count - 1)
    under = jnp.logical_and(z == 0, y > 0)

    @pl.when(over)
    def _():
        greet(me + 1, x)
        greet(me + 2, x)

    @pl.when(under)
    def _():
        greet(y * ring - 1, x)

    for step in sorted(range(1, ring), key=lambda step: (min(step, ring - step), -step)):
        greet(y * ring + lax.rem(place + step, ring), x)
    for step in range(1, ny):
        greet(lax.rem(me + step * ring, count), x)
    for step in range(1, nx):
        greet(me, lax.rem(x + step, nx))
    pl.semaphore_wait(
        barrier,
        (ring - 1) + (ny - 1) + (nx - 1) + 2 * over.astype(jnp.int32) + under.astype(jnp.int32),
    )

    def halo_copies(side):
        return [
            pltpu.make_async_remote_copy(
                src_ref=source.at[pl.ds(rows - TAIL, TAIL), cols_of(side, size)],
                dst_ref=target,
                send_sem=halo_send.at[3 * side + i],
                recv_sem=halo_recv.at[i],
                device_id=(2 * lax.rem(chip + 1, chips) + side, x),
                device_id_type=MESH,
            )
            for i, (source, _, target, _, _, size) in enumerate(streams)
        ]

    sends_halo = jnp.logical_and(core == 1, chip < chips - 1)

    @pl.when(sends_halo)
    def _():
        for side in range(2):
            for copy in halo_copies(side):
                copy.start()

    def swap_copies(shard):
        return [
            pltpu.make_async_remote_copy(
                src_ref=source,
                dst_ref=target.at[shard],
                send_sem=swap_send.at[i],
                recv_sem=swap_recv.at[i],
                device_id=(partner, x),
                device_id_type=MESH,
            )
            for i, (source, target) in enumerate(
                [
                    (source.at[:, cols_of(1 - core, size)], target)
                    for source, target, size in wide[:3]
                ]
                + [(a_hbm, a_in), (b_hbm, b_in)]
                + [
                    (source.at[:, cols_of(1 - core, size)], target)
                    for source, target, size in wide[3:]
                ]
            )
        ]

    swap = swap_copies(core)
    swapped = swap_copies(1 - core)
    for copy in swap:
        copy.start()

    @pl.when(chip == 0)
    def _():
        halo_k[...] = jnp.zeros_like(halo_k)
        halo_v[...] = jnp.zeros_like(halo_v)
        halo_q[...] = jnp.zeros_like(halo_q)

    def conv(before, data, taps_ref, size):
        height = data.shape[0]
        ext[0:8, 0:size] = before
        ext[8 : 8 + height, 0:size] = data.astype(F32)
        taps = taps_ref[:, cols_of(core, size)].astype(F32)
        total = jnp.zeros((height, size), F32)
        for j in range(4):
            total = total + taps[j : j + 1] * ext[5 + j : 5 + j + height, 0:size]
        return silu(total).astype(BF16)

    for i in first:
        loads[i].wait()
    for _, data, _, taps_ref, result, size in streams:
        result[core] = conv(jnp.zeros((8, size), F32), data[core], taps_ref, size)

    row = lax.broadcasted_iota(jnp.int32, (rows, rows), 0)
    col = lax.broadcasted_iota(jnp.int32, (rows, rows), 1)
    upto = row >= col
    strict = row > col
    apart = jnp.bitwise_xor(row, col)

    for i in range(3):
        swapped[i].wait_recv()
    for _, data, _, taps_ref, result, size in streams:
        result[1 - core] = conv(jnp.zeros((8, size), F32), data[1 - core], taps_ref, size)

    for i in range(3, 5):
        swapped[i].wait_recv()
    head_row = lax.broadcasted_iota(jnp.int32, (nz, nz), 0)
    head_lane = lax.broadcasted_iota(jnp.int32, (nz, nz), 1)

    def per_head(values):
        return jnp.sum(jnp.where(head_row == head_lane, values, 0.0), axis=1, keepdims=True)

    slot = lax.broadcasted_iota(jnp.int32, (128, nz), 0)
    from_head = lax.broadcasted_iota(jnp.int32, (128, nz), 1)

    def placing(start):
        wanted = set_heads * core + slot - start
        inside = jnp.logical_and(slot >= start, slot < start + set_heads)
        return jnp.where(jnp.logical_and(inside, wanted == from_head), 1.0, 0.0)

    def exact(left, right):
        return jnp.dot(left, right, preferred_element_type=F32, precision=HIGHEST)

    bias, rate = per_head(bias_ref[...]), jnp.exp(per_head(alog_ref[...]))
    before_or_at = jnp.where(row <= col, 1.0, 0.0)
    by_row = jnp.zeros((128, rows), F32)
    for u in both_shards:
        gate_in = a_in[u] + bias
        softplus = jnp.maximum(gate_in, 0.0) + jnp.log1p(jnp.exp(-jnp.abs(gate_in)))
        cumulative = exact(-rate * softplus, before_or_at)
        beta = 1.0 / (1.0 + jnp.exp(-b_in[u]))
        by_row = by_row + exact(placing(16 * u), cumulative)
        by_row = by_row + exact(placing(16 * u + set_heads), beta)
    columns = jnp.transpose(by_row)

    def decay_copy(h):
        return pltpu.make_async_remote_copy(
            src_ref=decay_out.at[h],
            dst_ref=decay_in.at[z],
            send_sem=decay_send.at[h],
            recv_sem=decay_recv.at[z],
            device_id=(owner_of(h), x),
            device_id_type=MESH,
        )

    for h in heads:
        chip_decay = [
            jnp.exp(columns[rows - 1 : rows, 16 * u + h : 16 * u + h + 1]) for u in both_shards
        ]
        decay_out[h] = jnp.broadcast_to(chip_decay[0] * chip_decay[1], (8, 128))
        decay_copy(h).start()

    @pl.when(chip > 0)
    def _():
        for copy in halo_copies(0):
            copy.wait_recv()

    def inverse_norm(block):
        entries = block.astype(F32)
        return lax.rsqrt(jnp.sum(entries * entries, axis=1, keepdims=True) + 1e-6)

    for _, data, halo, taps_ref, result, size in streams:
        for u in both_shards:
            before = halo[...] if u == 0 else data[0, rows - TAIL : rows, :]
            result[u, 0:TAIL, :] = conv(
                before.astype(F32)[8:16], data[u, 0:TAIL, :], taps_ref, size
            )

    def key_of(u, s):
        return kc_all[u, :, s * DK : (s + 1) * DK]

    def query_of(u, s):
        return qc_all[u, :, s * DK : (s + 1) * DK]

    wide_lane = lax.broadcasted_iota(jnp.int32, (rows, 128), 1)
    for u, s in key_units:
        place_of = 16 * u + 2 * set_heads + s
        columns = jnp.where(wide_lane == place_of, inverse_norm(key_of(u, s)), columns)
        columns = jnp.where(
            wide_lane == place_of + set_keys, inverse_norm(query_of(u, s)) * DK**-0.5, columns
        )
    by_row = jnp.transpose(columns)

    def column(u, index):
        return columns[:, 16 * u + index : 16 * u + index + 1]

    def lane_row(u, index):
        return by_row[16 * u + index : 16 * u + index + 1, :]

    gram, query_gram, key_t = {}, {}, {}
    for u, s in key_units:
        contract = (((1,), (1,)), ((), ()))
        gram[u, s] = lax.dot_general(
            key_of(u, s), key_of(u, s), contract, preferred_element_type=F32
        )
        query_gram[u, s] = lax.dot_general(
            query_of(u, s), key_of(u, s), contract, preferred_element_type=F32
        )
        key_t[u, s] = jnp.transpose(key_of(u, s).astype(F32)).astype(BF16)
    within, lower, inverse = {}, {}, {}
    for u, h in units:
        s = h // 2
        gaps = column(u, h) - lane_row(u, h)
        within[u, h] = jnp.exp(jnp.where(upto, gaps, -1e30)) * lane_row(u, 2 * set_heads + s)
        scale = column(u, set_heads + h) * column(u, 2 * set_heads + s)
        lower[u, h] = jnp.where(strict, scale * gram[u, s] * within[u, h], 0.0)
        inverse[u, h] = jnp.where(apart == 1, -lower[u, h], 0.0)
    level = 1
    while (1 << level) < rows:
        inner = {}
        for i in units:
            block = jnp.where((apart >> level) == 1, lower[i], 0.0)
            inner[i] = block + one_pass(block, inverse[i])
        for i in units:
            inverse[i] = inverse[i] - inner[i] - one_pass(inverse[i], inner[i])
        level += 1
    values, maps, shard_maps, decays = {}, {}, {}, {}
    for u, h in units:
        s = h // 2
        solve = jnp.where(row == col, 1.0, inverse[u, h]) * lane_row(u, set_heads + h)
        values[u, h] = split_left(solve, vc_all[u, :, h * DV : (h + 1) * DV])
        key_solve = solve * (jnp.exp(lane_row(u, h)) * lane_row(u, 2 * set_heads + s))
        maps[u, h] = split_left(key_solve, key_of(u, s))
    for u, h in units:
        s = h // 2
        last = column(u, h)[rows - 1 : rows, :]
        tail = jnp.exp(last - column(u, h)) * column(u, 2 * set_heads + s)
        both = jnp.concatenate([values[u, h] * tail, maps[u, h] * tail], axis=1)
        shard_maps[u, h] = split_right(key_t[u, s], both)
        decays[u, h] = jnp.exp(last)

    eye = row[0:DK, 0:DK] == col[0:DK, 0:DK]

    def decay_of(block):
        return jnp.sum(block.astype(F32), axis=0, keepdims=True)

    def map_of(message, decay):
        return jnp.where(eye, decay[:, 0:1], 0.0) - message[:, DV:].astype(F32)

    def compose(message, decay, carried):
        state = decay * carried[:, 0:DV] + message[:, 0:DV].astype(F32)
        fresh = jnp.concatenate([state, decay * carried[:, DV:]], axis=1)
        return fresh - mm(message[:, DV:].astype(BF16), carried.astype(BF16))

    def put_maps(target, carried, decay):
        target[0:DK, 0:DV] = carried[:, 0:DV].astype(BF16)
        target[0:DK, DV:] = map_of(carried, decay).astype(BF16)

    def up_copy(h):
        return pltpu.make_async_remote_copy(
            src_ref=up_out.at[h],
            dst_ref=up_in.at[z],
            send_sem=up_send.at[h],
            recv_sem=up_recv.at[z],
            device_id=(owner_of(h), x),
            device_id_type=MESH,
        )

    joined = {}
    for h in heads:
        early = shard_maps[0, h]
        carried = jnp.concatenate([early[:, 0:DV], map_of(early, decays[0, h])], axis=1)
        joined[h] = compose(shard_maps[1, h], decays[1, h], carried)
    for h in heads:
        put_maps(up_out.at[h], joined[h], decays[0, h] * decays[1, h])
    far_first = sorted(range(nz), key=lambda offset: -min(offset, nz - offset))
    for offset in far_first:
        target_chip = lax.rem(z + offset, nz)

        @pl.when(target_chip // set_heads == core)
        def _(h=lax.rem(target_chip, set_heads)):
            up_copy(h).start()

    for u, h in units:
        s = h // 2
        scale = column(u, 2 * set_heads + set_keys + s)
        attend = jnp.where(upto, query_gram[u, s] * within[u, h] * scale, 0.0)
        both = split_both(attend, jnp.concatenate([values[u, h], maps[u, h]], axis=1))
        fixed = both[:, 0:DV]
        read = jnp.exp(column(u, h)) * scale * query_of(u, s).astype(F32) - both[:, DV:]
        if u == 1:
            moved = split_both(read, shard_maps[0, h])
            fixed = fixed + moved[:, 0:DV]
            read = decays[0, h] * read - moved[:, DV:]
        high, low = split(read)
        local[h, u * rows : (u + 1) * rows, :] = fixed
        reads[h, u * rows : (u + 1) * rows, 0:DK] = high
        reads[h, u * rows : (u + 1) * rows, DK:] = low

    def carry_copy(source, target_y):
        return pltpu.make_async_remote_copy(
            src_ref=carry.at[source],
            dst_ref=carry.at[source],
            send_sem=y_send.at[target_y],
            recv_sem=y_recv.at[source],
            device_id=(target_y * ring + place, x),
            device_id_type=MESH,
        )

    def down_copy(target):
        slot = lax.rem(z, set_heads)
        return pltpu.make_async_remote_copy(
            src_ref=down_out.at[target],
            dst_ref=down_in.at[slot],
            send_sem=down_send.at[target],
            recv_sem=down_recv.at[slot],
            device_id=(y * ring + 2 * target + sender_core, x),
            device_id_type=MESH,
        )

    for i in rest:
        loads[i].wait()
    swapped[5].wait_recv()
    for h in heads:
        cols = slice(h * DV, (h + 1) * DV)
        for u in both_shards:
            gates[u, :, cols] = silu(z_in[u, :, cols].astype(F32)) * gain_ref[...]

    @pl.when(owns)
    def _():
        pre_state[0] = jnp.zeros((DK, DV), F32)
        pre_map[0] = jnp.zeros((DK, DK), BF16)
        pre_decay[0] = jnp.ones((8, 128), F32)
        spans = {}
        for j in range(nz):
            for source, target, sent, received in (
                (decay_out, decay_in, decay_send, decay_recv),
                (up_out, up_in, up_send, up_recv),
            ):
                pltpu.make_async_remote_copy(
                    src_ref=source.at[0],
                    dst_ref=target.at[j],
                    send_sem=sent.at[0],
                    recv_sem=received.at[j],
                    device_id=(partner, x),
                    device_id_type=MESH,
                ).wait_recv()
            decay = decay_in[j, 0:1, :]
            state, taken = up_in[j, :, 0:DV].astype(F32), up_in[j, :, DV:].astype(F32)
            carried = jnp.concatenate([state, jnp.where(eye, decay, 0.0) - taken], axis=1)
            spans[j, j + 1] = (carried, decay)

        def after(early, late):
            (carried, decay), (later_maps, later_decay) = spans[early], spans[late]
            message = jnp.concatenate(
                [later_maps[:, 0:DV], map_of(later_maps, later_decay)], axis=1
            )
            spans[early[0], late[1]] = (compose(message, later_decay, carried), decay * later_decay)

        size = 1
        while size < nz:
            for start in range(0, nz, 2 * size):
                after((start, start + size), (start + size, start + 2 * size))
            size *= 2
        carried, total_decay = spans[0, nz]
        put_maps(carry.at[y], carried, total_decay)
        carry[y, DK:, :] = pack_decay(total_decay[:, 0:1], DK + DV)

        for later in range(1, ny):

            @pl.when(y < later)
            def _(later=later):
                carry_copy(y, later).start()

        for j in range(1, nz):
            if (0, j) not in spans:
                size = j & -j
                after((0, j - size), (j - size, j))
            carried, total_decay = spans[0, j]
            pre_state[j] = carried[:, 0:DV]
            pre_map[j] = map_of(carried, total_decay).astype(BF16)
            pre_decay[j] = jnp.broadcast_to(total_decay, (8, 128))

        sigma[...] = jnp.zeros((DK, DV), F32)
        for earlier in range(ny - 1):

            @pl.when(y > earlier)
            def _(earlier=earlier):
                carry_copy(earlier, y).wait_recv()
                message = carry[earlier]
                state = sigma[...]
                sigma[...] = (
                    decay_of(message[DK:, 0:DV]) * state
                    - mm(message[0:DK, DV:], state.astype(BF16))
                    + message[0:DK, 0:DV].astype(F32)
                )

        start_state = sigma[...]
        rounded = start_state.astype(BF16)
        for offset in far_first:
            target = lax.rem(z + offset, nz)
            down_out[target] = (
                pre_decay[target, 0:1, :] * start_state
                - mm(pre_map[target], rounded)
                + pre_state[target]
            ).astype(BF16)
            down_copy(target).start()

    cores = {}
    for h in heads:
        pltpu.make_async_remote_copy(
            src_ref=down_out.at[0],
            dst_ref=down_in.at[h],
            send_sem=down_send.at[0],
            recv_sem=down_recv.at[h],
            device_id=(owner_of(h), x),
            device_id_type=MESH,
        ).wait_recv()
    for h in heads:
        state = down_in[h]
        cores[h] = mm(reads[h], jnp.concatenate([state, state], axis=0)) + local[h]
    hand_over = pltpu.make_async_remote_copy(
        src_ref=pass_out.at[1 - core],
        dst_ref=normed,
        send_sem=pass_sem.at[0],
        recv_sem=pass_sem.at[1],
        device_id=(partner, x),
        device_id_type=MESH,
    )
    for h in heads:
        power = jnp.mean(cores[h] * cores[h], axis=1, keepdims=True)
        scaled = cores[h] * lax.rsqrt(power + 1e-6)
        cols = slice(h * DV, (h + 1) * DV)
        for u in both_shards:
            part_rows = scaled[u * rows : (u + 1) * rows]
            pass_out[u, :, cols] = (part_rows * gates[u, :, cols]).astype(BF16)
    hand_over.start()

    depth = set_heads * DV

    def part(step, which, operand):
        depth_rows = pl.ds(pl.multiple_of(which * depth, 128), depth)
        return mm(operand, w_in[depth_rows, cols_of(lax.rem(x + step, nx), width)])

    order = (2, 1, nx - 1)
    parts = {step: part(step, core, pass_out[core]) for step in order}
    pltpu.make_async_remote_copy(
        src_ref=pass_out.at[core],
        dst_ref=normed,
        send_sem=pass_sem.at[0],
        recv_sem=pass_sem.at[1],
        device_id=(partner, x),
        device_id_type=MESH,
    ).wait_recv()

    def rs_copy(i, source, target, step):
        return pltpu.make_async_remote_copy(
            src_ref=source,
            dst_ref=target,
            send_sem=rs_send.at[i],
            recv_sem=rs_recv.at[i],
            device_id=(me, lax.rem(x + step, nx)),
            device_id_type=MESH,
        )

    quarter = width // 4
    ahead, back, across = 0, 1, 2
    relays = [
        rs_copy(i, relay_out.at[i], relay_in.at[i], step) for i, step in ((0, 1), (1, nx - 1))
    ]
    direct = rs_copy(2, rs_out.at[across, pl.ds(1, 2)], rs_in.at[across, pl.ds(1, 2)], 2)
    early = [
        rs_copy(3, rs_out.at[ahead, pl.ds(1, 3)], rs_in.at[ahead, pl.ds(1, 3)], 1),
        rs_copy(4, rs_out.at[back, pl.ds(0, 3)], rs_in.at[back, pl.ds(0, 3)], nx - 1),
    ]
    late = [
        rs_copy(5, rs_out.at[ahead, 0], rs_in.at[ahead, 0], 1),
        rs_copy(6, rs_out.at[back, 3], rs_in.at[back, 3], nx - 1),
    ]

    def block(step):
        whole = parts[step] + part(step, 1 - core, normed[...])
        return [whole[:, i * quarter : (i + 1) * quarter] for i in range(4)]

    pieces = block(2)
    relay_out[0] = pieces[0].astype(BF16)
    relays[0].start()
    relay_out[1] = pieces[3].astype(BF16)
    relays[1].start()
    rs_out[across, 1] = pieces[1].astype(BF16)
    rs_out[across, 2] = pieces[2].astype(BF16)
    direct.start()
    pieces = block(1)
    for i in (1, 2, 3):
        rs_out[ahead, i] = pieces[i].astype(BF16)
    early[0].start()
    waiting = [pieces[0]]
    pieces = block(nx - 1)
    for i in (0, 1, 2):
        rs_out[back, i] = pieces[i].astype(BF16)
    early[1].start()
    waiting.append(pieces[3])
    for i, (side, where) in enumerate(((ahead, 0), (back, 3))):
        relays[i].wait_recv()
        rs_out[side, where] = (waiting[i] + relay_in[i].astype(F32)).astype(BF16)
        late[i].start()
    total = part(0, core, pass_out[core]) + part(0, 1 - core, normed[...])
    for copy in early:
        copy.wait_recv()
    direct.wait_recv()
    for copy in late:
        copy.wait_recv()
    for i in range(4):
        cols = slice(i * quarter, (i + 1) * quarter)
        piece = total[:, cols] + rs_in[ahead, i].astype(F32) + rs_in[back, i].astype(F32)
        if i in (1, 2):
            piece = piece + rs_in[across, i].astype(F32)
        out_ref[:, cols] = piece

    @pl.when(sends_halo)
    def _():
        for side in range(2):
            for copy in halo_copies(side):
                copy.wait_send()

    for copy in swap:
        copy.wait_send()
    for h in heads:
        decay_copy(h).wait_send()
        up_copy(h).wait_send()

    @pl.when(owns)
    def _():
        for target in range(nz):
            down_copy(target).wait_send()
        for later in range(1, ny):

            @pl.when(y < later)
            def _(later=later):
                carry_copy(y, later).wait_send()

    hand_over.wait_send()
    for copy in relays + early + late + [direct]:
        copy.wait_send()


def shards(
    q_in, k_in, v_in, conv_q, conv_k, conv_v, a_in, b_in, a_log, dt_bias, norm_weight, z_in, out_weight
):
    rows = q_in.shape[0]
    nz = v_in.shape[1] // DV
    nx = lax.axis_size("heads")
    ny = lax.axis_size("ctx") // (2 * nz)
    width = out_weight.shape[1] // nx
    half = q_in.shape[1] // 2
    half_v = v_in.shape[1] // 2
    hbm = pl.BlockSpec(memory_space=pltpu.HBM)
    vmem = pl.BlockSpec(memory_space=pltpu.VMEM)
    dma = pltpu.SemaphoreType.DMA
    message = (DK + TAIL, DK + DV)
    scratch = [
        pltpu.VMEM((2, rows, half), BF16),
        pltpu.VMEM((2, rows, half), BF16),
        pltpu.VMEM((2, rows, half_v), BF16),
        pltpu.VMEM((2, rows, half_v), BF16),
        pltpu.VMEM(out_weight.shape, BF16),
        pltpu.VMEM((2, nz, rows), F32),
        pltpu.VMEM((2, nz, rows), F32),
        pltpu.VMEM((1, nz), F32),
        pltpu.VMEM((1, nz), F32),
        pltpu.VMEM((1, DV), F32),
        pltpu.VMEM(conv_q.shape, BF16),
        pltpu.VMEM(conv_k.shape, BF16),
        pltpu.VMEM(conv_v.shape, BF16),
        pltpu.VMEM((TAIL, half), BF16),
        pltpu.VMEM((TAIL, half), BF16),
        pltpu.VMEM((TAIL, half_v), BF16),
        pltpu.VMEM((rows + 8, half_v), F32),
        pltpu.VMEM((2, rows, half), BF16),
        pltpu.VMEM((2, rows, half), BF16),
        pltpu.VMEM((2, rows, half_v), BF16),
        pltpu.VMEM((nz // 2, 8, 128), F32),
        pltpu.VMEM((nz, 8, 128), F32),
        pltpu.VMEM((nz // 2, DK, DK + DV), BF16),
        pltpu.VMEM((nz, DK, DK + DV), BF16),
        pltpu.VMEM((ny,) + message, BF16),
        pltpu.VMEM((nz, DK, DV), F32),
        pltpu.VMEM((nz, DK, DK), BF16),
        pltpu.VMEM((nz, 8, 128), F32),
        pltpu.VMEM((DK, DV), F32),
        pltpu.VMEM((nz, DK, DV), BF16),
        pltpu.VMEM((nz // 2, DK, DV), BF16),
        pltpu.VMEM((nz // 2, 2 * rows, 2 * DK), BF16),
        pltpu.VMEM((nz // 2, 2 * rows, DV), F32),
        pltpu.VMEM((rows, half_v), BF16),
        pltpu.VMEM((2, rows, half_v), BF16),
        pltpu.VMEM((2, rows, half_v), F32),
        pltpu.VMEM((2, rows, width // 4), BF16),
        pltpu.VMEM((2, rows, width // 4), BF16),
        pltpu.VMEM((3, 4, rows, width // 4), BF16),
        pltpu.VMEM((3, 4, rows, width // 4), BF16),
        dma((13,)),
        dma((6,)),
        dma((6,)),
        dma((6,)),
        dma((3,)),
        dma((nz // 2,)),
        dma((nz,)),
        dma((nz // 2,)),
        dma((nz,)),
        dma((ny,)),
        dma((ny,)),
        dma((nz,)),
        dma((nz // 2,)),
        dma((2,)),
        dma((7,)),
        dma((7,)),
    ]
    call = pl.pallas_call(
        functools.partial(kernel, nx, ny, nz),
        out_shape=jax.ShapeDtypeStruct((rows, width), F32),
        in_specs=[hbm] * 13,
        out_specs=vmem,
        scratch_shapes=scratch,
        compiler_params=pltpu.CompilerParams(
            collective_id=0, has_side_effects=True, vmem_limit_bytes=40 * 1024 * 1024
        ),
        cost_estimate=pl.CostEstimate(
            flops=2_000_000_000, bytes_accessed=6_000_000, transcendentals=1_000_000
        ),
    )
    operands = (
        q_in,
        k_in,
        v_in,
        z_in,
        out_weight,
        a_in.T,
        b_in.T,
        a_log.reshape(1, nz),
        dt_bias.reshape(1, nz),
        norm_weight.reshape(1, DV),
        conv_q,
        conv_k,
        conv_v,
    )
    return call(*(pltpu.with_memory_space_constraint(value, pltpu.HBM) for value in operands))


def solution(mesh):
    in_specs = (
        P("ctx", "heads"),
        P("ctx", "heads"),
        P("ctx", "heads"),
        P(None, "heads"),
        P(None, "heads"),
        P(None, "heads"),
        P("ctx", "heads"),
        P("ctx", "heads"),
        P("heads"),
        P("heads"),
        P(),
        P("ctx", "heads"),
        P("heads", None),
    )
    out_specs = P("ctx", "heads")
    return jax.shard_map(shards, mesh=mesh, in_specs=in_specs, out_specs=out_specs, check_vma=False)
```

```python
import functools

import jax
import jax.numpy as jnp
from jax import lax
from jax.experimental import pallas as pl
from jax.experimental.pallas import tpu as pltpu
from jax.sharding import PartitionSpec as P

DK = 128
DV = 128
TAIL = 16
MESH = pl.DeviceIdType.MESH
F32 = jnp.float32
BF16 = jnp.bfloat16
HIGHEST = lax.Precision.HIGHEST


def split(value):
    high = value.astype(BF16)
    return high, (value - high.astype(F32)).astype(BF16)


def mm(left, right):
    return jnp.dot(left, right, preferred_element_type=F32)


def one_pass(left, right):
    return mm(left.astype(BF16), right.astype(BF16))


def split_left(left, right):
    high, low = split(left)
    return mm(jnp.concatenate([high, low], axis=1), jnp.concatenate([right, right], axis=0))


def split_right(left, right):
    high, low = split(right)
    return mm(jnp.concatenate([left, left], axis=1), jnp.concatenate([high, low], axis=0))


def split_both(left, right):
    left_high, left_low = split(left)
    right_high, right_low = split(right)
    return mm(
        jnp.concatenate([left_high, left_low], axis=1),
        jnp.concatenate([right_high, right_high], axis=0),
    ) + mm(left_high, right_low)


def silu(value):
    return value * (1.0 / (1.0 + jnp.exp(-value)))


def three_parts(value):
    first = value.astype(BF16).astype(F32)
    second = (value - first).astype(BF16).astype(F32)
    return first, second, value - first - second


def pack_decay(decay, width):
    row = lax.broadcasted_iota(jnp.int32, (TAIL, width), 0)
    first, second, third = three_parts(decay)
    zero = jnp.zeros((TAIL, width), F32)
    block = jnp.where(row == 0, first, jnp.where(row == 1, second, jnp.where(row == 2, third, zero)))
    return block.astype(BF16)


def kernel(
    nx,
    ny,
    nz,
    q_hbm,
    k_hbm,
    v_hbm,
    z_hbm,
    w_hbm,
    a_hbm,
    b_hbm,
    alog_hbm,
    bias_hbm,
    gain_hbm,
    cq_hbm,
    ck_hbm,
    cv_hbm,
    out_ref,
    q_in,
    k_in,
    v_in,
    z_in,
    w_in,
    a_in,
    b_in,
    alog_ref,
    bias_ref,
    gain_ref,
    cq_ref,
    ck_ref,
    cv_ref,
    halo_q,
    halo_k,
    halo_v,
    ext,
    qc_all,
    kc_all,
    vc_all,
    decay_out,
    decay_in,
    up_out,
    up_in,
    carry_state,
    carry_map,
    pre_state,
    pre_map,
    pre_decay,
    sigma,
    down_out,
    down_in,
    reads,
    local,
    normed,
    pass_out,
    gates,
    relay_out,
    relay_in,
    rs_out,
    rs_in,
    load_sem,
    swap_send,
    swap_recv,
    halo_send,
    halo_recv,
    decay_send,
    decay_recv,
    up_send,
    up_recv,
    y_send,
    y_recv,
    down_send,
    down_recv,
    pass_sem,
    rs_send,
    rs_recv,
):
    rows = out_ref.shape[0]
    width = out_ref.shape[1]
    set_heads = nz // 2
    set_keys = nz // 4
    ring = 2 * nz
    count = ny * ring
    me = lax.axis_index("ctx")
    x = lax.axis_index("heads")
    y = me // ring
    place = lax.rem(me, ring)
    z = place // 2
    core = lax.rem(place, 2)
    chip = me // 2
    chips = count // 2
    partner = me + 1 - 2 * core
    heads = range(set_heads)
    keys = range(set_keys)
    both_shards = range(2)
    units = [(u, h) for u in both_shards for h in heads]
    key_units = [(u, s) for u in both_shards for s in keys]

    sender_core = z // set_heads
    owns = core != sender_core

    def owner_of(h):
        return y * ring + 2 * (set_heads * core + h) + 1 - core

    def cols_of(which, size):
        return pl.ds(pl.multiple_of(which * size, 128), size)

    streams = (
        (k_hbm, k_in, halo_k, ck_ref, kc_all, set_keys * DK),
        (v_hbm, v_in, halo_v, cv_ref, vc_all, set_heads * DV),
        (q_hbm, q_in, halo_q, cq_ref, qc_all, set_keys * DK),
    )
    wide = [(source, target, size) for source, target, _, _, _, size in streams]
    wide.append((z_hbm, z_in, set_heads * DV))
    pairs = [(source.at[:, cols_of(core, size)], target.at[core]) for source, target, size in wide]
    pairs += [
        (a_hbm, a_in.at[core]),
        (b_hbm, b_in.at[core]),
        (alog_hbm, alog_ref),
        (bias_hbm, bias_ref),
        (ck_hbm, ck_ref),
        (cv_hbm, cv_ref),
        (cq_hbm, cq_ref),
        (gain_hbm, gain_ref),
        (w_hbm, w_in),
    ]
    loads = [
        pltpu.make_async_copy(source, target, load_sem.at[i])
        for i, (source, target) in enumerate(pairs)
    ]
    first = [0, 1, 2, 8, 9, 10, 4, 5, 6, 7]
    rest = [3, 11, 12]
    for i in first + rest:
        loads[i].start()

    barrier = pltpu.get_barrier_semaphore()

    def greet(ctx, heads):
        pl.semaphore_signal(barrier, inc=1, device_id=(ctx, heads), device_id_type=MESH)

    over = jnp.logical_and(place == ring - 1, me < count - 1)
    under = jnp.logical_and(z == 0, y > 0)

    @pl.when(over)
    def _():
        greet(me + 1, x)
        greet(me + 2, x)

    @pl.when(under)
    def _():
        greet(y * ring - 1, x)

    for step in sorted(range(1, ring), key=lambda step: (min(step, ring - step), -step)):
        greet(y * ring + lax.rem(place + step, ring), x)
    for step in range(1, ny):
        greet(lax.rem(me + step * ring, count), x)
    for step in range(1, nx):
        greet(me, lax.rem(x + step, nx))
    pl.semaphore_wait(
        barrier,
        (ring - 1) + (ny - 1) + (nx - 1) + 2 * over.astype(jnp.int32) + under.astype(jnp.int32),
    )

    def halo_copies(side):
        return [
            pltpu.make_async_remote_copy(
                src_ref=source.at[pl.ds(rows - TAIL, TAIL), cols_of(side, size)],
                dst_ref=target,
                send_sem=halo_send.at[3 * side + i],
                recv_sem=halo_recv.at[i],
                device_id=(2 * lax.rem(chip + 1, chips) + side, x),
                device_id_type=MESH,
            )
            for i, (source, _, target, _, _, size) in enumerate(streams)
        ]

    sends_halo = jnp.logical_and(core == 1, chip < chips - 1)

    @pl.when(sends_halo)
    def _():
        for side in range(2):
            for copy in halo_copies(side):
                copy.start()

    def swap_copies(shard):
        return [
            pltpu.make_async_remote_copy(
                src_ref=source,
                dst_ref=target.at[shard],
                send_sem=swap_send.at[i],
                recv_sem=swap_recv.at[i],
                device_id=(partner, x),
                device_id_type=MESH,
            )
            for i, (source, target) in enumerate(
                [
                    (source.at[:, cols_of(1 - core, size)], target)
                    for source, target, size in wide[:3]
                ]
                + [(a_hbm, a_in), (b_hbm, b_in)]
                + [
                    (source.at[:, cols_of(1 - core, size)], target)
                    for source, target, size in wide[3:]
                ]
            )
        ]

    swap = swap_copies(core)
    swapped = swap_copies(1 - core)
    for copy in swap:
        copy.start()

    @pl.when(chip == 0)
    def _():
        halo_k[...] = jnp.zeros_like(halo_k)
        halo_v[...] = jnp.zeros_like(halo_v)
        halo_q[...] = jnp.zeros_like(halo_q)

    def conv(before, data, taps_ref, size):
        height = data.shape[0]
        ext[0:8, 0:size] = before
        ext[8 : 8 + height, 0:size] = data.astype(F32)
        taps = taps_ref[:, cols_of(core, size)].astype(F32)
        total = jnp.zeros((height, size), F32)
        for j in range(4):
            total = total + taps[j : j + 1] * ext[5 + j : 5 + j + height, 0:size]
        return silu(total).astype(BF16)

    for i in first:
        loads[i].wait()
    for _, data, _, taps_ref, result, size in streams:
        result[core] = conv(jnp.zeros((8, size), F32), data[core], taps_ref, size)

    row = lax.broadcasted_iota(jnp.int32, (rows, rows), 0)
    col = lax.broadcasted_iota(jnp.int32, (rows, rows), 1)
    upto = row >= col
    strict = row > col
    apart = jnp.bitwise_xor(row, col)

    for i in range(3):
        swapped[i].wait_recv()
    for _, data, _, taps_ref, result, size in streams:
        result[1 - core] = conv(jnp.zeros((8, size), F32), data[1 - core], taps_ref, size)

    for i in range(3, 5):
        swapped[i].wait_recv()
    head_row = lax.broadcasted_iota(jnp.int32, (nz, nz), 0)
    head_lane = lax.broadcasted_iota(jnp.int32, (nz, nz), 1)

    def per_head(values):
        return jnp.sum(jnp.where(head_row == head_lane, values, 0.0), axis=1, keepdims=True)

    slot = lax.broadcasted_iota(jnp.int32, (128, nz), 0)
    from_head = lax.broadcasted_iota(jnp.int32, (128, nz), 1)

    def placing(start):
        wanted = set_heads * core + slot - start
        inside = jnp.logical_and(slot >= start, slot < start + set_heads)
        return jnp.where(jnp.logical_and(inside, wanted == from_head), 1.0, 0.0)

    def exact(left, right):
        return jnp.dot(left, right, preferred_element_type=F32, precision=HIGHEST)

    bias, rate = per_head(bias_ref[...]), jnp.exp(per_head(alog_ref[...]))
    before_or_at = jnp.where(row <= col, 1.0, 0.0)
    by_row = jnp.zeros((128, rows), F32)
    for u in both_shards:
        gate_in = a_in[u] + bias
        softplus = jnp.maximum(gate_in, 0.0) + jnp.log1p(jnp.exp(-jnp.abs(gate_in)))
        cumulative = exact(-rate * softplus, before_or_at)
        beta = 1.0 / (1.0 + jnp.exp(-b_in[u]))
        by_row = by_row + exact(placing(16 * u), cumulative)
        by_row = by_row + exact(placing(16 * u + set_heads), beta)
    columns = jnp.transpose(by_row)

    def decay_copy(h):
        return pltpu.make_async_remote_copy(
            src_ref=decay_out.at[h],
            dst_ref=decay_in.at[z],
            send_sem=decay_send.at[h],
            recv_sem=decay_recv.at[z],
            device_id=(owner_of(h), x),
            device_id_type=MESH,
        )

    for h in heads:
        chip_decay = [
            jnp.exp(columns[rows - 1 : rows, 16 * u + h : 16 * u + h + 1]) for u in both_shards
        ]
        decay_out[h] = jnp.broadcast_to(chip_decay[0] * chip_decay[1], (8, 128))
        decay_copy(h).start()

    @pl.when(chip > 0)
    def _():
        for copy in halo_copies(0):
            copy.wait_recv()

    def inverse_norm(block):
        entries = block.astype(F32)
        return lax.rsqrt(jnp.sum(entries * entries, axis=1, keepdims=True) + 1e-6)

    for _, data, halo, taps_ref, result, size in streams:
        for u in both_shards:
            before = halo[...] if u == 0 else data[0, rows - TAIL : rows, :]
            result[u, 0:TAIL, :] = conv(
                before.astype(F32)[8:16], data[u, 0:TAIL, :], taps_ref, size
            )

    def key_of(u, s):
        return kc_all[u, :, s * DK : (s + 1) * DK]

    def query_of(u, s):
        return qc_all[u, :, s * DK : (s + 1) * DK]

    wide_lane = lax.broadcasted_iota(jnp.int32, (rows, 128), 1)
    for u, s in key_units:
        place_of = 16 * u + 2 * set_heads + s
        columns = jnp.where(wide_lane == place_of, inverse_norm(key_of(u, s)), columns)
        columns = jnp.where(
            wide_lane == place_of + set_keys, inverse_norm(query_of(u, s)) * DK**-0.5, columns
        )
    by_row = jnp.transpose(columns)

    def column(u, index):
        return columns[:, 16 * u + index : 16 * u + index + 1]

    def lane_row(u, index):
        return by_row[16 * u + index : 16 * u + index + 1, :]

    gram, query_gram, key_t = {}, {}, {}
    for u, s in key_units:
        contract = (((1,), (1,)), ((), ()))
        gram[u, s] = lax.dot_general(
            key_of(u, s), key_of(u, s), contract, preferred_element_type=F32
        )
        query_gram[u, s] = lax.dot_general(
            query_of(u, s), key_of(u, s), contract, preferred_element_type=F32
        )
        key_t[u, s] = jnp.transpose(key_of(u, s).astype(F32)).astype(BF16)
    within, lower, inverse = {}, {}, {}
    for u, h in units:
        s = h // 2
        gaps = column(u, h) - lane_row(u, h)
        within[u, h] = jnp.exp(jnp.where(upto, gaps, -1e30)) * lane_row(u, 2 * set_heads + s)
        scale = column(u, set_heads + h) * column(u, 2 * set_heads + s)
        lower[u, h] = jnp.where(strict, scale * gram[u, s] * within[u, h], 0.0)
        inverse[u, h] = jnp.where(apart == 1, -lower[u, h], 0.0)
    level = 1
    while (1 << level) < rows:
        inner = {}
        for i in units:
            block = jnp.where((apart >> level) == 1, lower[i], 0.0)
            inner[i] = block + one_pass(block, inverse[i])
        for i in units:
            inverse[i] = inverse[i] - inner[i] - one_pass(inverse[i], inner[i])
        level += 1
    values, maps, shard_maps, decays = {}, {}, {}, {}
    for u, h in units:
        s = h // 2
        solve = jnp.where(row == col, 1.0, inverse[u, h]) * lane_row(u, set_heads + h)
        values[u, h] = split_left(solve, vc_all[u, :, h * DV : (h + 1) * DV])
        key_solve = solve * (jnp.exp(lane_row(u, h)) * lane_row(u, 2 * set_heads + s))
        maps[u, h] = split_left(key_solve, key_of(u, s))
    for u, h in units:
        s = h // 2
        last = column(u, h)[rows - 1 : rows, :]
        tail = jnp.exp(last - column(u, h)) * column(u, 2 * set_heads + s)
        both = jnp.concatenate([values[u, h] * tail, maps[u, h] * tail], axis=1)
        shard_maps[u, h] = split_right(key_t[u, s], both)
        decays[u, h] = jnp.exp(last)

    eye = row[0:DK, 0:DK] == col[0:DK, 0:DK]

    def decay_of(block):
        return jnp.sum(block.astype(F32), axis=0, keepdims=True)

    def map_of(message, decay):
        return jnp.where(eye, decay[:, 0:1], 0.0) - message[:, DV:].astype(F32)

    def compose(message, decay, carried):
        state = decay * carried[:, 0:DV] + message[:, 0:DV].astype(F32)
        fresh = jnp.concatenate([state, decay * carried[:, DV:]], axis=1)
        return fresh - mm(message[:, DV:].astype(BF16), carried.astype(BF16))

    def put_maps(target, carried, decay):
        target[0:DK, 0:DV] = carried[:, 0:DV].astype(BF16)
        target[0:DK, DV:] = map_of(carried, decay).astype(BF16)

    def up_copy(h):
        return pltpu.make_async_remote_copy(
            src_ref=up_out.at[h],
            dst_ref=up_in.at[z],
            send_sem=up_send.at[h],
            recv_sem=up_recv.at[z],
            device_id=(owner_of(h), x),
            device_id_type=MESH,
        )

    joined = {}
    for h in heads:
        early = shard_maps[0, h]
        carried = jnp.concatenate([early[:, 0:DV], map_of(early, decays[0, h])], axis=1)
        joined[h] = compose(shard_maps[1, h], decays[1, h], carried)
    for h in heads:
        put_maps(up_out.at[h], joined[h], decays[0, h] * decays[1, h])
    far_first = sorted(range(nz), key=lambda offset: -min(offset, nz - offset))
    for offset in far_first:
        target_chip = lax.rem(z + offset, nz)

        @pl.when(target_chip // set_heads == core)
        def _(h=lax.rem(target_chip, set_heads)):
            up_copy(h).start()

    for u, h in units:
        s = h // 2
        scale = column(u, 2 * set_heads + set_keys + s)
        attend = jnp.where(upto, query_gram[u, s] * within[u, h] * scale, 0.0)
        both = split_both(attend, jnp.concatenate([values[u, h], maps[u, h]], axis=1))
        fixed = both[:, 0:DV]
        read = jnp.exp(column(u, h)) * scale * query_of(u, s).astype(F32) - both[:, DV:]
        if u == 1:
            moved = split_both(read, shard_maps[0, h])
            fixed = fixed + moved[:, 0:DV]
            read = decays[0, h] * read - moved[:, DV:]
        high, low = split(read)
        local[h, u * rows : (u + 1) * rows, :] = fixed
        reads[h, u * rows : (u + 1) * rows, 0:DK] = high
        reads[h, u * rows : (u + 1) * rows, DK:] = low

    def carry_copy(source, target_y, i):
        held = (carry_state, carry_map)[i]
        return pltpu.make_async_remote_copy(
            src_ref=held.at[source],
            dst_ref=held.at[source],
            send_sem=y_send.at[i * ny + target_y],
            recv_sem=y_recv.at[i * ny + source],
            device_id=(target_y * ring + place, x),
            device_id_type=MESH,
        )

    def each_carry(act):
        for later in range(1, ny):

            @pl.when(y < later)
            def _(later=later):
                act(carry_copy(y, later, 0))

                @pl.when(y > 0)
                def _():
                    act(carry_copy(y, later, 1))

    def down_copy(target):
        slot = lax.rem(z, set_heads)
        return pltpu.make_async_remote_copy(
            src_ref=down_out.at[target],
            dst_ref=down_in.at[slot],
            send_sem=down_send.at[target],
            recv_sem=down_recv.at[slot],
            device_id=(y * ring + 2 * target + sender_core, x),
            device_id_type=MESH,
        )

    for i in rest:
        loads[i].wait()
    swapped[5].wait_recv()
    for h in heads:
        cols = slice(h * DV, (h + 1) * DV)
        for u in both_shards:
            gates[u, :, cols] = silu(z_in[u, :, cols].astype(F32)) * gain_ref[...]

    @pl.when(owns)
    def _():
        pre_state[0] = jnp.zeros((DK, DV), F32)
        pre_map[0] = jnp.zeros((DK, DK), BF16)
        pre_decay[0] = jnp.ones((8, 128), F32)
        spans = {}
        for j in range(nz):
            for source, target, sent, received in (
                (decay_out, decay_in, decay_send, decay_recv),
                (up_out, up_in, up_send, up_recv),
            ):
                pltpu.make_async_remote_copy(
                    src_ref=source.at[0],
                    dst_ref=target.at[j],
                    send_sem=sent.at[0],
                    recv_sem=received.at[j],
                    device_id=(partner, x),
                    device_id_type=MESH,
                ).wait_recv()
            decay = decay_in[j, 0:1, :]
            state, taken = up_in[j, :, 0:DV].astype(F32), up_in[j, :, DV:].astype(F32)
            carried = jnp.concatenate([state, jnp.where(eye, decay, 0.0) - taken], axis=1)
            spans[j, j + 1] = (carried, decay)

        def after(early, late):
            (carried, decay), (later_maps, later_decay) = spans[early], spans[late]
            message = jnp.concatenate(
                [later_maps[:, 0:DV], map_of(later_maps, later_decay)], axis=1
            )
            spans[early[0], late[1]] = (compose(message, later_decay, carried), decay * later_decay)

        size = 1
        while size < nz:
            for start in range(0, nz, 2 * size):
                after((start, start + size), (start + size, start + 2 * size))
            size *= 2
        carried, total_decay = spans[0, nz]
        carry_state[y] = carried[:, 0:DV].astype(BF16)
        carry_map[y, 0:DK, :] = map_of(carried, total_decay).astype(BF16)
        carry_map[y, DK:, :] = pack_decay(total_decay[:, 0:1], DK)
        each_carry(lambda copy: copy.start())

        for j in range(1, nz):
            if (0, j) not in spans:
                size = j & -j
                after((0, j - size), (j - size, j))
            carried, total_decay = spans[0, j]
            pre_state[j] = carried[:, 0:DV]
            pre_map[j] = map_of(carried, total_decay).astype(BF16)
            pre_decay[j] = jnp.broadcast_to(total_decay, (8, 128))

        sigma[...] = jnp.zeros((DK, DV), F32)
        for earlier in range(ny - 1):

            @pl.when(y > earlier)
            def _(earlier=earlier):
                carry_copy(earlier, y, 0).wait_recv()
                fresh = carry_state[earlier].astype(F32)
                if earlier == 0:
                    sigma[...] = fresh
                else:
                    carry_copy(earlier, y, 1).wait_recv()
                    state = sigma[...]
                    sigma[...] = (
                        decay_of(carry_map[earlier, DK:, :]) * state
                        - mm(carry_map[earlier, 0:DK, :], state.astype(BF16))
                        + fresh
                    )

        start_state = sigma[...]
        rounded = start_state.astype(BF16)
        for offset in far_first:
            target = lax.rem(z + offset, nz)
            down_out[target] = (
                pre_decay[target, 0:1, :] * start_state
                - mm(pre_map[target], rounded)
                + pre_state[target]
            ).astype(BF16)
            down_copy(target).start()

    cores = {}
    for h in heads:
        pltpu.make_async_remote_copy(
            src_ref=down_out.at[0],
            dst_ref=down_in.at[h],
            send_sem=down_send.at[0],
            recv_sem=down_recv.at[h],
            device_id=(owner_of(h), x),
            device_id_type=MESH,
        ).wait_recv()
    for h in heads:
        state = down_in[h]
        cores[h] = mm(reads[h], jnp.concatenate([state, state], axis=0)) + local[h]
    hand_over = pltpu.make_async_remote_copy(
        src_ref=pass_out.at[1 - core],
        dst_ref=normed,
        send_sem=pass_sem.at[0],
        recv_sem=pass_sem.at[1],
        device_id=(partner, x),
        device_id_type=MESH,
    )
    for h in heads:
        power = jnp.mean(cores[h] * cores[h], axis=1, keepdims=True)
        scaled = cores[h] * lax.rsqrt(power + 1e-6)
        cols = slice(h * DV, (h + 1) * DV)
        for u in both_shards:
            part_rows = scaled[u * rows : (u + 1) * rows]
            pass_out[u, :, cols] = (part_rows * gates[u, :, cols]).astype(BF16)
    hand_over.start()

    depth = set_heads * DV

    def part(step, which, operand):
        depth_rows = pl.ds(pl.multiple_of(which * depth, 128), depth)
        return mm(operand, w_in[depth_rows, cols_of(lax.rem(x + step, nx), width)])

    order = (2, 1, nx - 1)
    parts = {step: part(step, core, pass_out[core]) for step in order}
    pltpu.make_async_remote_copy(
        src_ref=pass_out.at[core],
        dst_ref=normed,
        send_sem=pass_sem.at[0],
        recv_sem=pass_sem.at[1],
        device_id=(partner, x),
        device_id_type=MESH,
    ).wait_recv()

    def rs_copy(i, source, target, step):
        return pltpu.make_async_remote_copy(
            src_ref=source,
            dst_ref=target,
            send_sem=rs_send.at[i],
            recv_sem=rs_recv.at[i],
            device_id=(me, lax.rem(x + step, nx)),
            device_id_type=MESH,
        )

    quarter = width // 4
    ahead, back, across = 0, 1, 2
    relays = [
        rs_copy(i, relay_out.at[i], relay_in.at[i], step) for i, step in ((0, 1), (1, nx - 1))
    ]
    direct = rs_copy(2, rs_out.at[across, pl.ds(1, 2)], rs_in.at[across, pl.ds(1, 2)], 2)
    early = [
        rs_copy(3, rs_out.at[ahead, pl.ds(1, 3)], rs_in.at[ahead, pl.ds(1, 3)], 1),
        rs_copy(4, rs_out.at[back, pl.ds(0, 3)], rs_in.at[back, pl.ds(0, 3)], nx - 1),
    ]
    late = [
        rs_copy(5, rs_out.at[ahead, 0], rs_in.at[ahead, 0], 1),
        rs_copy(6, rs_out.at[back, 3], rs_in.at[back, 3], nx - 1),
    ]

    def block(step):
        whole = parts[step] + part(step, 1 - core, normed[...])
        return [whole[:, i * quarter : (i + 1) * quarter] for i in range(4)]

    pieces = block(2)
    relay_out[0] = pieces[0].astype(BF16)
    relays[0].start()
    relay_out[1] = pieces[3].astype(BF16)
    relays[1].start()
    rs_out[across, 1] = pieces[1].astype(BF16)
    rs_out[across, 2] = pieces[2].astype(BF16)
    direct.start()
    pieces = block(1)
    for i in (1, 2, 3):
        rs_out[ahead, i] = pieces[i].astype(BF16)
    early[0].start()
    waiting = [pieces[0]]
    pieces = block(nx - 1)
    for i in (0, 1, 2):
        rs_out[back, i] = pieces[i].astype(BF16)
    early[1].start()
    waiting.append(pieces[3])
    for i, (side, where) in enumerate(((ahead, 0), (back, 3))):
        relays[i].wait_recv()
        rs_out[side, where] = (waiting[i] + relay_in[i].astype(F32)).astype(BF16)
        late[i].start()
    total = part(0, core, pass_out[core]) + part(0, 1 - core, normed[...])
    for copy in early:
        copy.wait_recv()
    direct.wait_recv()
    for copy in late:
        copy.wait_recv()
    for i in range(4):
        cols = slice(i * quarter, (i + 1) * quarter)
        piece = total[:, cols] + rs_in[ahead, i].astype(F32) + rs_in[back, i].astype(F32)
        if i in (1, 2):
            piece = piece + rs_in[across, i].astype(F32)
        out_ref[:, cols] = piece

    @pl.when(sends_halo)
    def _():
        for side in range(2):
            for copy in halo_copies(side):
                copy.wait_send()

    for copy in swap:
        copy.wait_send()
    for h in heads:
        decay_copy(h).wait_send()
        up_copy(h).wait_send()

    @pl.when(owns)
    def _():
        for target in range(nz):
            down_copy(target).wait_send()
        each_carry(lambda copy: copy.wait_send())

    hand_over.wait_send()
    for copy in relays + early + late + [direct]:
        copy.wait_send()


def shards(
    q_in, k_in, v_in, conv_q, conv_k, conv_v, a_in, b_in, a_log, dt_bias, norm_weight, z_in, out_weight
):
    rows = q_in.shape[0]
    nz = v_in.shape[1] // DV
    nx = lax.axis_size("heads")
    ny = lax.axis_size("ctx") // (2 * nz)
    width = out_weight.shape[1] // nx
    half = q_in.shape[1] // 2
    half_v = v_in.shape[1] // 2
    hbm = pl.BlockSpec(memory_space=pltpu.HBM)
    vmem = pl.BlockSpec(memory_space=pltpu.VMEM)
    dma = pltpu.SemaphoreType.DMA
    scratch = [
        pltpu.VMEM((2, rows, half), BF16),
        pltpu.VMEM((2, rows, half), BF16),
        pltpu.VMEM((2, rows, half_v), BF16),
        pltpu.VMEM((2, rows, half_v), BF16),
        pltpu.VMEM(out_weight.shape, BF16),
        pltpu.VMEM((2, nz, rows), F32),
        pltpu.VMEM((2, nz, rows), F32),
        pltpu.VMEM((1, nz), F32),
        pltpu.VMEM((1, nz), F32),
        pltpu.VMEM((1, DV), F32),
        pltpu.VMEM(conv_q.shape, BF16),
        pltpu.VMEM(conv_k.shape, BF16),
        pltpu.VMEM(conv_v.shape, BF16),
        pltpu.VMEM((TAIL, half), BF16),
        pltpu.VMEM((TAIL, half), BF16),
        pltpu.VMEM((TAIL, half_v), BF16),
        pltpu.VMEM((rows + 8, half_v), F32),
        pltpu.VMEM((2, rows, half), BF16),
        pltpu.VMEM((2, rows, half), BF16),
        pltpu.VMEM((2, rows, half_v), BF16),
        pltpu.VMEM((nz // 2, 8, 128), F32),
        pltpu.VMEM((nz, 8, 128), F32),
        pltpu.VMEM((nz // 2, DK, DK + DV), BF16),
        pltpu.VMEM((nz, DK, DK + DV), BF16),
        pltpu.VMEM((ny, DK, DV), BF16),
        pltpu.VMEM((ny, DK + TAIL, DK), BF16),
        pltpu.VMEM((nz, DK, DV), F32),
        pltpu.VMEM((nz, DK, DK), BF16),
        pltpu.VMEM((nz, 8, 128), F32),
        pltpu.VMEM((DK, DV), F32),
        pltpu.VMEM((nz, DK, DV), BF16),
        pltpu.VMEM((nz // 2, DK, DV), BF16),
        pltpu.VMEM((nz // 2, 2 * rows, 2 * DK), BF16),
        pltpu.VMEM((nz // 2, 2 * rows, DV), F32),
        pltpu.VMEM((rows, half_v), BF16),
        pltpu.VMEM((2, rows, half_v), BF16),
        pltpu.VMEM((2, rows, half_v), F32),
        pltpu.VMEM((2, rows, width // 4), BF16),
        pltpu.VMEM((2, rows, width // 4), BF16),
        pltpu.VMEM((3, 4, rows, width // 4), BF16),
        pltpu.VMEM((3, 4, rows, width // 4), BF16),
        dma((13,)),
        dma((6,)),
        dma((6,)),
        dma((6,)),
        dma((3,)),
        dma((nz // 2,)),
        dma((nz,)),
        dma((nz // 2,)),
        dma((nz,)),
        dma((2 * ny,)),
        dma((2 * ny,)),
        dma((nz,)),
        dma((nz // 2,)),
        dma((2,)),
        dma((7,)),
        dma((7,)),
    ]
    call = pl.pallas_call(
        functools.partial(kernel, nx, ny, nz),
        out_shape=jax.ShapeDtypeStruct((rows, width), F32),
        in_specs=[hbm] * 13,
        out_specs=vmem,
        scratch_shapes=scratch,
        compiler_params=pltpu.CompilerParams(
            collective_id=0, has_side_effects=True, vmem_limit_bytes=40 * 1024 * 1024
        ),
        cost_estimate=pl.CostEstimate(
            flops=2_000_000_000, bytes_accessed=6_000_000, transcendentals=1_000_000
        ),
    )
    operands = (
        q_in,
        k_in,
        v_in,
        z_in,
        out_weight,
        a_in.T,
        b_in.T,
        a_log.reshape(1, nz),
        dt_bias.reshape(1, nz),
        norm_weight.reshape(1, DV),
        conv_q,
        conv_k,
        conv_v,
    )
    return call(*(pltpu.with_memory_space_constraint(value, pltpu.HBM) for value in operands))


def solution(mesh):
    in_specs = (
        P("ctx", "heads"),
        P("ctx", "heads"),
        P("ctx", "heads"),
        P(None, "heads"),
        P(None, "heads"),
        P(None, "heads"),
        P("ctx", "heads"),
        P("ctx", "heads"),
        P("heads"),
        P("heads"),
        P(),
        P("ctx", "heads"),
        P("heads", None),
    )
    out_specs = P("ctx", "heads")
    return jax.shard_map(shards, mesh=mesh, in_specs=in_specs, out_specs=out_specs, check_vma=False)
```

```python
import functools

import jax
import jax.numpy as jnp
from jax import lax
from jax.experimental import pallas as pl
from jax.experimental.pallas import tpu as pltpu
from jax.sharding import PartitionSpec as P

DK = 128
DV = 128
TAIL = 16
MESH = pl.DeviceIdType.MESH
F32 = jnp.float32
BF16 = jnp.bfloat16
HIGHEST = lax.Precision.HIGHEST


def split(value):
    high = value.astype(BF16)
    return high, (value - high.astype(F32)).astype(BF16)


def mm(left, right):
    return jnp.dot(left, right, preferred_element_type=F32)


def one_pass(left, right):
    return mm(left.astype(BF16), right.astype(BF16))


def split_left(left, right):
    high, low = split(left)
    return mm(jnp.concatenate([high, low], axis=1), jnp.concatenate([right, right], axis=0))


def split_right(left, right):
    high, low = split(right)
    return mm(jnp.concatenate([left, left], axis=1), jnp.concatenate([high, low], axis=0))


def split_both(left, right):
    left_high, left_low = split(left)
    right_high, right_low = split(right)
    return mm(
        jnp.concatenate([left_high, left_low], axis=1),
        jnp.concatenate([right_high, right_high], axis=0),
    ) + mm(left_high, right_low)


def silu(value):
    return value * (1.0 / (1.0 + jnp.exp(-value)))


def three_parts(value):
    first = value.astype(BF16).astype(F32)
    second = (value - first).astype(BF16).astype(F32)
    return first, second, value - first - second


def pack_decay(decay, width):
    row = lax.broadcasted_iota(jnp.int32, (TAIL, width), 0)
    first, second, third = three_parts(decay)
    zero = jnp.zeros((TAIL, width), F32)
    block = jnp.where(row == 0, first, jnp.where(row == 1, second, jnp.where(row == 2, third, zero)))
    return block.astype(BF16)


def kernel(
    nx,
    ny,
    nz,
    q_hbm,
    k_hbm,
    v_hbm,
    z_hbm,
    w_hbm,
    a_hbm,
    b_hbm,
    alog_hbm,
    bias_hbm,
    gain_hbm,
    cq_hbm,
    ck_hbm,
    cv_hbm,
    out_ref,
    q_in,
    k_in,
    v_in,
    z_in,
    w_in,
    a_in,
    b_in,
    alog_ref,
    bias_ref,
    gain_ref,
    cq_ref,
    ck_ref,
    cv_ref,
    halo_q,
    halo_k,
    halo_v,
    ext,
    qc_all,
    kc_all,
    vc_all,
    decay_out,
    decay_in,
    up_out,
    up_in,
    carry_state,
    carry_map,
    pre_state,
    pre_map,
    pre_decay,
    sigma,
    down_out,
    down_in,
    reads,
    local,
    normed,
    pass_out,
    gates,
    relay_out,
    relay_in,
    rs_out,
    rs_in,
    load_sem,
    swap_send,
    swap_recv,
    halo_send,
    halo_recv,
    decay_send,
    decay_recv,
    up_send,
    up_recv,
    y_send,
    y_recv,
    down_send,
    down_recv,
    pass_sem,
    rs_send,
    rs_recv,
):
    rows = out_ref.shape[0]
    width = out_ref.shape[1]
    set_heads = nz // 2
    set_keys = nz // 4
    ring = 2 * nz
    count = ny * ring
    me = lax.axis_index("ctx")
    x = lax.axis_index("heads")
    y = me // ring
    place = lax.rem(me, ring)
    z = place // 2
    core = lax.rem(place, 2)
    chip = me // 2
    chips = count // 2
    partner = me + 1 - 2 * core
    heads = range(set_heads)
    keys = range(set_keys)
    both_shards = range(2)
    units = [(u, h) for u in both_shards for h in heads]
    key_units = [(u, s) for u in both_shards for s in keys]

    sender_core = z // set_heads
    owns = core != sender_core

    def owner_of(h):
        return y * ring + 2 * (set_heads * core + h) + 1 - core

    def cols_of(which, size):
        return pl.ds(pl.multiple_of(which * size, 128), size)

    streams = (
        (k_hbm, k_in, halo_k, ck_ref, kc_all, set_keys * DK),
        (v_hbm, v_in, halo_v, cv_ref, vc_all, set_heads * DV),
        (q_hbm, q_in, halo_q, cq_ref, qc_all, set_keys * DK),
    )
    wide = [(source, target, size) for source, target, _, _, _, size in streams]
    wide.append((z_hbm, z_in, set_heads * DV))
    pairs = [(source.at[:, cols_of(core, size)], target.at[core]) for source, target, size in wide]
    pairs += [
        (a_hbm, a_in.at[core]),
        (b_hbm, b_in.at[core]),
        (alog_hbm, alog_ref),
        (bias_hbm, bias_ref),
        (ck_hbm, ck_ref),
        (cv_hbm, cv_ref),
        (cq_hbm, cq_ref),
        (gain_hbm, gain_ref),
        (w_hbm, w_in),
    ]
    loads = [
        pltpu.make_async_copy(source, target, load_sem.at[i])
        for i, (source, target) in enumerate(pairs)
    ]
    first = [0, 1, 2, 8, 9, 10, 4, 5, 6, 7]
    rest = [3, 11, 12]
    for i in first:
        loads[i].start()

    barrier = pltpu.get_barrier_semaphore()

    def greet(ctx, heads):
        pl.semaphore_signal(barrier, inc=1, device_id=(ctx, heads), device_id_type=MESH)

    over = jnp.logical_and(place == ring - 1, me < count - 1)
    under = jnp.logical_and(z == 0, y > 0)

    @pl.when(over)
    def _():
        greet(me + 1, x)
        greet(me + 2, x)

    @pl.when(under)
    def _():
        greet(y * ring - 1, x)

    for step in sorted(range(1, ring), key=lambda step: (min(step, ring - step), -step)):
        greet(y * ring + lax.rem(place + step, ring), x)
    for step in range(1, ny):
        greet(lax.rem(me + step * ring, count), x)
    for step in range(1, nx):
        greet(me, lax.rem(x + step, nx))
    pl.semaphore_wait(
        barrier,
        (ring - 1) + (ny - 1) + (nx - 1) + 2 * over.astype(jnp.int32) + under.astype(jnp.int32),
    )

    def halo_copies(side):
        return [
            pltpu.make_async_remote_copy(
                src_ref=source.at[pl.ds(rows - TAIL, TAIL), cols_of(side, size)],
                dst_ref=target,
                send_sem=halo_send.at[3 * side + i],
                recv_sem=halo_recv.at[i],
                device_id=(2 * lax.rem(chip + 1, chips) + side, x),
                device_id_type=MESH,
            )
            for i, (source, _, target, _, _, size) in enumerate(streams)
        ]

    sends_halo = jnp.logical_and(core == 1, chip < chips - 1)

    @pl.when(sends_halo)
    def _():
        for side in range(2):
            for copy in halo_copies(side):
                copy.start()

    def swap_copies(shard):
        return [
            pltpu.make_async_remote_copy(
                src_ref=source,
                dst_ref=target.at[shard],
                send_sem=swap_send.at[i],
                recv_sem=swap_recv.at[i],
                device_id=(partner, x),
                device_id_type=MESH,
            )
            for i, (source, target) in enumerate(
                [
                    (source.at[:, cols_of(1 - core, size)], target)
                    for source, target, size in wide[:3]
                ]
                + [(a_hbm, a_in), (b_hbm, b_in)]
                + [
                    (source.at[:, cols_of(1 - core, size)], target)
                    for source, target, size in wide[3:]
                ]
            )
        ]

    swap = swap_copies(core)
    swapped = swap_copies(1 - core)
    for copy in swap:
        copy.start()

    @pl.when(chip == 0)
    def _():
        halo_k[...] = jnp.zeros_like(halo_k)
        halo_v[...] = jnp.zeros_like(halo_v)
        halo_q[...] = jnp.zeros_like(halo_q)

    def conv(before, data, taps_ref, size):
        height = data.shape[0]
        ext[0:8, 0:size] = before
        ext[8 : 8 + height, 0:size] = data.astype(F32)
        taps = taps_ref[:, cols_of(core, size)].astype(F32)
        total = jnp.zeros((height, size), F32)
        for j in range(4):
            total = total + taps[j : j + 1] * ext[5 + j : 5 + j + height, 0:size]
        return silu(total).astype(BF16)

    for i in first:
        loads[i].wait()
    for _, data, _, taps_ref, result, size in streams:
        result[core] = conv(jnp.zeros((8, size), F32), data[core], taps_ref, size)

    row = lax.broadcasted_iota(jnp.int32, (rows, rows), 0)
    col = lax.broadcasted_iota(jnp.int32, (rows, rows), 1)
    upto = row >= col
    strict = row > col
    apart = jnp.bitwise_xor(row, col)

    for i in range(3):
        swapped[i].wait_recv()
    for i in rest:
        loads[i].start()
    for _, data, _, taps_ref, result, size in streams:
        result[1 - core] = conv(jnp.zeros((8, size), F32), data[1 - core], taps_ref, size)

    for i in range(3, 5):
        swapped[i].wait_recv()
    head_row = lax.broadcasted_iota(jnp.int32, (nz, nz), 0)
    head_lane = lax.broadcasted_iota(jnp.int32, (nz, nz), 1)

    def per_head(values):
        return jnp.sum(jnp.where(head_row == head_lane, values, 0.0), axis=1, keepdims=True)

    slot = lax.broadcasted_iota(jnp.int32, (128, nz), 0)
    from_head = lax.broadcasted_iota(jnp.int32, (128, nz), 1)

    def placing(start):
        wanted = set_heads * core + slot - start
        inside = jnp.logical_and(slot >= start, slot < start + set_heads)
        return jnp.where(jnp.logical_and(inside, wanted == from_head), 1.0, 0.0)

    def exact(left, right):
        return jnp.dot(left, right, preferred_element_type=F32, precision=HIGHEST)

    bias, rate = per_head(bias_ref[...]), jnp.exp(per_head(alog_ref[...]))
    before_or_at = jnp.where(row <= col, 1.0, 0.0)
    by_row = jnp.zeros((128, rows), F32)
    for u in both_shards:
        gate_in = a_in[u] + bias
        softplus = jnp.maximum(gate_in, 0.0) + jnp.log1p(jnp.exp(-jnp.abs(gate_in)))
        cumulative = exact(-rate * softplus, before_or_at)
        beta = 1.0 / (1.0 + jnp.exp(-b_in[u]))
        by_row = by_row + exact(placing(16 * u), cumulative)
        by_row = by_row + exact(placing(16 * u + set_heads), beta)
    columns = jnp.transpose(by_row)

    def decay_copy(h):
        return pltpu.make_async_remote_copy(
            src_ref=decay_out.at[h],
            dst_ref=decay_in.at[z],
            send_sem=decay_send.at[h],
            recv_sem=decay_recv.at[z],
            device_id=(owner_of(h), x),
            device_id_type=MESH,
        )

    for h in heads:
        chip_decay = [
            jnp.exp(columns[rows - 1 : rows, 16 * u + h : 16 * u + h + 1]) for u in both_shards
        ]
        decay_out[h] = jnp.broadcast_to(chip_decay[0] * chip_decay[1], (8, 128))
        decay_copy(h).start()

    @pl.when(chip > 0)
    def _():
        for copy in halo_copies(0):
            copy.wait_recv()

    def inverse_norm(block):
        entries = block.astype(F32)
        return lax.rsqrt(jnp.sum(entries * entries, axis=1, keepdims=True) + 1e-6)

    for _, data, halo, taps_ref, result, size in streams:
        for u in both_shards:
            before = halo[...] if u == 0 else data[0, rows - TAIL : rows, :]
            result[u, 0:TAIL, :] = conv(
                before.astype(F32)[8:16], data[u, 0:TAIL, :], taps_ref, size
            )

    def key_of(u, s):
        return kc_all[u, :, s * DK : (s + 1) * DK]

    def query_of(u, s):
        return qc_all[u, :, s * DK : (s + 1) * DK]

    wide_lane = lax.broadcasted_iota(jnp.int32, (rows, 128), 1)
    for u, s in key_units:
        place_of = 16 * u + 2 * set_heads + s
        columns = jnp.where(wide_lane == place_of, inverse_norm(key_of(u, s)), columns)
        columns = jnp.where(
            wide_lane == place_of + set_keys, inverse_norm(query_of(u, s)) * DK**-0.5, columns
        )
    by_row = jnp.transpose(columns)

    def column(u, index):
        return columns[:, 16 * u + index : 16 * u + index + 1]

    def lane_row(u, index):
        return by_row[16 * u + index : 16 * u + index + 1, :]

    gram, query_gram, key_t = {}, {}, {}
    for u, s in key_units:
        contract = (((1,), (1,)), ((), ()))
        gram[u, s] = lax.dot_general(
            key_of(u, s), key_of(u, s), contract, preferred_element_type=F32
        )
        query_gram[u, s] = lax.dot_general(
            query_of(u, s), key_of(u, s), contract, preferred_element_type=F32
        )
        key_t[u, s] = jnp.transpose(key_of(u, s).astype(F32)).astype(BF16)
    within, lower, inverse = {}, {}, {}
    for u, h in units:
        s = h // 2
        gaps = column(u, h) - lane_row(u, h)
        within[u, h] = jnp.exp(jnp.where(upto, gaps, -1e30)) * lane_row(u, 2 * set_heads + s)
        scale = column(u, set_heads + h) * column(u, 2 * set_heads + s)
        lower[u, h] = jnp.where(strict, scale * gram[u, s] * within[u, h], 0.0)
        inverse[u, h] = jnp.where(apart == 1, -lower[u, h], 0.0)
    level = 1
    while (1 << level) < rows:
        inner = {}
        for i in units:
            block = jnp.where((apart >> level) == 1, lower[i], 0.0)
            inner[i] = block + one_pass(block, inverse[i])
        for i in units:
            inverse[i] = inverse[i] - inner[i] - one_pass(inverse[i], inner[i])
        level += 1
    values, maps, shard_maps, decays = {}, {}, {}, {}
    for u, h in units:
        s = h // 2
        solve = jnp.where(row == col, 1.0, inverse[u, h]) * lane_row(u, set_heads + h)
        values[u, h] = split_left(solve, vc_all[u, :, h * DV : (h + 1) * DV])
        key_solve = solve * (jnp.exp(lane_row(u, h)) * lane_row(u, 2 * set_heads + s))
        maps[u, h] = split_left(key_solve, key_of(u, s))
    for u, h in units:
        s = h // 2
        last = column(u, h)[rows - 1 : rows, :]
        tail = jnp.exp(last - column(u, h)) * column(u, 2 * set_heads + s)
        both = jnp.concatenate([values[u, h] * tail, maps[u, h] * tail], axis=1)
        shard_maps[u, h] = split_right(key_t[u, s], both)
        decays[u, h] = jnp.exp(last)

    eye = row[0:DK, 0:DK] == col[0:DK, 0:DK]

    def decay_of(block):
        return jnp.sum(block.astype(F32), axis=0, keepdims=True)

    def map_of(message, decay):
        return jnp.where(eye, decay[:, 0:1], 0.0) - message[:, DV:].astype(F32)

    def compose(message, decay, carried):
        state = decay * carried[:, 0:DV] + message[:, 0:DV].astype(F32)
        fresh = jnp.concatenate([state, decay * carried[:, DV:]], axis=1)
        return fresh - mm(message[:, DV:].astype(BF16), carried.astype(BF16))

    def put_maps(target, carried, decay):
        target[0:DK, 0:DV] = carried[:, 0:DV].astype(BF16)
        target[0:DK, DV:] = map_of(carried, decay).astype(BF16)

    def up_copy(h):
        return pltpu.make_async_remote_copy(
            src_ref=up_out.at[h],
            dst_ref=up_in.at[z],
            send_sem=up_send.at[h],
            recv_sem=up_recv.at[z],
            device_id=(owner_of(h), x),
            device_id_type=MESH,
        )

    joined = {}
    for h in heads:
        early = shard_maps[0, h]
        carried = jnp.concatenate([early[:, 0:DV], map_of(early, decays[0, h])], axis=1)
        joined[h] = compose(shard_maps[1, h], decays[1, h], carried)
    for h in heads:
        put_maps(up_out.at[h], joined[h], decays[0, h] * decays[1, h])
    far_first = sorted(range(nz), key=lambda offset: -min(offset, nz - offset))
    for offset in far_first:
        target_chip = lax.rem(z + offset, nz)

        @pl.when(target_chip // set_heads == core)
        def _(h=lax.rem(target_chip, set_heads)):
            up_copy(h).start()

    for u, h in units:
        s = h // 2
        scale = column(u, 2 * set_heads + set_keys + s)
        attend = jnp.where(upto, query_gram[u, s] * within[u, h] * scale, 0.0)
        both = split_both(attend, jnp.concatenate([values[u, h], maps[u, h]], axis=1))
        fixed = both[:, 0:DV]
        read = jnp.exp(column(u, h)) * scale * query_of(u, s).astype(F32) - both[:, DV:]
        if u == 1:
            moved = split_both(read, shard_maps[0, h])
            fixed = fixed + moved[:, 0:DV]
            read = decays[0, h] * read - moved[:, DV:]
        high, low = split(read)
        local[h, u * rows : (u + 1) * rows, :] = fixed
        reads[h, u * rows : (u + 1) * rows, 0:DK] = high
        reads[h, u * rows : (u + 1) * rows, DK:] = low

    def carry_copy(source, target_y, i):
        held = (carry_state, carry_map)[i]
        return pltpu.make_async_remote_copy(
            src_ref=held.at[source],
            dst_ref=held.at[source],
            send_sem=y_send.at[i * ny + target_y],
            recv_sem=y_recv.at[i * ny + source],
            device_id=(target_y * ring + place, x),
            device_id_type=MESH,
        )

    def each_carry(act):
        for later in range(1, ny):

            @pl.when(y < later)
            def _(later=later):
                act(carry_copy(y, later, 0))

                @pl.when(y > 0)
                def _():
                    act(carry_copy(y, later, 1))

    def down_copy(target):
        slot = lax.rem(z, set_heads)
        return pltpu.make_async_remote_copy(
            src_ref=down_out.at[target],
            dst_ref=down_in.at[slot],
            send_sem=down_send.at[target],
            recv_sem=down_recv.at[slot],
            device_id=(y * ring + 2 * target + sender_core, x),
            device_id_type=MESH,
        )

    for i in rest:
        loads[i].wait()
    swapped[5].wait_recv()
    for h in heads:
        cols = slice(h * DV, (h + 1) * DV)
        for u in both_shards:
            gates[u, :, cols] = silu(z_in[u, :, cols].astype(F32)) * gain_ref[...]

    @pl.when(owns)
    def _():
        pre_state[0] = jnp.zeros((DK, DV), F32)
        pre_map[0] = jnp.zeros((DK, DK), BF16)
        pre_decay[0] = jnp.ones((8, 128), F32)
        spans = {}
        for j in range(nz):
            for source, target, sent, received in (
                (decay_out, decay_in, decay_send, decay_recv),
                (up_out, up_in, up_send, up_recv),
            ):
                pltpu.make_async_remote_copy(
                    src_ref=source.at[0],
                    dst_ref=target.at[j],
                    send_sem=sent.at[0],
                    recv_sem=received.at[j],
                    device_id=(partner, x),
                    device_id_type=MESH,
                ).wait_recv()
            decay = decay_in[j, 0:1, :]
            state, taken = up_in[j, :, 0:DV].astype(F32), up_in[j, :, DV:].astype(F32)
            carried = jnp.concatenate([state, jnp.where(eye, decay, 0.0) - taken], axis=1)
            spans[j, j + 1] = (carried, decay)

        def after(early, late):
            (carried, decay), (later_maps, later_decay) = spans[early], spans[late]
            message = jnp.concatenate(
                [later_maps[:, 0:DV], map_of(later_maps, later_decay)], axis=1
            )
            spans[early[0], late[1]] = (compose(message, later_decay, carried), decay * later_decay)

        size = 1
        while size < nz:
            for start in range(0, nz, 2 * size):
                after((start, start + size), (start + size, start + 2 * size))
            size *= 2
        carried, total_decay = spans[0, nz]
        carry_state[y] = carried[:, 0:DV].astype(BF16)
        carry_map[y, 0:DK, :] = map_of(carried, total_decay).astype(BF16)
        carry_map[y, DK:, :] = pack_decay(total_decay[:, 0:1], DK)
        each_carry(lambda copy: copy.start())

        for j in range(1, nz):
            if (0, j) not in spans:
                size = j & -j
                after((0, j - size), (j - size, j))
            carried, total_decay = spans[0, j]
            pre_state[j] = carried[:, 0:DV]
            pre_map[j] = map_of(carried, total_decay).astype(BF16)
            pre_decay[j] = jnp.broadcast_to(total_decay, (8, 128))

        sigma[...] = jnp.zeros((DK, DV), F32)
        for earlier in range(ny - 1):

            @pl.when(y > earlier)
            def _(earlier=earlier):
                carry_copy(earlier, y, 0).wait_recv()
                fresh = carry_state[earlier].astype(F32)
                if earlier == 0:
                    sigma[...] = fresh
                else:
                    carry_copy(earlier, y, 1).wait_recv()
                    state = sigma[...]
                    sigma[...] = (
                        decay_of(carry_map[earlier, DK:, :]) * state
                        - mm(carry_map[earlier, 0:DK, :], state.astype(BF16))
                        + fresh
                    )

        start_state = sigma[...]
        rounded = start_state.astype(BF16)
        for offset in far_first:
            target = lax.rem(z + offset, nz)
            down_out[target] = (
                pre_decay[target, 0:1, :] * start_state
                - mm(pre_map[target], rounded)
                + pre_state[target]
            ).astype(BF16)
            down_copy(target).start()

    cores = {}
    for h in heads:
        pltpu.make_async_remote_copy(
            src_ref=down_out.at[0],
            dst_ref=down_in.at[h],
            send_sem=down_send.at[0],
            recv_sem=down_recv.at[h],
            device_id=(owner_of(h), x),
            device_id_type=MESH,
        ).wait_recv()
    for h in heads:
        state = down_in[h]
        cores[h] = mm(reads[h], jnp.concatenate([state, state], axis=0)) + local[h]
    hand_over = pltpu.make_async_remote_copy(
        src_ref=pass_out.at[1 - core],
        dst_ref=normed,
        send_sem=pass_sem.at[0],
        recv_sem=pass_sem.at[1],
        device_id=(partner, x),
        device_id_type=MESH,
    )
    for h in heads:
        power = jnp.mean(cores[h] * cores[h], axis=1, keepdims=True)
        scaled = cores[h] * lax.rsqrt(power + 1e-6)
        cols = slice(h * DV, (h + 1) * DV)
        for u in both_shards:
            part_rows = scaled[u * rows : (u + 1) * rows]
            pass_out[u, :, cols] = (part_rows * gates[u, :, cols]).astype(BF16)
    hand_over.start()

    depth = set_heads * DV

    def part(step, which, operand):
        depth_rows = pl.ds(pl.multiple_of(which * depth, 128), depth)
        return mm(operand, w_in[depth_rows, cols_of(lax.rem(x + step, nx), width)])

    order = (2, 1, nx - 1)
    parts = {step: part(step, core, pass_out[core]) for step in order}
    pltpu.make_async_remote_copy(
        src_ref=pass_out.at[core],
        dst_ref=normed,
        send_sem=pass_sem.at[0],
        recv_sem=pass_sem.at[1],
        device_id=(partner, x),
        device_id_type=MESH,
    ).wait_recv()

    def rs_copy(i, source, target, step):
        return pltpu.make_async_remote_copy(
            src_ref=source,
            dst_ref=target,
            send_sem=rs_send.at[i],
            recv_sem=rs_recv.at[i],
            device_id=(me, lax.rem(x + step, nx)),
            device_id_type=MESH,
        )

    quarter = width // 4
    ahead, back, across = 0, 1, 2
    relays = [
        rs_copy(i, relay_out.at[i], relay_in.at[i], step) for i, step in ((0, 1), (1, nx - 1))
    ]
    direct = rs_copy(2, rs_out.at[across, pl.ds(1, 2)], rs_in.at[across, pl.ds(1, 2)], 2)
    early = [
        rs_copy(3, rs_out.at[ahead, pl.ds(1, 3)], rs_in.at[ahead, pl.ds(1, 3)], 1),
        rs_copy(4, rs_out.at[back, pl.ds(0, 3)], rs_in.at[back, pl.ds(0, 3)], nx - 1),
    ]
    late = [
        rs_copy(5, rs_out.at[ahead, 0], rs_in.at[ahead, 0], 1),
        rs_copy(6, rs_out.at[back, 3], rs_in.at[back, 3], nx - 1),
    ]

    def block(step):
        whole = parts[step] + part(step, 1 - core, normed[...])
        return [whole[:, i * quarter : (i + 1) * quarter] for i in range(4)]

    pieces = block(2)
    relay_out[0] = pieces[0].astype(BF16)
    relays[0].start()
    relay_out[1] = pieces[3].astype(BF16)
    relays[1].start()
    rs_out[across, 1] = pieces[1].astype(BF16)
    rs_out[across, 2] = pieces[2].astype(BF16)
    direct.start()
    pieces = block(1)
    for i in (1, 2, 3):
        rs_out[ahead, i] = pieces[i].astype(BF16)
    early[0].start()
    waiting = [pieces[0]]
    pieces = block(nx - 1)
    for i in (0, 1, 2):
        rs_out[back, i] = pieces[i].astype(BF16)
    early[1].start()
    waiting.append(pieces[3])
    for i, (side, where) in enumerate(((ahead, 0), (back, 3))):
        relays[i].wait_recv()
        rs_out[side, where] = (waiting[i] + relay_in[i].astype(F32)).astype(BF16)
        late[i].start()
    total = part(0, core, pass_out[core]) + part(0, 1 - core, normed[...])
    for copy in early:
        copy.wait_recv()
    direct.wait_recv()
    for copy in late:
        copy.wait_recv()
    for i in range(4):
        cols = slice(i * quarter, (i + 1) * quarter)
        piece = total[:, cols] + rs_in[ahead, i].astype(F32) + rs_in[back, i].astype(F32)
        if i in (1, 2):
            piece = piece + rs_in[across, i].astype(F32)
        out_ref[:, cols] = piece

    @pl.when(sends_halo)
    def _():
        for side in range(2):
            for copy in halo_copies(side):
                copy.wait_send()

    for copy in swap:
        copy.wait_send()
    for h in heads:
        decay_copy(h).wait_send()
        up_copy(h).wait_send()

    @pl.when(owns)
    def _():
        for target in range(nz):
            down_copy(target).wait_send()
        each_carry(lambda copy: copy.wait_send())

    hand_over.wait_send()
    for copy in relays + early + late + [direct]:
        copy.wait_send()


def shards(
    q_in, k_in, v_in, conv_q, conv_k, conv_v, a_in, b_in, a_log, dt_bias, norm_weight, z_in, out_weight
):
    rows = q_in.shape[0]
    nz = v_in.shape[1] // DV
    nx = lax.axis_size("heads")
    ny = lax.axis_size("ctx") // (2 * nz)
    width = out_weight.shape[1] // nx
    half = q_in.shape[1] // 2
    half_v = v_in.shape[1] // 2
    hbm = pl.BlockSpec(memory_space=pltpu.HBM)
    vmem = pl.BlockSpec(memory_space=pltpu.VMEM)
    dma = pltpu.SemaphoreType.DMA
    scratch = [
        pltpu.VMEM((2, rows, half), BF16),
        pltpu.VMEM((2, rows, half), BF16),
        pltpu.VMEM((2, rows, half_v), BF16),
        pltpu.VMEM((2, rows, half_v), BF16),
        pltpu.VMEM(out_weight.shape, BF16),
        pltpu.VMEM((2, nz, rows), F32),
        pltpu.VMEM((2, nz, rows), F32),
        pltpu.VMEM((1, nz), F32),
        pltpu.VMEM((1, nz), F32),
        pltpu.VMEM((1, DV), F32),
        pltpu.VMEM(conv_q.shape, BF16),
        pltpu.VMEM(conv_k.shape, BF16),
        pltpu.VMEM(conv_v.shape, BF16),
        pltpu.VMEM((TAIL, half), BF16),
        pltpu.VMEM((TAIL, half), BF16),
        pltpu.VMEM((TAIL, half_v), BF16),
        pltpu.VMEM((rows + 8, half_v), F32),
        pltpu.VMEM((2, rows, half), BF16),
        pltpu.VMEM((2, rows, half), BF16),
        pltpu.VMEM((2, rows, half_v), BF16),
        pltpu.VMEM((nz // 2, 8, 128), F32),
        pltpu.VMEM((nz, 8, 128), F32),
        pltpu.VMEM((nz // 2, DK, DK + DV), BF16),
        pltpu.VMEM((nz, DK, DK + DV), BF16),
        pltpu.VMEM((ny, DK, DV), BF16),
        pltpu.VMEM((ny, DK + TAIL, DK), BF16),
        pltpu.VMEM((nz, DK, DV), F32),
        pltpu.VMEM((nz, DK, DK), BF16),
        pltpu.VMEM((nz, 8, 128), F32),
        pltpu.VMEM((DK, DV), F32),
        pltpu.VMEM((nz, DK, DV), BF16),
        pltpu.VMEM((nz // 2, DK, DV), BF16),
        pltpu.VMEM((nz // 2, 2 * rows, 2 * DK), BF16),
        pltpu.VMEM((nz // 2, 2 * rows, DV), F32),
        pltpu.VMEM((rows, half_v), BF16),
        pltpu.VMEM((2, rows, half_v), BF16),
        pltpu.VMEM((2, rows, half_v), F32),
        pltpu.VMEM((2, rows, width // 4), BF16),
        pltpu.VMEM((2, rows, width // 4), BF16),
        pltpu.VMEM((3, 4, rows, width // 4), BF16),
        pltpu.VMEM((3, 4, rows, width // 4), BF16),
        dma((13,)),
        dma((6,)),
        dma((6,)),
        dma((6,)),
        dma((3,)),
        dma((nz // 2,)),
        dma((nz,)),
        dma((nz // 2,)),
        dma((nz,)),
        dma((2 * ny,)),
        dma((2 * ny,)),
        dma((nz,)),
        dma((nz // 2,)),
        dma((2,)),
        dma((7,)),
        dma((7,)),
    ]
    call = pl.pallas_call(
        functools.partial(kernel, nx, ny, nz),
        out_shape=jax.ShapeDtypeStruct((rows, width), F32),
        in_specs=[hbm] * 13,
        out_specs=vmem,
        scratch_shapes=scratch,
        compiler_params=pltpu.CompilerParams(
            collective_id=0, has_side_effects=True, vmem_limit_bytes=40 * 1024 * 1024
        ),
        cost_estimate=pl.CostEstimate(
            flops=2_000_000_000, bytes_accessed=6_000_000, transcendentals=1_000_000
        ),
    )
    operands = (
        q_in,
        k_in,
        v_in,
        z_in,
        out_weight,
        a_in.T,
        b_in.T,
        a_log.reshape(1, nz),
        dt_bias.reshape(1, nz),
        norm_weight.reshape(1, DV),
        conv_q,
        conv_k,
        conv_v,
    )
    return call(*(pltpu.with_memory_space_constraint(value, pltpu.HBM) for value in operands))


def solution(mesh):
    in_specs = (
        P("ctx", "heads"),
        P("ctx", "heads"),
        P("ctx", "heads"),
        P(None, "heads"),
        P(None, "heads"),
        P(None, "heads"),
        P("ctx", "heads"),
        P("ctx", "heads"),
        P("heads"),
        P("heads"),
        P(),
        P("ctx", "heads"),
        P("heads", None),
    )
    out_specs = P("ctx", "heads")
    return jax.shard_map(shards, mesh=mesh, in_specs=in_specs, out_specs=out_specs, check_vma=False)
```
